128 devices in a mesh: seq: 32 (over z, y, core), head: 4 (over x).
Axes of the slice: x: 4, y: 4, z: 4, core: 2. Of those that a mesh axis runs over, the one named last changes fastest.
Arguments:
- tokens: bfloat16 [2, 8192, 2048], P(None, 'seq', 'head'), may hold values from -6 to 6
- lengths: int32 [2], replicated, may hold values from 2048 to 8192, as said below
- norm_gain: float32 [2048], replicated, may hold values from 0.25 to 1.75
- query_key_value_weight: bfloat16 [3, 2048, 2048], P(None, None, 'head'), may hold values from -0.125 to 0.125
- strength_projection: bfloat16 [2048, 16], P(None, 'head'), may hold values from -0.125 to 0.125
- conv_weight: float32 [3, 4, 2048], P(None, None, 'head'), may hold values from -3 to 3
- head_gain: float32 [128], replicated, may hold values from 0.25 to 1.75
- output_projection: bfloat16 [2048, 2048], P('head'), may hold values from -0.125 to 0.125
- mlp_gain: float32 [2048], replicated, may hold values from 0.25 to 1.75
- gate_up_weight: bfloat16 [2, 2048, 5632], P(None, None, 'head'), may hold values from -0.125 to 0.125
- down_projection: bfloat16 [5632, 2048], P('head'), may hold values from -0.109375 to 0.109375
- out_grad: bfloat16 [2, 8192, 2048], P(None, 'seq', 'head'), may hold values from -6 to 6
Outputs:
- output: bfloat16 [2, 8192, 2048], P(None, 'seq', 'head')
- tokens_grad: bfloat16 [2, 8192, 2048], P(None, 'seq', 'head')
- norm_gain_grad: float32 [2048], P(('head', 'seq'))
- query_key_value_gradient: float32 [3, 2048, 2048], P(None, 'seq', 'head')
- strength_weight_gradient: float32 [2048, 16], P('seq', 'head')
- conv_grad: float32 [3, 4, 2048], P(None, None, ('head', 'seq'))
- head_gain_grad: float32 [128], P('seq')
- out_weight_grad: float32 [2048, 2048], P('head', 'seq')
- mlp_gain_grad: float32 [2048], P(('head', 'seq'))
- gate_up_grad: float32 [2, 2048, 5632], P(None, 'seq', 'head')
- down_projection_gradient: float32 [5632, 2048], P('head', 'seq')
The draws below stay inside these ranges and needn't reach their ends.
Inputs may be any that keep to these rules, and one draw needn't show every extreme that they name: Sequence s has lengths[s] real tokens at the start of its 8192 positions and padding after them; one sequence, drawn from the seed, has exactly 8192.
All inputs are finite; a program needn't handle non-finite values.
Results may differ from the reference program's by a relative error of at most 0.04.
Values may be sent and summed in bfloat16 or wider, within the bound.
No kernel may reach another device: no remote copies, remote signals or barrier semaphores. Data moves between devices by JAX's collectives and lax.ppermute only.
A program may use at most 256 MiB of HBM per device.

```python
import jax
import jax.numpy as jnp
from jax import lax

D = 2048
HEADS = 16
HEAD_DIM = 128
FF = 5632
CONV = 4
BLOCK = 64
SEQS = 2
LENGTH = 8192


def draw_lengths(key, part):
    key = jax.random.fold_in(key, 11)
    key_len, key_pick = jax.random.split(key)
    drawn_lengths = jax.random.randint(key_len, (SEQS,), LENGTH // 4, LENGTH + 1)
    longest = jax.random.randint(key_pick, (), 0, SEQS)
    return jnp.where(jnp.arange(SEQS) == longest, LENGTH, drawn_lengths).astype(jnp.int32)


def raised(array, rng, source, target, blocks, factor):
    owner, partner = [(jnp.arange(array.shape[position]) // (array.shape[position] // blocks)).reshape([-1 if axis == position else 1 for axis in range(array.ndim)]) for position in (source, target)]
    chosen = jax.random.permutation(rng, blocks)[partner]
    strong = (owner == chosen) | (owner == (partner + blocks // 2) % blocks)
    return jnp.where(strong, factor * array, array)


def steps_of(rng, extent, pieces, smallest, high):
    factor_of = 1.0
    for axis_at, shards_of in pieces:
        draws = jax.random.uniform(jax.random.fold_in(jax.random.fold_in(rng, 6), axis_at), (shards_of,), jnp.float32, smallest / len(pieces), high / len(pieces))
        factor_of = factor_of * jnp.repeat(jnp.exp(draws), extent[axis_at] // shards_of).reshape((-1,) + (1,) * (len(extent) - 1 - axis_at))
    return factor_of


def gaussian(key, dims, deviation, most, cuts=(), kind=jnp.bfloat16):
    values = jax.random.normal(key, dims, jnp.float32) * deviation
    if len(cuts) > 0:
        values = steps_of(key, dims, cuts, -0.22, 0.18) * values
    return jnp.clip(values, min=-most, max=most).astype(kind)


def gaussian_with(key, extent, scale, reach, cuts, heavy, held_as=jnp.bfloat16):
    array = scale * jax.random.normal(key, extent, jnp.float32)
    if cuts:
        array = array * steps_of(key, extent, cuts, -0.22, 0.18)
    return jnp.clip(raised(array, jax.random.fold_in(key, 3), *heavy), -reach, reach).astype(held_as)


def setup_inputs(seed: int = 0) -> dict:
    keys = jax.random.split(jax.random.key(seed), 13)
    tokens = gaussian(keys[0], (SEQS, LENGTH, D), 1.0, 6.0, ((1, 32), (2, 4)))
    lengths = draw_lengths(jax.random.fold_in(keys[12], 71), 0)
    norm_gain = jnp.clip(1.0 + 0.15 * jax.random.normal(keys[2], (D,), jnp.float32), 0.25, 1.75)
    query_key_value_weight = gaussian(keys[3], (3, D, D), D ** -0.5, 0.125, ((2, 4),))
    strength_projection = gaussian(keys[4], (D, HEADS), D ** -0.5, 0.125, ((1, 4),))
    conv_weight = gaussian(keys[5], (3, CONV, D), CONV ** -0.5, 3.0, ((2, 4),), jnp.float32)
    head_gain = jnp.clip(1.0 + 0.15 * jax.random.normal(keys[6], (HEAD_DIM,), jnp.float32), 0.25, 1.75)
    output_projection = gaussian(keys[7], (D, D), D ** -0.5, 0.125, ((0, 4),))
    mlp_gain = jnp.clip(1.0 + 0.15 * jax.random.normal(keys[8], (D,), jnp.float32), 0.25, 1.75)
    gate_up_weight = gaussian(keys[9], (2, D, FF), D ** -0.5, 0.125, ((2, 4),))
    down_projection = gaussian(keys[10], (FF, D), (FF // 2) ** -0.5, 0.109375, ((0, 4),))
    out_grad = gaussian_with(keys[11], (SEQS, LENGTH, D), 1.0, 6.0, ((1, 32), (2, 4)), (1, 2, 32, 2.75))
    return dict(tokens=tokens, lengths=lengths, norm_gain=norm_gain, query_key_value_weight=query_key_value_weight, strength_projection=strength_projection, conv_weight=conv_weight, head_gain=head_gain, output_projection=output_projection, mlp_gain=mlp_gain, gate_up_weight=gate_up_weight, down_projection=down_projection, out_grad=out_grad)


norm_eps = 1e-06
highest_precision = lax.Precision.HIGHEST

@jax.custom_vjp
def reduced_precision(v):
    return lax.optimization_barrier(v.astype(jnp.bfloat16)).astype(jnp.float32)

@jax.custom_vjp
def reduced_precision_backward(v):
    return v

def low_keep(v):
    return (reduced_precision(v), None)

def low_pass(kept, grad):
    return (grad,)

def back_keep(v):
    return (v, None)

def back_low(kept, grad):
    return (reduced_precision(grad),)
reduced_precision.defvjp(low_keep, low_pass)
reduced_precision_backward.defvjp(back_keep, back_low)

def row_norm(values, gain_vec):
    return values * lax.rsqrt(lax.optimization_barrier(jnp.mean(values * values, axis=-1, keepdims=True)) + norm_eps) * gain_vec

def unit_rows(values):
    return values * lax.rsqrt(lax.optimization_barrier(jnp.sum(values * values, axis=-1, keepdims=True)) + norm_eps)

def delta_rule(queries, keys_unit, values, strength):
    seq_count, length, head_count, head_width = queries.shape
    num_blocks = length // BLOCK

    def blocked(tensor):
        time_first = jnp.moveaxis(tensor, 1, 0)
        return time_first.reshape((num_blocks, BLOCK) + time_first.shape[1:])

    def token_step(memory, token_item):
        query_row, key_row, value_row, write_rate = token_item
        recalled = jnp.einsum('shk,shkv->shv', key_row, memory, precision=highest_precision)
        memory = memory + write_rate[:, :, None, None] * key_row[:, :, :, None] * (value_row - recalled)[:, :, None, :]
        return (memory, jnp.einsum('shk,shkv->shv', query_row, memory, precision=highest_precision))

    @jax.checkpoint
    def block_step(memory, block_items):
        return lax.scan(token_step, memory, block_items)
    initial = jnp.zeros((seq_count, head_count, head_width, head_width), jnp.float32)
    _, produced = lax.scan(block_step, initial, (blocked(queries), blocked(keys_unit), blocked(values), blocked(strength)))
    return jnp.moveaxis(produced.reshape((length, seq_count, head_count, head_width)), 0, 1)

def forward(tokens, norm_gain, query_key_value_weight, strength_projection, conv_weight, head_gain, output_projection, mlp_gain, gate_up_weight, down_projection, valid_mask):
    seq_count, length, model_width = tokens.shape
    normalized_input = reduced_precision(row_norm(tokens, norm_gain))
    projected_tokens = reduced_precision_backward(reduced_precision(jnp.einsum('pit,ftw->fpiw', normalized_input, query_key_value_weight, precision=highest_precision)))
    logit_values = reduced_precision_backward(jnp.einsum('qbx,xg->qbg', normalized_input, strength_projection, precision=highest_precision))
    padded = jnp.pad(projected_tokens, ((0, 0), (0, 0), (CONV - 1, 0), (0, 0)))
    conv_mixed = conv_weight[:, 0][:, None, None, :] * padded[:, :, 0:length, :]
    for tap_index in range(1, CONV):
        conv_mixed = conv_mixed + conv_weight[:, tap_index][:, None, None, :] * padded[:, :, tap_index:tap_index + length, :]
    active = jax.nn.silu(conv_mixed)
    shape_heads = (seq_count, length, HEADS, HEAD_DIM)
    queries = unit_rows(active[0].reshape(shape_heads))
    keys_unit = unit_rows(active[1].reshape(shape_heads))
    values = active[2].reshape(shape_heads)
    strength = jax.nn.sigmoid(logit_values) * valid_mask[:, :, None]
    mixer = delta_rule(queries, keys_unit, values, strength)
    head_output = reduced_precision((row_norm(mixer, head_gain) * valid_mask[:, :, None, None]).reshape(seq_count, length, model_width))
    middle_residual = tokens + reduced_precision_backward(jnp.einsum('rpj,jk->rpk', head_output, output_projection, precision=highest_precision))
    normalized_middle = reduced_precision(row_norm(middle_residual, mlp_gain))
    gated_preactivation = reduced_precision_backward(jnp.einsum('rux,gxt->grut', normalized_middle, gate_up_weight, precision=highest_precision))
    hidden_features = reduced_precision(jax.nn.silu(gated_preactivation[0]) * gated_preactivation[1])
    return middle_residual + jnp.einsum('yqj,jo->yqo', hidden_features, down_projection, precision=highest_precision)

def reference(tokens, lengths, norm_gain, query_key_value_weight, strength_projection, conv_weight, head_gain, output_projection, mlp_gain, gate_up_weight, down_projection, out_grad):
    positions = jnp.arange(LENGTH, dtype=jnp.int32)
    valid_mask = (positions[None, :] < lengths[:, None].astype(jnp.int32)).astype(jnp.float32)

    def wrapped(tokens_in, gain_in, qkv_in, beta_in, conv_in, head_in, out_in, mlp_in, gate_in, down_in):
        return forward(tokens_in, gain_in, qkv_in, beta_in, conv_in, head_in, out_in, mlp_in, gate_in, down_in, valid_mask)
    result, pullback = jax.vjp(wrapped, tokens.astype(jnp.float32), norm_gain.astype(jnp.float32), query_key_value_weight.astype(jnp.float32), strength_projection.astype(jnp.float32), conv_weight.astype(jnp.float32), head_gain.astype(jnp.float32), output_projection.astype(jnp.float32), mlp_gain.astype(jnp.float32), gate_up_weight.astype(jnp.float32), down_projection.astype(jnp.float32))
    grads = pullback(out_grad.astype(jnp.float32))
    return (result.astype(jnp.bfloat16), grads[0].astype(jnp.bfloat16), grads[1], grads[2], grads[3], grads[4], grads[5], grads[6], grads[7], grads[8], grads[9])
```

```python
from functools import partial

import jax
import jax.numpy as jnp
from jax import lax
from jax.experimental import pallas as pl
from jax.experimental.pallas import tpu as pltpu
from jax.sharding import PartitionSpec as P

HEAD_DIM = 128
CONV = 4
HALF = 128
HALO = 8
EPS = 1e-06

f32 = jnp.float32
bf16 = jnp.bfloat16


def dot(a, b, dims=((1,), (0,))):
    return lax.dot_general(
        a.astype(bf16), b.astype(bf16), (dims, ((), ())), preferred_element_type=f32
    )


NT = ((1,), (1,))
TN = ((0,), (0,))


def split(a):
    high = a.astype(bf16)
    return high, (a - high.astype(f32)).astype(bf16)


def dot3(a, b):
    a_high, a_low = split(a)
    b_high, b_low = split(b)
    return dot(a_high, b_high) + (dot(a_high, b_low) + dot(a_low, b_high))


def unit_lower_inverse(strict):
    size = strict.shape[0]
    row = lax.broadcasted_iota(jnp.int32, (size, size), 0)
    col = lax.broadcasted_iota(jnp.int32, (size, size), 1)
    inverse = jnp.where(row == col, 1.0, 0.0)
    width = 1
    while width < size:
        below = (row // (2 * width) == col // (2 * width)) & (row // width != col // width)
        part = jnp.where(below, strict, 0.0)
        if width == 1:
            inverse = inverse - part
        else:
            inverse = inverse - dot3(inverse, dot3(part, inverse))
        width *= 2
    return inverse


def sigmoid(x):
    return 1.0 / (1.0 + jnp.exp(-x))


def masks():
    row = lax.broadcasted_iota(jnp.int32, (HALF, HALF), 0)
    col = lax.broadcasted_iota(jnp.int32, (HALF, HALF), 1)
    return row > col, row >= col


def conv_rows(j, proj_ref, halo_ref, conv_ref, rows, lanes):
    length = proj_ref.shape[2]
    rows[0:HALO, :] = halo_ref[j, 0, :, lanes].astype(f32)
    rows[HALO : HALO + length, :] = proj_ref[j, 0, :, lanes].astype(f32)
    mixed = None
    for i in range(CONV):
        start = HALO - (CONV - 1) + i
        term = conv_ref[j, i : i + 1, lanes] * rows[start : start + length, :]
        mixed = term if mixed is None else mixed + term
    return mixed


def column_of(values, at):
    lane = lax.broadcasted_iota(jnp.int32, values.shape, 1)
    return jnp.sum(jnp.where(lane == at, values, 0.0), axis=1, keepdims=True)


def span_kernel(
    heads, proj_ref, halo_ref, conv_ref, strength_ref,
    send_ref, q_ref, k_ref, v_ref, w_ref, u_ref, gram_ref, score_ref, inv_ref, rows,
):
    lower, lower_diag = masks()
    for h in range(heads):
        lanes = slice(h * HEAD_DIM, (h + 1) * HEAD_DIM)
        active = []
        for j in range(3):
            mixed = conv_rows(j, proj_ref, halo_ref, conv_ref, rows.at[h * 3 + j], lanes)
            active.append(mixed * sigmoid(mixed))
        q = active[0] * lax.rsqrt(jnp.sum(active[0] * active[0], axis=1, keepdims=True) + EPS)
        k = active[1] * lax.rsqrt(jnp.sum(active[1] * active[1], axis=1, keepdims=True) + EPS)
        v = active[2]
        q_ref[h] = q.astype(bf16)
        k_ref[h] = k.astype(bf16)
        v_ref[h] = v.astype(bf16)
        beta = column_of(strength_ref[0], h)
        gram = dot(k, k, NT)
        score = dot(q, k, NT)
        a, b = slice(0, HALF), slice(HALF, 2 * HALF)
        gaa = jnp.where(lower, gram[a, a], 0.0)
        gbb = jnp.where(lower, gram[b, b], 0.0)
        gba = gram[b, a]
        gram_ref[h, 0] = gaa.astype(bf16)
        gram_ref[h, 1] = gba.astype(bf16)
        gram_ref[h, 2] = gbb.astype(bf16)
        score_ref[h, 0] = jnp.where(lower_diag, score[a, a], 0.0).astype(bf16)
        score_ref[h, 1] = score[b, a].astype(bf16)
        score_ref[h, 2] = jnp.where(lower_diag, score[b, b], 0.0).astype(bf16)
        taa = unit_lower_inverse(beta[a] * gaa)
        tbb = unit_lower_inverse(beta[b] * gbb)
        inv_ref[h, 0] = taa.astype(bf16)
        inv_ref[h, 1] = tbb.astype(bf16)
        right = beta * jnp.concatenate([k, v], axis=1)
        top = dot(taa, right[a])
        bottom = dot(tbb, right[b] - beta[b] * dot(gba, top))
        w = jnp.concatenate([top[:, :HEAD_DIM], bottom[:, :HEAD_DIM]], axis=0)
        u = jnp.concatenate([top[:, HEAD_DIM:], bottom[:, HEAD_DIM:]], axis=0)
        w_ref[h] = w.astype(bf16)
        u_ref[h] = u.astype(bf16)
        step = -dot(w, k, TN)
        add = dot(u, k, TN)
        groups, rows_each = send_ref.shape[1], send_ref.shape[2] - HEAD_DIM
        for g in range(groups):
            send_ref[h, g, 0:HEAD_DIM, :] = step.astype(bf16)
            send_ref[h, g, HEAD_DIM:, :] = add[g * rows_each : (g + 1) * rows_each].astype(bf16)


def chain_kernel(blocks, recv_ref, out_ref):
    state = jnp.zeros(out_ref.shape[1:], f32)
    for d in range(blocks):
        high, low = split(state)
        out_ref[d] = high
        if d < blocks - 1:
            step = recv_ref[d, 0:HEAD_DIM, :]
            add = recv_ref[d, HEAD_DIM:, :].astype(f32)
            state = state + add + (dot(high, step) + dot(low, step))


def back_chain_kernel(blocks, recv_ref, add_ref, out_ref):
    state = jnp.zeros(out_ref.shape[1:], f32)
    for d in range(blocks - 1, -1, -1):
        high, low = split(state)
        out_ref[d] = high
        if d > 0:
            step = recv_ref[d, 0:HEAD_DIM, :]
            add = add_ref[d].astype(f32)
            state = state + add + (dot(high, step, NT) + dot(low, step, NT))


def mixer_kernel(
    heads, state_ref, q_ref, w_ref, u_ref, score_ref, gain_ref, mask_ref, out_ref, x_ref, mix_ref
):
    a, b = slice(0, HALF), slice(HALF, 2 * HALF)
    mask = mask_ref[0]
    for h in range(heads):
        lanes = slice(h * HEAD_DIM, (h + 1) * HEAD_DIM)
        state = state_ref[h]
        x = u_ref[h].astype(f32) - dot(w_ref[h], state, NT)
        x_ref[h] = x.astype(bf16)
        base = dot(q_ref[h], state, NT)
        top = dot(score_ref[h, 0], x[a])
        bottom = dot(score_ref[h, 1], x[a]) + dot(score_ref[h, 2], x[b])
        mixer = base + jnp.concatenate([top, bottom], axis=0)
        mix_ref[h] = mixer
        inv = lax.rsqrt(jnp.mean(mixer * mixer, axis=1, keepdims=True) + EPS)
        out_ref[0, :, lanes] = (mixer * inv * gain_ref[...] * mask).astype(bf16)


def head_back_kernel(
    heads, grad_ref, mix_ref, gain_ref, mask_ref, q_ref, w_ref, score_ref,
    send_ref, dmix_ref, dx_ref, dgain_ref,
):
    a, b = slice(0, HALF), slice(HALF, 2 * HALF)
    mask = mask_ref[0]
    gain = gain_ref[...]
    for h in range(heads):
        lanes = slice(h * HEAD_DIM, (h + 1) * HEAD_DIM)
        grad = grad_ref[0, :, lanes].astype(f32) * mask
        mixer = mix_ref[h]
        inv = lax.rsqrt(jnp.mean(mixer * mixer, axis=1, keepdims=True) + EPS)
        scaled = mixer * inv
        dgain_ref[h] = jnp.sum(grad * scaled, axis=0, keepdims=True)
        inner = jnp.mean(gain * grad * scaled, axis=1, keepdims=True)
        dmix = inv * (gain * grad - scaled * inner)
        dmix_ref[h] = dmix.astype(bf16)
        top = dot(score_ref[h, 0], dmix[a], TN) + dot(score_ref[h, 1], dmix[b], TN)
        bottom = dot(score_ref[h, 2], dmix[b], TN)
        dx = jnp.concatenate([top, bottom], axis=0)
        dx_ref[h] = dx
        send_ref[h] = (dot(dmix, q_ref[h], TN) - dot(dx, w_ref[h], TN)).astype(bf16)


def span_back_kernel(
    heads, proj_ref, halo_ref, conv_ref, strength_ref, state_ref, dstate_ref,
    x_ref, dmix_ref, dx_ref, gram_ref, inv_ref,
    dproj_ref, tail_ref, ahead_ref, dlogit_ref, dconv_ref, rows, grads,
):
    lower, lower_diag = masks()
    a, b = slice(0, HALF), slice(HALF, 2 * HALF)
    length = proj_ref.shape[2]
    lane = lax.broadcasted_iota(jnp.int32, strength_ref.shape[1:], 1)
    dlogit = jnp.zeros(strength_ref.shape[1:], f32)
    for h in range(heads):
        lanes = slice(h * HEAD_DIM, (h + 1) * HEAD_DIM)
        mixed, sig, active = [], [], []
        for j in range(3):
            mixed.append(conv_rows(j, proj_ref, halo_ref, conv_ref, rows.at[h * 3 + j], lanes))
            sig.append(sigmoid(mixed[j]))
            active.append(mixed[j] * sig[j])
        q_inv = lax.rsqrt(jnp.sum(active[0] * active[0], axis=1, keepdims=True) + EPS)
        k_inv = lax.rsqrt(jnp.sum(active[1] * active[1], axis=1, keepdims=True) + EPS)
        q, k, v = active[0] * q_inv, active[1] * k_inv, active[2]
        kb = k.astype(bf16)
        beta = column_of(strength_ref[0], h)
        state, dstate = state_ref[h], dstate_ref[h]
        x, dmix = x_ref[h], dmix_ref[h]
        gaa, gba, gbb = gram_ref[h, 0], gram_ref[h, 1], gram_ref[h, 2]
        dx = dx_ref[h] + dot(kb, dstate, NT)
        y_b = dot(inv_ref[h, 1], dx[b], TN)
        y_a = dot(inv_ref[h, 0], dx[a] - dot(gba, beta[b] * y_b, TN), TN)
        y = jnp.concatenate([y_a, y_b], axis=0)
        inner = jnp.concatenate([dot(gaa, x[a]), dot(gba, x[a]) + dot(gbb, x[b])], axis=0)
        residual = v - dot(kb, state, NT) - inner
        dbeta = jnp.sum(y * residual, axis=1, keepdims=True)
        dlogit = jnp.where(lane == h, dbeta * beta * (1.0 - beta), dlogit)
        dv = beta * y
        dgram = -dot(dv, x, NT)
        dscore = dot(dmix, x, NT)
        dg_aa = jnp.where(lower, dgram[a, a], 0.0).astype(bf16)
        dg_bb = jnp.where(lower, dgram[b, b], 0.0).astype(bf16)
        dg_ba = dgram[b, a].astype(bf16)
        ds_aa = jnp.where(lower_diag, dscore[a, a], 0.0).astype(bf16)
        ds_bb = jnp.where(lower_diag, dscore[b, b], 0.0).astype(bf16)
        ds_ba = dscore[b, a].astype(bf16)
        qb = q.astype(bf16)
        dq = dot(dmix, state) + jnp.concatenate(
            [dot(ds_aa, kb[a]), dot(ds_ba, kb[a]) + dot(ds_bb, kb[b])], axis=0
        )
        dk = dot(x, dstate) - dot(dv, state)
        dk_a = (
            dot(ds_aa, qb[a], TN) + dot(ds_ba, qb[b], TN)
            + dot(dg_aa, kb[a]) + dot(dg_aa, kb[a], TN) + dot(dg_ba, kb[b], TN)
        )
        dk_b = (
            dot(ds_bb, qb[b], TN) + dot(dg_ba, kb[a])
            + dot(dg_bb, kb[b]) + dot(dg_bb, kb[b], TN)
        )
        dk = dk + jnp.concatenate([dk_a, dk_b], axis=0)
        dact = [
            (dq - q * jnp.sum(q * dq, axis=1, keepdims=True)) * q_inv,
            (dk - k * jnp.sum(k * dk, axis=1, keepdims=True)) * k_inv,
            dv,
        ]
        for j in range(3):
            dmixed = dact[j] * sig[j] * (1.0 + mixed[j] * (1.0 - sig[j]))
            own = rows.at[h * 3 + j]
            pad = grads.at[h * 3 + j]
            pad[0:HALO, :] = jnp.zeros((HALO, HEAD_DIM), f32)
            pad[HALO : HALO + length, :] = dmixed
            pad[HALO + length :, :] = jnp.zeros((HALO, HEAD_DIM), f32)
            whole = None
            for i in range(CONV):
                start = HALO - (CONV - 1) + i
                dconv_ref[j, 0, i : i + 1, lanes] = jnp.sum(
                    dmixed * own[start : start + length, :], axis=0, keepdims=True
                )
                shift = CONV - 1 - i
                term = conv_ref[j, i : i + 1, lanes] * pad[shift : shift + HALO + length, :]
                whole = term if whole is None else whole + term
            ahead_ref[j, 0, :, lanes] = whole[0:HALO].astype(bf16)
            dproj_ref[j, 0, :, lanes] = whole[HALO:].astype(bf16)
            tail_ref[j, 0, :, lanes] = whole[length:]
    dlogit_ref[0] = dlogit


def kernel_params():
    return pltpu.CompilerParams(vmem_limit_bytes=48 * 1024 * 1024)


def spec(block, index):
    return pl.BlockSpec(block, index)


def mixer_calls(seqs, length, heads):
    chains = seqs * heads
    width = heads * HEAD_DIM
    at = {
        "proj": spec((3, 1, length, width), lambda s: (0, s, 0, 0)),
        "halo": spec((3, 1, HALO, width), lambda s: (0, s, 0, 0)),
        "conv": spec((3, CONV, width), lambda s: (0, 0, 0)),
        "strength": spec((1, length, heads), lambda s: (s, 0, 0)),
        "tokens": spec((heads, length, HEAD_DIM), lambda s: (s, 0, 0)),
        "state": spec((heads, HEAD_DIM, HEAD_DIM), lambda s: (s, 0, 0)),
        "three": spec((heads, 3, HALF, HALF), lambda s: (s, 0, 0, 0)),
        "two": spec((heads, 2, HALF, HALF), lambda s: (s, 0, 0, 0)),
        "rows": spec((1, length, width), lambda s: (s, 0, 0)),
        "mask": spec((1, length, 1), lambda s: (s, 0, 0)),
        "gain": spec((1, HEAD_DIM), lambda s: (0, 0)),
    }
    shape = {
        "tokens": lambda kind: jax.ShapeDtypeStruct((chains, length, HEAD_DIM), kind),
        "three": jax.ShapeDtypeStruct((chains, 3, HALF, HALF), bf16),
        "two": jax.ShapeDtypeStruct((chains, 2, HALF, HALF), bf16),
    }
    return at, shape


def from_behind(value, axis, steps):
    count = lax.axis_size(axis)
    initial, last = (max(0, -steps), min(count, count - steps))
    return lax.ppermute(value, axis, [(source, source + steps) for source in range(initial, last)])


def exchange(blocks, axis):
    return lax.all_to_all(blocks, axis, 0, 0)


def gather_columns(own):
    count = lax.axis_size("head")
    parts = exchange(jnp.broadcast_to(own[None], (count,) + own.shape), "head")
    return jnp.moveaxis(parts, 0, 2).reshape(own.shape[:2] + (count * own.shape[2],))


def scatter_sum(partial_rows):
    count = lax.axis_size("head")
    seqs, length, columns = partial_rows.shape
    parts = jnp.moveaxis(partial_rows.reshape(seqs, length, count, columns // count), 2, 0)
    return jnp.sum(exchange(parts, "head").astype(f32), axis=0)


def row_scale(rows):
    return lax.rsqrt(jnp.mean(rows * rows, axis=-1, keepdims=True) + EPS)


def shards(
    tokens,
    lengths,
    norm_gain,
    query_key_value_weight,
    strength_projection,
    conv_weight,
    head_gain,
    output_projection,
    mlp_gain,
    gate_up_weight,
    down_projection,
    out_grad,
):
    seqs, length, width = tokens.shape
    model = norm_gain.shape[0]
    heads = width // HEAD_DIM
    chains = seqs * heads
    blocks = lax.axis_size("seq")
    groups = blocks // chains
    cols = HEAD_DIM // groups
    hidden = down_projection.shape[0]
    col_start = lax.axis_index("head") * width
    positions = lax.axis_index("seq") * length + jnp.arange(length, dtype=jnp.int32)
    mask = (positions[None, :] < lengths[:, None]).astype(f32)[:, :, None]
    at, shape = mixer_calls(seqs, length, heads)
    gain_row = head_gain[None, :]

    full = gather_columns(tokens)
    grad_rows = lax.all_gather(out_grad, "head", axis=2, tiled=True)
    full32 = full.astype(f32)
    in_scale = row_scale(full32)
    normed_in = (full32 * in_scale * norm_gain).astype(bf16)
    projected = jnp.einsum(
        "pit,ftw->fpiw", normed_in, query_key_value_weight, preferred_element_type=f32
    ).astype(bf16)
    logits = jnp.einsum(
        "qbx,xg->qbg", normed_in, strength_projection, preferred_element_type=f32
    )
    strength = jax.nn.sigmoid(logits) * mask
    halo = from_behind(projected[:, :, length - HALO :, :], "seq", 1)

    send, q, k, v, w, u, gram, score, inv = pl.pallas_call(
        partial(span_kernel, heads),
        grid=(seqs,),
        in_specs=[at["proj"], at["halo"], at["conv"], at["strength"]],
        out_specs=[
            spec((heads, groups, HEAD_DIM + cols, HEAD_DIM), lambda s: (s, 0, 0, 0)),
            at["tokens"], at["tokens"], at["tokens"], at["tokens"], at["tokens"],
            at["three"], at["three"], at["two"],
        ],
        out_shape=[
            jax.ShapeDtypeStruct((chains, groups, HEAD_DIM + cols, HEAD_DIM), bf16),
            *[shape["tokens"](bf16)] * 5,
            shape["three"], shape["three"], shape["two"],
        ],
        scratch_shapes=[pltpu.VMEM((heads * 3, HALO + length, HEAD_DIM), f32)],
        compiler_params=kernel_params(),
    )(projected, halo, conv_weight, strength)

    received = exchange(send.reshape(blocks, HEAD_DIM + cols, HEAD_DIM), "seq")
    entering = pl.pallas_call(
        partial(chain_kernel, blocks),
        out_shape=jax.ShapeDtypeStruct((blocks, cols, HEAD_DIM), bf16),
        compiler_params=kernel_params(),
    )(received)
    state = exchange(entering, "seq").reshape(chains, HEAD_DIM, HEAD_DIM)

    head_out, x, mixer = pl.pallas_call(
        partial(mixer_kernel, heads),
        grid=(seqs,),
        in_specs=[
            at["state"], at["tokens"], at["tokens"], at["tokens"], at["three"], at["gain"],
            at["mask"],
        ],
        out_specs=[at["rows"], at["tokens"], at["tokens"]],
        out_shape=[
            jax.ShapeDtypeStruct((seqs, length, width), bf16),
            shape["tokens"](bf16),
            shape["tokens"](f32),
        ],
        compiler_params=kernel_params(),
    )(state, q, w, u, score, gain_row, mask)

    branch = jnp.einsum("rpj,jk->rpk", head_out, output_projection, preferred_element_type=f32)
    middle_own = tokens.astype(f32) + scatter_sum(branch.astype(bf16))
    middle = gather_columns(middle_own.astype(bf16)).astype(f32)
    mid_scale = row_scale(middle)
    normed_mid = (middle * mid_scale * mlp_gain).astype(bf16)

    gated = jnp.einsum("rux,gxt->grut", normed_mid, gate_up_weight, preferred_element_type=f32)
    gate_sig = jax.nn.sigmoid(gated[0])
    gate_act = gated[0] * gate_sig
    features = (gate_act * gated[1]).astype(bf16)
    feed = jnp.einsum("yqj,jo->yqo", features, down_projection, preferred_element_type=f32)
    feed_own = lax.psum_scatter(
        feed.astype(bf16), "head", scatter_dimension=2, tiled=True
    ).astype(f32)
    output = (middle_own + feed_own).astype(bf16)
    hidden_grad = jnp.einsum("zxp,hp->zxh", grad_rows, down_projection, preferred_element_type=f32)
    gate_grad = hidden_grad * gated[1] * gate_sig * (1.0 + gated[0] * (1.0 - gate_sig))
    up_grad = hidden_grad * gate_act
    gated_grad = jnp.stack([gate_grad, up_grad]).astype(bf16)
    mid_part = jnp.einsum("nyqp,ngp->yqg", gated_grad, gate_up_weight, preferred_element_type=f32)
    mid_grad_own = scatter_sum(mid_part.astype(bf16))
    mid_grad = gather_columns(mid_grad_own.astype(bf16)).astype(f32)

    gate_up_part = jnp.einsum("qig,kqiv->gkv", normed_mid, gated_grad, preferred_element_type=f32)
    down_part = jnp.einsum("rtx,rtq->xq", grad_rows, features, preferred_element_type=f32)
    feed_part = jnp.concatenate(
        [gate_up_part.reshape(model, 2 * hidden).astype(bf16), down_part.astype(bf16)], axis=1
    )
    feed_sum = lax.psum_scatter(feed_part, "seq", scatter_dimension=0, tiled=True).astype(f32)

    mid_dot = jnp.mean(mlp_gain * mid_grad * middle, axis=-1, keepdims=True)
    middle_grad = grad_rows.astype(f32) + (
        mid_scale * mlp_gain * mid_grad - mid_scale * mid_scale * mid_scale * middle * mid_dot
    )
    branch_grad = middle_grad.astype(bf16)
    own_gain = lax.dynamic_slice_in_dim(mlp_gain, col_start, width, 0)
    middle_grad_own = out_grad.astype(f32) + (
        mid_scale * own_gain * mid_grad_own
        - mid_scale * mid_scale * mid_scale * middle_own * mid_dot
    )
    mlp_gain_part = jnp.sum(mid_grad_own * middle_own * mid_scale, axis=(0, 1))
    head_grad = jnp.einsum(
        "hpj,wj->hpw", branch_grad, output_projection, preferred_element_type=f32
    ).astype(bf16)

    send_back, dmix, dx, dgain = pl.pallas_call(
        partial(head_back_kernel, heads),
        grid=(seqs,),
        in_specs=[
            at["rows"], at["tokens"], at["gain"], at["mask"], at["tokens"], at["tokens"],
            at["three"],
        ],
        out_specs=[
            at["state"], at["tokens"], at["tokens"],
            spec((heads, 1, HEAD_DIM), lambda s: (s, 0, 0)),
        ],
        out_shape=[
            jax.ShapeDtypeStruct((chains, HEAD_DIM, HEAD_DIM), bf16),
            shape["tokens"](bf16),
            shape["tokens"](f32),
            jax.ShapeDtypeStruct((chains, 1, HEAD_DIM), f32),
        ],
        compiler_params=kernel_params(),
    )(head_grad, mixer, gain_row, mask, q, w, score)

    added = exchange(send_back.reshape(blocks, cols, HEAD_DIM), "seq")
    leaving = pl.pallas_call(
        partial(back_chain_kernel, blocks),
        out_shape=jax.ShapeDtypeStruct((blocks, cols, HEAD_DIM), bf16),
        compiler_params=kernel_params(),
    )(received, added)
    dstate = exchange(leaving, "seq").reshape(chains, HEAD_DIM, HEAD_DIM)

    dproj, tail, ahead, dlogit, dconv = pl.pallas_call(
        partial(span_back_kernel, heads),
        grid=(seqs,),
        in_specs=[
            at["proj"], at["halo"], at["conv"], at["strength"], at["state"], at["state"],
            at["tokens"], at["tokens"], at["tokens"], at["three"], at["two"],
        ],
        out_specs=[
            at["proj"], at["halo"], at["halo"], at["strength"],
            spec((3, 1, CONV, width), lambda s: (0, s, 0, 0)),
        ],
        out_shape=[
            jax.ShapeDtypeStruct((3, seqs, length, width), bf16),
            jax.ShapeDtypeStruct((3, seqs, HALO, width), f32),
            jax.ShapeDtypeStruct((3, seqs, HALO, width), bf16),
            jax.ShapeDtypeStruct((seqs, length, heads), f32),
            jax.ShapeDtypeStruct((3, seqs, CONV, width), f32),
        ],
        scratch_shapes=[
            pltpu.VMEM((heads * 3, HALO + length, HEAD_DIM), f32),
            pltpu.VMEM((heads * 3, 2 * HALO + length, HEAD_DIM), f32),
        ],
        compiler_params=kernel_params(),
    )(projected, halo, conv_weight, strength, state, dstate, x, dmix, dx, gram, inv)

    sent_back = from_behind(ahead, "seq", -1).astype(f32)
    proj_grad = lax.dynamic_update_slice_in_dim(
        dproj, (tail + sent_back).astype(bf16), length - HALO, 2
    )
    logit_grad = dlogit.astype(bf16)

    in_part = jnp.einsum(
        "qxtm,qbm->xtb", proj_grad, query_key_value_weight, preferred_element_type=f32
    ) + jnp.einsum("xzi,pi->xzp", logit_grad, strength_projection, preferred_element_type=f32)
    in_dot_part = jnp.mean(norm_gain * in_part * full32, axis=-1, keepdims=True)
    in_dot, head_gain_part = lax.psum((in_dot_part, jnp.sum(dgain, axis=(0, 1))), "head")
    in_grad = scatter_sum(in_part.astype(bf16))
    own = tokens.astype(f32)
    in_gain = lax.dynamic_slice_in_dim(norm_gain, col_start, width, 0)
    tokens_grad = (
        in_scale * in_gain * in_grad - in_scale * in_scale * in_scale * own * in_dot
        + middle_grad_own
    ).astype(bf16)
    norm_gain_part = jnp.sum(in_grad * own * in_scale, axis=(0, 1))

    qkv_part = jnp.einsum("kub,hkuy->bhy", normed_in, proj_grad, preferred_element_type=f32)
    out_part = jnp.einsum("gmv,gmx->vx", branch_grad, head_out, preferred_element_type=f32)
    strength_part = jnp.einsum("qrg,qre->ge", normed_in, logit_grad, preferred_element_type=f32)
    mix_part = jnp.concatenate(
        [
            qkv_part.reshape(model, 3 * width).astype(bf16),
            out_part.astype(bf16),
            jnp.pad(strength_part.astype(bf16), ((0, 0), (0, HEAD_DIM - heads))),
        ],
        axis=1,
    )
    mix_sum = lax.psum_scatter(mix_part, "seq", scatter_dimension=0, tiled=True).astype(f32)
    small = jnp.concatenate(
        [
            jnp.sum(dconv, axis=1).reshape(3 * CONV, width),
            norm_gain_part[None],
            mlp_gain_part[None],
            jnp.pad(head_gain_part[None], ((0, 0), (0, width - HEAD_DIM))),
        ]
    ).astype(bf16)
    small_sum = lax.psum(small, "seq").astype(f32)
    mine = lax.axis_index("seq")
    each = width // blocks
    own_small = lax.dynamic_slice_in_dim(small_sum[: 3 * CONV + 2], mine * each, each, 1)
    gain_each = HEAD_DIM // blocks
    head_gain_own = lax.dynamic_slice_in_dim(
        small_sum[3 * CONV + 2], mine * gain_each, gain_each, 0
    )
    rows_own = model // blocks
    qkv_grad = jnp.moveaxis(mix_sum[:, : 3 * width].reshape(rows_own, 3, width), 1, 0)
    return (
        output,
        tokens_grad,
        own_small[3 * CONV],
        qkv_grad,
        mix_sum[:, 4 * width : 4 * width + heads],
        own_small[: 3 * CONV].reshape(3, CONV, each),
        head_gain_own,
        mix_sum[:, 3 * width : 4 * width].T,
        own_small[3 * CONV + 1],
        jnp.moveaxis(feed_sum[:, : 2 * hidden].reshape(rows_own, 2, hidden), 1, 0),
        feed_sum[:, 2 * hidden :].T,
    )


def solution(mesh):
    return jax.shard_map(
        shards,
        mesh=mesh,
        in_specs=(
            P(None, "seq", "head"),
            P(),
            P(),
            P(None, None, "head"),
            P(None, "head"),
            P(None, None, "head"),
            P(),
            P("head", None),
            P(),
            P(None, None, "head"),
            P("head", None),
            P(None, "seq", "head"),
        ),
        out_specs=(
            P(None, "seq", "head"),
            P(None, "seq", "head"),
            P(("head", "seq")),
            P(None, "seq", "head"),
            P("seq", "head"),
            P(None, None, ("head", "seq")),
            P("seq"),
            P("head", "seq"),
            P(("head", "seq")),
            P(None, "seq", "head"),
            P("head", "seq"),
        ),
        check_vma=False,
    )
```

```python
from functools import partial

import jax
import jax.numpy as jnp
from jax import lax
from jax.experimental import pallas as pl
from jax.experimental.pallas import tpu as pltpu
from jax.sharding import PartitionSpec as P

HEAD_DIM = 128
CONV = 4
HALF = 128
HALO = 8
EPS = 1e-06

f32 = jnp.float32
bf16 = jnp.bfloat16


def dot(a, b, dims=((1,), (0,))):
    return lax.dot_general(
        a.astype(bf16), b.astype(bf16), (dims, ((), ())), preferred_element_type=f32
    )


NT = ((1,), (1,))
TN = ((0,), (0,))


def split(a):
    high = a.astype(bf16)
    return high, (a - high.astype(f32)).astype(bf16)


def dot3(a, b):
    a_high, a_low = split(a)
    b_high, b_low = split(b)
    return dot(a_high, b_high) + (dot(a_high, b_low) + dot(a_low, b_high))


def unit_lower_inverses(stricts):
    size = stricts[0].shape[0]
    row = lax.broadcasted_iota(jnp.int32, (size, size), 0)
    col = lax.broadcasted_iota(jnp.int32, (size, size), 1)
    eye = jnp.where(row == col, 1.0, 0.0)
    below = (row // 2 == col // 2) & (row != col)
    inverses = [eye - jnp.where(below, strict, 0.0) for strict in stricts]
    width = 2
    while width < size:
        below = (row // (2 * width) == col // (2 * width)) & (row // width != col // width)
        parts = [
            dot(jnp.where(below, strict, 0.0), inverse)
            for strict, inverse in zip(stricts, inverses)
        ]
        inverses = [inverse - dot(inverse, part) for inverse, part in zip(inverses, parts)]
        width *= 2
    errors = [
        eye - inverse - dot3(strict, inverse) for strict, inverse in zip(stricts, inverses)
    ]
    return [inverse + dot(inverse, error) for inverse, error in zip(inverses, errors)]


def sigmoid(x):
    return 1.0 / (1.0 + jnp.exp(-x))


def masks():
    row = lax.broadcasted_iota(jnp.int32, (HALF, HALF), 0)
    col = lax.broadcasted_iota(jnp.int32, (HALF, HALF), 1)
    return row > col, row >= col


def conv_rows(j, proj_ref, halo_ref, conv_ref, rows, lanes):
    length = proj_ref.shape[2]
    rows[0:HALO, :] = halo_ref[j, 0, :, lanes].astype(f32)
    rows[HALO : HALO + length, :] = proj_ref[j, 0, :, lanes].astype(f32)
    mixed = None
    for i in range(CONV):
        start = HALO - (CONV - 1) + i
        term = conv_ref[j, i : i + 1, lanes] * rows[start : start + length, :]
        mixed = term if mixed is None else mixed + term
    return mixed


def column_of(values, at):
    lane = lax.broadcasted_iota(jnp.int32, values.shape, 1)
    return jnp.sum(jnp.where(lane == at, values, 0.0), axis=1, keepdims=True)


def span_kernel(
    heads, proj_ref, halo_ref, conv_ref, strength_ref,
    send_ref, q_ref, k_ref, w_ref, u_ref, gram_ref, score_ref, inv_ref, rows,
):
    lower, lower_diag = masks()
    a, b = slice(0, HALF), slice(HALF, 2 * HALF)
    rights, grams, stricts = [], [], []
    for h in range(heads):
        lanes = slice(h * HEAD_DIM, (h + 1) * HEAD_DIM)
        active = []
        for j in range(3):
            mixed = conv_rows(j, proj_ref, halo_ref, conv_ref, rows.at[h * 3 + j], lanes)
            active.append(mixed * sigmoid(mixed))
        q = active[0] * lax.rsqrt(jnp.sum(active[0] * active[0], axis=1, keepdims=True) + EPS)
        k = active[1] * lax.rsqrt(jnp.sum(active[1] * active[1], axis=1, keepdims=True) + EPS)
        v = active[2]
        q_ref[h] = q.astype(bf16)
        k_ref[h] = k.astype(bf16)
        beta = column_of(strength_ref[0], h)
        gram = dot(k, k, NT)
        score = dot(q, k, NT)
        gaa = jnp.where(lower, gram[a, a], 0.0)
        gbb = jnp.where(lower, gram[b, b], 0.0)
        gba = gram[b, a]
        gram_ref[h, 0] = gaa.astype(bf16)
        gram_ref[h, 1] = gba.astype(bf16)
        gram_ref[h, 2] = gbb.astype(bf16)
        score_ref[h, 0] = jnp.where(lower_diag, score[a, a], 0.0).astype(bf16)
        score_ref[h, 1] = score[b, a].astype(bf16)
        score_ref[h, 2] = jnp.where(lower_diag, score[b, b], 0.0).astype(bf16)
        stricts += [beta[a] * gaa, beta[b] * gbb]
        grams.append((beta[b] * gba).astype(bf16))
        rights.append(beta * jnp.concatenate([k, v], axis=1))
    inverses = unit_lower_inverses(stricts)
    for h in range(heads):
        taa, tbb = inverses[2 * h].astype(bf16), inverses[2 * h + 1].astype(bf16)
        inv_ref[h, 0] = taa
        inv_ref[h, 1] = tbb
        k = k_ref[h]
        top = dot(taa, rights[h][a])
        bottom = dot(tbb, rights[h][b] - dot(grams[h], top))
        w = jnp.concatenate([top[:, :HEAD_DIM], bottom[:, :HEAD_DIM]], axis=0)
        u = jnp.concatenate([top[:, HEAD_DIM:], bottom[:, HEAD_DIM:]], axis=0)
        w_ref[h] = w.astype(bf16)
        u_ref[h] = u.astype(bf16)
        step = -dot(w, k, TN)
        add = dot(u, k, TN)
        groups, rows_each = send_ref.shape[1], send_ref.shape[2] - HEAD_DIM
        for g in range(groups):
            send_ref[h, g, 0:HEAD_DIM, :] = step.astype(bf16)
            send_ref[h, g, HEAD_DIM:, :] = add[g * rows_each : (g + 1) * rows_each].astype(bf16)


def chain_kernel(blocks, recv_ref, out_ref):
    state = jnp.zeros(out_ref.shape[1:], f32)
    for d in range(blocks):
        high, low = split(state)
        out_ref[d] = high
        if d < blocks - 1:
            step = recv_ref[d, 0:HEAD_DIM, :]
            add = recv_ref[d, HEAD_DIM:, :].astype(f32)
            state = state + add + (dot(high, step) + dot(low, step))


def back_chain_kernel(blocks, recv_ref, add_ref, out_ref):
    state = jnp.zeros(out_ref.shape[1:], f32)
    for d in range(blocks - 1, -1, -1):
        high, low = split(state)
        out_ref[d] = high
        if d > 0:
            step = recv_ref[d, 0:HEAD_DIM, :]
            add = add_ref[d].astype(f32)
            state = state + add + (dot(high, step, NT) + dot(low, step, NT))


def mixer_kernel(
    heads, state_ref, q_ref, w_ref, u_ref, score_ref, gain_ref, mask_ref, out_ref, x_ref, mix_ref
):
    a, b = slice(0, HALF), slice(HALF, 2 * HALF)
    mask = mask_ref[0]
    for h in range(heads):
        lanes = slice(h * HEAD_DIM, (h + 1) * HEAD_DIM)
        state = state_ref[h]
        x = u_ref[h].astype(f32) - dot(w_ref[h], state, NT)
        x_ref[h] = x.astype(bf16)
        base = dot(q_ref[h], state, NT)
        top = dot(score_ref[h, 0], x[a])
        bottom = dot(score_ref[h, 1], x[a]) + dot(score_ref[h, 2], x[b])
        mixer = base + jnp.concatenate([top, bottom], axis=0)
        mix_ref[h] = mixer
        inv = lax.rsqrt(jnp.mean(mixer * mixer, axis=1, keepdims=True) + EPS)
        out_ref[0, :, lanes] = (mixer * inv * gain_ref[...] * mask).astype(bf16)


def head_back_kernel(
    heads, grad_ref, mix_ref, gain_ref, mask_ref, q_ref, w_ref, score_ref,
    send_ref, dmix_ref, dx_ref, dgain_ref,
):
    a, b = slice(0, HALF), slice(HALF, 2 * HALF)
    mask = mask_ref[0]
    gain = gain_ref[...]
    for h in range(heads):
        lanes = slice(h * HEAD_DIM, (h + 1) * HEAD_DIM)
        grad = grad_ref[0, :, lanes].astype(f32) * mask
        mixer = mix_ref[h]
        inv = lax.rsqrt(jnp.mean(mixer * mixer, axis=1, keepdims=True) + EPS)
        scaled = mixer * inv
        dgain_ref[h] = jnp.sum(grad * scaled, axis=0, keepdims=True)
        inner = jnp.mean(gain * grad * scaled, axis=1, keepdims=True)
        dmix = inv * (gain * grad - scaled * inner)
        dmix_ref[h] = dmix.astype(bf16)
        top = dot(score_ref[h, 0], dmix[a], TN) + dot(score_ref[h, 1], dmix[b], TN)
        bottom = dot(score_ref[h, 2], dmix[b], TN)
        dx = jnp.concatenate([top, bottom], axis=0)
        dx_ref[h] = dx
        send_ref[h] = (dot(dmix, q_ref[h], TN) - dot(dx, w_ref[h], TN)).astype(bf16)


def span_back_kernel(
    heads, proj_ref, halo_ref, conv_ref, strength_ref, state_ref, dstate_ref,
    x_ref, dmix_ref, dx_ref, gram_ref, inv_ref,
    dproj_ref, tail_ref, ahead_ref, dlogit_ref, dconv_ref, rows, grads,
):
    lower, lower_diag = masks()
    a, b = slice(0, HALF), slice(HALF, 2 * HALF)
    length = proj_ref.shape[2]
    lane = lax.broadcasted_iota(jnp.int32, strength_ref.shape[1:], 1)
    dlogit = jnp.zeros(strength_ref.shape[1:], f32)
    for h in range(heads):
        lanes = slice(h * HEAD_DIM, (h + 1) * HEAD_DIM)
        mixed, sig, active = [], [], []
        for j in range(3):
            mixed.append(conv_rows(j, proj_ref, halo_ref, conv_ref, rows.at[h * 3 + j], lanes))
            sig.append(sigmoid(mixed[j]))
            active.append(mixed[j] * sig[j])
        q_inv = lax.rsqrt(jnp.sum(active[0] * active[0], axis=1, keepdims=True) + EPS)
        k_inv = lax.rsqrt(jnp.sum(active[1] * active[1], axis=1, keepdims=True) + EPS)
        q, k, v = active[0] * q_inv, active[1] * k_inv, active[2]
        kb = k.astype(bf16)
        beta = column_of(strength_ref[0], h)
        state, dstate = state_ref[h], dstate_ref[h]
        x, dmix = x_ref[h], dmix_ref[h]
        gaa, gba, gbb = gram_ref[h, 0], gram_ref[h, 1], gram_ref[h, 2]
        dx = dx_ref[h] + dot(kb, dstate, NT)
        y_b = dot(inv_ref[h, 1], dx[b], TN)
        y_a = dot(inv_ref[h, 0], dx[a] - dot(gba, beta[b] * y_b, TN), TN)
        y = jnp.concatenate([y_a, y_b], axis=0)
        inner = jnp.concatenate([dot(gaa, x[a]), dot(gba, x[a]) + dot(gbb, x[b])], axis=0)
        residual = v - dot(kb, state, NT) - inner
        dbeta = jnp.sum(y * residual, axis=1, keepdims=True)
        dlogit = jnp.where(lane == h, dbeta * beta * (1.0 - beta), dlogit)
        dv = beta * y
        dgram = -dot(dv, x, NT)
        dscore = dot(dmix, x, NT)
        dg_aa = jnp.where(lower, dgram[a, a], 0.0).astype(bf16)
        dg_bb = jnp.where(lower, dgram[b, b], 0.0).astype(bf16)
        dg_ba = dgram[b, a].astype(bf16)
        ds_aa = jnp.where(lower_diag, dscore[a, a], 0.0).astype(bf16)
        ds_bb = jnp.where(lower_diag, dscore[b, b], 0.0).astype(bf16)
        ds_ba = dscore[b, a].astype(bf16)
        qb = q.astype(bf16)
        dq = dot(dmix, state) + jnp.concatenate(
            [dot(ds_aa, kb[a]), dot(ds_ba, kb[a]) + dot(ds_bb, kb[b])], axis=0
        )
        dk = dot(x, dstate) - dot(dv, state)
        dk_a = (
            dot(ds_aa, qb[a], TN) + dot(ds_ba, qb[b], TN)
            + dot(dg_aa, kb[a]) + dot(dg_aa, kb[a], TN) + dot(dg_ba, kb[b], TN)
        )
        dk_b = (
            dot(ds_bb, qb[b], TN) + dot(dg_ba, kb[a])
            + dot(dg_bb, kb[b]) + dot(dg_bb, kb[b], TN)
        )
        dk = dk + jnp.concatenate([dk_a, dk_b], axis=0)
        dact = [
            (dq - q * jnp.sum(q * dq, axis=1, keepdims=True)) * q_inv,
            (dk - k * jnp.sum(k * dk, axis=1, keepdims=True)) * k_inv,
            dv,
        ]
        for j in range(3):
            dmixed = dact[j] * sig[j] * (1.0 + mixed[j] * (1.0 - sig[j]))
            own = rows.at[h * 3 + j]
            pad = grads.at[h * 3 + j]
            pad[0:HALO, :] = jnp.zeros((HALO, HEAD_DIM), f32)
            pad[HALO : HALO + length, :] = dmixed
            pad[HALO + length :, :] = jnp.zeros((HALO, HEAD_DIM), f32)
            whole = None
            for i in range(CONV):
                start = HALO - (CONV - 1) + i
                dconv_ref[j, 0, i : i + 1, lanes] = jnp.sum(
                    dmixed * own[start : start + length, :], axis=0, keepdims=True
                )
                shift = CONV - 1 - i
                term = conv_ref[j, i : i + 1, lanes] * pad[shift : shift + HALO + length, :]
                whole = term if whole is None else whole + term
            ahead_ref[j, 0, :, lanes] = whole[0:HALO].astype(bf16)
            dproj_ref[j, 0, :, lanes] = whole[HALO:].astype(bf16)
            tail_ref[j, 0, :, lanes] = whole[length:]
    dlogit_ref[0] = dlogit


def columns_of(me_ref, offset, count, width):
    return pl.ds(pl.multiple_of(lax.rem(me_ref[0] + offset, count) * width, width), width)


def piece(refs, offset):
    first, second = refs[2 * offset], refs[2 * offset + 1]
    in_first = 2 * pl.program_id(0) < pl.num_programs(0)
    return jnp.where(in_first, first[...].astype(f32), second[...].astype(f32))


def norm_pieces(me_ref, refs, gain_ref, normed_ref, scale_ref):
    count = len(refs) // 2
    values = [piece(refs, i) for i in range(count)]
    width = values[0].shape[1]
    total = None
    for value in values:
        square = jnp.sum(value * value, axis=1, keepdims=True)
        total = square if total is None else total + square
    scale = lax.rsqrt(total / (count * width) + EPS)
    scale_ref[...] = scale
    for i in range(count):
        at = columns_of(me_ref, i, count, width)
        normed_ref[:, at] = (values[i] * scale * gain_ref[:, at]).astype(bf16)


def in_norm_kernel(me_ref, *args):
    *refs, gain_ref, weight_ref, mask_ref, normed_ref, scale_ref, strength_ref = args
    norm_pieces(me_ref, refs, gain_ref, normed_ref, scale_ref)
    strength_ref[...] = sigmoid(dot(normed_ref[...], weight_ref[...])) * mask_ref[...]


def mid_norm_kernel(me_ref, *args):
    *refs, gain_ref, normed_ref, scale_ref = args
    norm_pieces(me_ref, refs, gain_ref, normed_ref, scale_ref)


def mid_back_kernel(me_ref, *args):
    *refs, rows_ref, gain_ref, scale_ref, branch_ref, dot_ref = args
    count = len(refs) // 4
    values = [piece(refs[: 2 * count], i) for i in range(count)]
    grads = [piece(refs[2 * count :], i) for i in range(count)]
    width = values[0].shape[1]
    total = None
    for i in range(count):
        at = columns_of(me_ref, i, count, width)
        grads[i] = grads[i] * gain_ref[:, at]
        inner = jnp.sum(grads[i] * values[i], axis=1, keepdims=True)
        total = inner if total is None else total + inner
    inner = total / (count * width)
    dot_ref[...] = inner
    scale = scale_ref[...]
    cubed = scale * scale * scale * inner
    for i in range(count):
        at = columns_of(me_ref, i, count, width)
        grad = grads[i] * scale - values[i] * cubed
        branch_ref[:, at] = (rows_ref[:, at].astype(f32) + grad).astype(bf16)


def store_halves(block, step, halves):
    length = block.shape[0] // 2
    for i in range(len(halves) // 2):

        @pl.when(step == i)
        def _(first=halves[2 * i], second=halves[2 * i + 1]):
            first[...] = block[:length]
            second[...] = block[length:]


def branch_part_kernel(me_ref, head_ref, weight_ref, *halves):
    store_halves(dot(head_ref[...], weight_ref[...]).astype(bf16), pl.program_id(0), halves)


def mid_part_kernel(me_ref, grad_ref, weight_ref, *halves):
    part = dot(grad_ref[0], weight_ref[0], NT) + dot(grad_ref[1], weight_ref[1], NT)
    store_halves(part.astype(bf16), pl.program_id(0), halves)


def in_part_kernel(
    me_ref, proj_ref, logit_ref, weight_ref, strength_ref, normed_ref, *outs
):
    *halves, inner_ref = outs
    step = pl.program_id(0)
    part = dot(logit_ref[...], strength_ref[...], NT)
    for j in range(3):
        part = part + dot(proj_ref[j], weight_ref[j], NT)
    store_halves(part.astype(bf16), step, halves)
    ones = jnp.ones((8, part.shape[1]), f32)
    product = dot(ones, part * normed_ref[...].astype(f32), NT)

    @pl.when(step == 0)
    def _():
        inner_ref[...] = product

    @pl.when(step > 0)
    def _():
        inner_ref[...] += product


def feed_weights_kernel(normed_ref, grad_ref, gated_ref, features_ref, out_ref):
    step = pl.program_id(0)

    @pl.when(step < 2)
    def _():
        out_ref[...] = dot(normed_ref[...], gated_ref[0], TN).astype(bf16)

    @pl.when(step == 2)
    def _():
        out_ref[...] = dot(grad_ref[...], features_ref[...], TN).astype(bf16)


def gate_kernel(gated_ref, hidden_ref, grad_ref, features_ref):
    gate, up, hidden = gated_ref[0], gated_ref[1], hidden_ref[...]
    sig = sigmoid(gate)
    act = gate * sig
    features_ref[...] = (act * up).astype(bf16)
    grad_ref[0] = (hidden * up * sig * (1.0 + gate * (1.0 - sig))).astype(bf16)
    grad_ref[1] = (hidden * act).astype(bf16)


def store_by_core(core_ref, block, columns, ours_ref, theirs_ref):
    chips, rows, _ = ours_ref.shape

    def store(first, second):
        for chip in range(chips):
            start = 2 * chip * rows
            first[chip, :, columns] = block[start : start + rows]
            second[chip, :, columns] = block[start + rows : start + 2 * rows]

    @pl.when(core_ref[0] == 0)
    def _():
        store(ours_ref, theirs_ref)

    @pl.when(core_ref[0] == 1)
    def _():
        store(theirs_ref, ours_ref)


def mix_weights_kernel(
    core_ref, normed_ref, proj_ref, logit_ref, ours_ref, theirs_ref, strength_ref
):
    count, _, width = proj_ref.shape
    for j in range(count):
        block = dot(normed_ref[...], proj_ref[j], TN).astype(bf16)
        columns = slice(j * width, (j + 1) * width)
        store_by_core(core_ref, block, columns, ours_ref, theirs_ref)
    strength_ref[...] = dot(logit_ref[...], normed_ref[...], TN)


def out_weights_kernel(core_ref, branch_ref, head_ref, ours_ref, theirs_ref):
    block = dot(branch_ref[...], head_ref[...], TN).astype(bf16)
    store_by_core(core_ref, block, slice(0, head_ref.shape[1]), ours_ref, theirs_ref)


def kernel_params():
    return pltpu.CompilerParams(vmem_limit_bytes=20 * 1024 * 1024)


def spec(block, index):
    return pl.BlockSpec(block, index)


def mixer_calls(seqs, length, heads):
    chains = seqs * heads
    width = heads * HEAD_DIM
    at = {
        "proj": spec((3, 1, length, width), lambda s: (0, s, 0, 0)),
        "halo": spec((3, 1, HALO, width), lambda s: (0, s, 0, 0)),
        "conv": spec((3, CONV, width), lambda s: (0, 0, 0)),
        "strength": spec((1, length, heads), lambda s: (s, 0, 0)),
        "tokens": spec((heads, length, HEAD_DIM), lambda s: (s, 0, 0)),
        "state": spec((heads, HEAD_DIM, HEAD_DIM), lambda s: (s, 0, 0)),
        "three": spec((heads, 3, HALF, HALF), lambda s: (s, 0, 0, 0)),
        "two": spec((heads, 2, HALF, HALF), lambda s: (s, 0, 0, 0)),
        "rows": spec((1, length, width), lambda s: (s, 0, 0)),
        "mask": spec((1, length, 1), lambda s: (s, 0, 0)),
        "gain": spec((1, HEAD_DIM), lambda s: (0, 0)),
    }
    shape = {
        "tokens": lambda kind: jax.ShapeDtypeStruct((chains, length, HEAD_DIM), kind),
        "three": jax.ShapeDtypeStruct((chains, 3, HALF, HALF), bf16),
        "two": jax.ShapeDtypeStruct((chains, 2, HALF, HALF), bf16),
    }
    return at, shape


def from_behind(value, axis, steps):
    count = lax.axis_size(axis)
    initial, last = (max(0, -steps), min(count, count - steps))
    return lax.ppermute(value, axis, [(source, source + steps) for source in range(initial, last)])


def exchange(blocks, axis):
    return lax.all_to_all(blocks, axis, 0, 0)


def along_head(value, steps):
    count = lax.axis_size("head")
    return lax.ppermute(value, "head", [(i, (i + steps) % count) for i in range(count)])


def gather_pieces(first, second):
    left_first, right_second = along_head(first, 1), along_head(second, -1)
    left_second, right_first = along_head(second, 1), along_head(first, -1)
    far_first, far_second = along_head(left_first, 1), along_head(right_second, -1)
    return (
        first, second, right_first, right_second,
        far_first, far_second, left_first, left_second,
    )


def reduce_pieces(pieces):
    first, second, right_first, right_second, far_first, far_second, left_first, left_second = pieces
    came_first, came_second = along_head(far_first, 1), along_head(far_second, -1)
    from_left = along_head(right_second, 1)
    from_right = along_head(left_first, -1)
    far_left = along_head((right_first.astype(f32) + came_first.astype(f32)).astype(bf16), 1)
    far_right = along_head((left_second.astype(f32) + came_second.astype(f32)).astype(bf16), -1)
    return (
        first.astype(f32) + from_right.astype(f32) + far_left.astype(f32),
        second.astype(f32) + from_left.astype(f32) + far_right.astype(f32),
    )


def sum_over_blocks(value):
    count = lax.axis_size("seq")
    side = 4
    value = value + lax.ppermute(value, "seq", [(i, i ^ 1) for i in range(count)])
    for stride in (2, 2 * side):
        came = []
        for steps in range(1, side):
            pairs = []
            for i in range(count):
                at = i // stride % side
                pairs.append((i, i + ((at + steps) % side - at) * stride))
            came.append(lax.ppermute(value, "seq", pairs))
        value = value + came[0] + came[1] + came[2]
    return value


def join_cores(ours, theirs):
    count = lax.axis_size("seq")
    came = lax.ppermute(theirs, "seq", [(i, i ^ 1) for i in range(count)])
    return (ours.astype(f32) + came.astype(f32)).astype(bf16)


def exchange_chips(parts):
    count = lax.axis_size("seq")
    groups = [list(range(first, count, 2)) for first in range(2)]
    return lax.all_to_all(parts, "seq", 0, 0, axis_index_groups=groups)


def together(*values):
    return lax.optimization_barrier(values)


def shards(
    tokens,
    lengths,
    norm_gain,
    query_key_value_weight,
    strength_projection,
    conv_weight,
    head_gain,
    output_projection,
    mlp_gain,
    gate_up_weight,
    down_projection,
    out_grad,
):
    seqs, length, width = tokens.shape
    model = norm_gain.shape[0]
    heads = width // HEAD_DIM
    chains = seqs * heads
    rows = seqs * length
    devices = lax.axis_size("head")
    blocks = lax.axis_size("seq")
    groups = blocks // chains
    cols = HEAD_DIM // groups
    hidden = down_projection.shape[0]
    col_start = lax.axis_index("head") * width
    positions = lax.axis_index("seq") * length + jnp.arange(length, dtype=jnp.int32)
    mask = (positions[None, :] < lengths[:, None]).astype(f32)[:, :, None]
    at, shape = mixer_calls(seqs, length, heads)
    gain_row = head_gain[None, :]
    norm_row, mlp_row = norm_gain[None, :], mlp_gain[None, :]
    own = tokens.reshape(rows, width)
    tile = 128
    whole = lambda *size: spec(size, lambda i: (0,) * len(size))
    row_tile = lambda n: spec((tile, n), lambda i: (i, 0))
    part_tile = spec((devices, tile, width), lambda i: (0, i, 0))

    me = lax.axis_index("head").reshape(1)
    half = rows // 2
    first_half = spec((tile, width), lambda i, me: (jnp.minimum(i, half // tile - 1), 0))
    second_half = spec((tile, width), lambda i, me: (jnp.maximum(i - half // tile, 0), 0))
    pieces = [first_half, second_half] * devices
    on = lambda step, offset: lax.rem(step + offset, devices)
    fixed = lambda *size: spec(size, lambda i, me: (0,) * len(size))
    moving = lambda n: spec((tile, n), lambda i, me: (i, 0))

    def on_pieces(kernel, grid, in_specs, out_specs, out_shape):
        return pl.pallas_call(
            kernel,
            grid_spec=pltpu.PrefetchScalarGridSpec(
                num_scalar_prefetch=1, grid=(grid,), in_specs=in_specs, out_specs=out_specs
            ),
            out_shape=out_shape,
            compiler_params=kernel_params(),
        )

    half_shape = jax.ShapeDtypeStruct((half, width), bf16)
    own_halves = (tokens[0], tokens[1])
    full = gather_pieces(*own_halves)
    full, grad_own = together(full, out_grad.reshape(rows, width))
    grad_rows = lax.all_gather(grad_own, "head", axis=1, tiled=True)
    normed_in, in_scale, strength = on_pieces(
        in_norm_kernel,
        rows // tile,
        [*pieces, fixed(1, model), fixed(model, heads), moving(1)],
        [moving(model), moving(1), moving(heads)],
        [
            jax.ShapeDtypeStruct((rows, model), bf16),
            jax.ShapeDtypeStruct((rows, 1), f32),
            jax.ShapeDtypeStruct((rows, heads), f32),
        ],
    )(me, *full, norm_row, strength_projection, mask.reshape(rows, 1))
    strength = strength.reshape(seqs, length, heads)
    projected = jnp.einsum(
        "if,tfw->tiw", normed_in, query_key_value_weight, preferred_element_type=f32
    ).astype(bf16).reshape(3, seqs, length, width)
    halo = from_behind(projected[:, :, length - HALO :, :], "seq", 1)

    send, q, k, w, u, gram, score, inv = pl.pallas_call(
        partial(span_kernel, heads),
        grid=(seqs,),
        in_specs=[at["proj"], at["halo"], at["conv"], at["strength"]],
        out_specs=[
            spec((heads, groups, HEAD_DIM + cols, HEAD_DIM), lambda s: (s, 0, 0, 0)),
            at["tokens"], at["tokens"], at["tokens"], at["tokens"],
            at["three"], at["three"], at["two"],
        ],
        out_shape=[
            pltpu.HBM((chains, groups, HEAD_DIM + cols, HEAD_DIM), bf16),
            *[shape["tokens"](bf16)] * 4,
            shape["three"], shape["three"], shape["two"],
        ],
        scratch_shapes=[pltpu.VMEM((heads * 3, HALO + length, HEAD_DIM), f32)],
        compiler_params=kernel_params(),
    )(projected, halo, conv_weight, strength)

    received = exchange(send.reshape(blocks, HEAD_DIM + cols, HEAD_DIM), "seq")
    hidden_grad = jnp.einsum("xp,hp->xh", grad_rows, down_projection, preferred_element_type=f32)
    received, hidden_grad = together(received, hidden_grad)
    entering = pl.pallas_call(
        partial(chain_kernel, blocks),
        out_shape=jax.ShapeDtypeStruct((blocks, cols, HEAD_DIM), bf16),
        compiler_params=kernel_params(),
    )(received)
    state = exchange(entering, "seq").reshape(chains, HEAD_DIM, HEAD_DIM)

    head_out, x, mixer = pl.pallas_call(
        partial(mixer_kernel, heads),
        grid=(seqs,),
        in_specs=[
            at["state"], at["tokens"], at["tokens"], at["tokens"], at["three"], at["gain"],
            at["mask"],
        ],
        out_specs=[at["rows"], at["tokens"], at["tokens"]],
        out_shape=[
            jax.ShapeDtypeStruct((seqs, length, width), bf16),
            shape["tokens"](bf16),
            shape["tokens"](f32),
        ],
        compiler_params=kernel_params(),
    )(state, q, w, u, score, gain_row, mask)
    head_out = head_out.reshape(rows, width)

    def place(order):
        return lambda i, me: lax.rem(me[0] + sum((i == n) * at for n, at in enumerate(order)), devices)

    order = (2, 1, 3, 0)
    to = place(order)
    came = on_pieces(
        branch_part_kernel,
        devices,
        [fixed(rows, width), spec((width, width), lambda i, me: (0, to(i, me)))],
        [fixed(half, width)] * 8,
        [half_shape] * 8,
    )(me, head_out, output_projection)
    branch = [came[2 * order.index(i // 2) + i % 2] for i in range(8)]
    middle_own = [
        mine.astype(f32) + other for mine, other in zip(own_halves, reduce_pieces(branch))
    ]
    middle = gather_pieces(*[value.astype(bf16) for value in middle_own])
    normed_mid, mid_scale = on_pieces(
        mid_norm_kernel,
        rows // tile,
        [*pieces, fixed(1, model)],
        [moving(model), moving(1)],
        [jax.ShapeDtypeStruct((rows, model), bf16), jax.ShapeDtypeStruct((rows, 1), f32)],
    )(me, *middle, mlp_row)

    gated = jnp.einsum("ux,gxt->gut", normed_mid, gate_up_weight, preferred_element_type=f32)
    gated_grad, features = pl.pallas_call(
        gate_kernel,
        grid=(rows // tile,),
        in_specs=[spec((2, tile, hidden), lambda i: (0, i, 0)), row_tile(hidden)],
        out_specs=[spec((2, tile, hidden), lambda i: (0, i, 0)), row_tile(hidden)],
        out_shape=[
            jax.ShapeDtypeStruct((2, rows, hidden), bf16),
            jax.ShapeDtypeStruct((rows, hidden), bf16),
        ],
        compiler_params=kernel_params(),
    )(gated, hidden_grad)
    mid_parts = []
    for order in ((2,), (1, 3, 0)):
        to = place(order)
        mid_parts += on_pieces(
            mid_part_kernel,
            len(order),
            [
                fixed(2, rows, hidden),
                spec((2, width, hidden), lambda i, me, to=to: (0, to(i, me), 0)),
            ],
            [fixed(half, width)] * (2 * len(order)),
            [half_shape] * (2 * len(order)),
        )(me, gated_grad, gate_up_weight)
    order = (2, 1, 3, 0)
    mid_parts = [mid_parts[2 * order.index(i // 2) + i % 2] for i in range(8)]

    split_rows = 4
    feed_part = pl.pallas_call(
        feed_weights_kernel,
        grid=(3, split_rows),
        in_specs=[
            spec((rows, model // split_rows), lambda j, i: (0, i)),
            spec((rows, model // split_rows), lambda j, i: (0, i)),
            spec((1, rows, hidden), lambda j, i: (jnp.minimum(j, 1), 0, 0)),
            spec((rows, hidden), lambda j, i: (0, 0)),
        ],
        out_specs=spec((model // split_rows, hidden), lambda j, i: (i, j)),
        out_shape=pltpu.HBM((model, 3 * hidden), bf16),
        compiler_params=kernel_params(),
    )(normed_mid, grad_rows, gated_grad, features)
    mid_grad_own = reduce_pieces(mid_parts)
    mid_grad_own, feed_part = together(mid_grad_own, feed_part)
    feed_sum = lax.psum_scatter(feed_part, "seq", scatter_dimension=0, tiled=True)
    mid_grad = gather_pieces(*[value.astype(bf16) for value in mid_grad_own])
    feed = jnp.dot(features, down_projection, preferred_element_type=f32).astype(bf16)
    mid_grad, feed = together(mid_grad, feed)
    feed, feed_sum = together(feed, feed_sum)
    feed_sum = feed_sum.astype(f32)
    feed_own = lax.psum_scatter(feed, "head", scatter_dimension=1, tiled=True).astype(f32)
    output = jnp.concatenate(middle_own) + feed_own

    branch_grad, mid_dot = on_pieces(
        mid_back_kernel,
        rows // tile,
        [*pieces, *pieces, moving(model), fixed(1, model), moving(1)],
        [moving(model), moving(1)],
        [jax.ShapeDtypeStruct((rows, model), bf16), jax.ShapeDtypeStruct((rows, 1), f32)],
    )(me, *middle, *mid_grad, grad_rows, mlp_row, mid_scale)
    own_gain = lax.dynamic_slice_in_dim(mlp_gain, col_start, width, 0)
    middle_grad_own, mlp_gain_part = [], 0.0
    for i in range(2):
        scale, inner = mid_scale[i * half : (i + 1) * half], mid_dot[i * half : (i + 1) * half]
        middle_grad_own.append(
            out_grad[i].astype(f32) + scale * own_gain * mid_grad_own[i]
            - scale * scale * scale * middle_own[i] * inner
        )
        mlp_gain_part += jnp.sum(mid_grad_own[i] * middle_own[i] * scale, axis=0)
    head_grad = jnp.einsum(
        "pj,wj->pw", branch_grad, output_projection, preferred_element_type=f32
    ).astype(bf16).reshape(seqs, length, width)

    send_back, dmix, dx, dgain = pl.pallas_call(
        partial(head_back_kernel, heads),
        grid=(seqs,),
        in_specs=[
            at["rows"], at["tokens"], at["gain"], at["mask"], at["tokens"], at["tokens"],
            at["three"],
        ],
        out_specs=[
            at["state"], at["tokens"], at["tokens"],
            spec((heads, 1, HEAD_DIM), lambda s: (s, 0, 0)),
        ],
        out_shape=[
            jax.ShapeDtypeStruct((chains, HEAD_DIM, HEAD_DIM), bf16),
            shape["tokens"](bf16),
            shape["tokens"](f32),
            jax.ShapeDtypeStruct((chains, 1, HEAD_DIM), f32),
        ],
        compiler_params=kernel_params(),
    )(head_grad, mixer, gain_row, mask, q, w, score)

    steps, rows_own = 4, model // blocks
    chips = blocks // 2
    core = lax.rem(lax.axis_index("seq"), 2).reshape(1)
    by_core = lambda n: spec((chips // steps, rows_own, n), lambda i: (i, 0, 0))
    core_shape = lambda n: jax.ShapeDtypeStruct((chips, rows_own, n), bf16)
    scalar = pl.BlockSpec(memory_space=pltpu.SMEM)
    model_tile = spec((rows, model // steps), lambda i: (0, i))

    added = exchange(send_back.reshape(blocks, cols, HEAD_DIM), "seq")
    out_ours, out_theirs = pl.pallas_call(
        out_weights_kernel,
        grid=(steps,),
        in_specs=[scalar, model_tile, whole(rows, width)],
        out_specs=[by_core(width)] * 2,
        out_shape=[core_shape(width)] * 2,
        compiler_params=kernel_params(),
    )(core, branch_grad, head_out)
    added, out_ours, out_theirs = together(added, out_ours, out_theirs)
    leaving = pl.pallas_call(
        partial(back_chain_kernel, blocks),
        out_shape=jax.ShapeDtypeStruct((blocks, cols, HEAD_DIM), bf16),
        compiler_params=kernel_params(),
    )(received, added)
    dstate = exchange(leaving, "seq").reshape(chains, HEAD_DIM, HEAD_DIM)
    out_joined = join_cores(out_ours, out_theirs)
    dstate, out_joined = together(dstate, out_joined)
    out_spread = exchange_chips(out_joined)

    dproj, tail, ahead, dlogit, dconv = pl.pallas_call(
        partial(span_back_kernel, heads),
        grid=(seqs,),
        in_specs=[
            at["proj"], at["halo"], at["conv"], at["strength"], at["state"], at["state"],
            at["tokens"], at["tokens"], at["tokens"], at["three"], at["two"],
        ],
        out_specs=[
            at["proj"], at["halo"], at["halo"], at["strength"],
            spec((3, 1, CONV, width), lambda s: (0, s, 0, 0)),
        ],
        out_shape=[
            jax.ShapeDtypeStruct((3, seqs, length, width), bf16),
            jax.ShapeDtypeStruct((3, seqs, HALO, width), f32),
            jax.ShapeDtypeStruct((3, seqs, HALO, width), bf16),
            jax.ShapeDtypeStruct((seqs, length, heads), f32),
            jax.ShapeDtypeStruct((3, seqs, CONV, width), f32),
        ],
        scratch_shapes=[
            pltpu.VMEM((heads * 3, HALO + length, HEAD_DIM), f32),
            pltpu.VMEM((heads * 3, 2 * HALO + length, HEAD_DIM), f32),
        ],
        compiler_params=kernel_params(),
    )(projected, halo, conv_weight, strength, state, dstate, x, dmix, dx, gram, inv)

    sent_back = from_behind(ahead, "seq", -1).astype(f32)
    proj_grad = lax.dynamic_update_slice_in_dim(
        dproj, (tail + sent_back).astype(bf16), length - HALO, 2
    ).reshape(3, rows, width)
    logit_grad = dlogit.astype(bf16).reshape(rows, heads)

    mix_ours, mix_theirs, strength_part = pl.pallas_call(
        mix_weights_kernel,
        grid=(steps,),
        in_specs=[scalar, model_tile, whole(3, rows, width), whole(rows, heads)],
        out_specs=[by_core(3 * width)] * 2 + [spec((heads, model // steps), lambda i: (0, i))],
        out_shape=[core_shape(3 * width)] * 2 + [jax.ShapeDtypeStruct((heads, model), f32)],
        compiler_params=kernel_params(),
    )(core, normed_in, proj_grad, logit_grad)
    mix_ours, mix_theirs, out_spread = together(mix_ours, mix_theirs, out_spread)
    out_sum = jnp.sum(out_spread.astype(f32), axis=0)
    mix_joined = join_cores(mix_ours, mix_theirs)

    in_parts, inners = [], []
    for order in ((2,), (1, 3, 0)):
        to = place(order)
        *parts, inner = on_pieces(
            in_part_kernel,
            len(order),
            [
                fixed(3, rows, width), fixed(rows, heads),
                spec((3, width, width), lambda i, me, to=to: (0, to(i, me), 0)),
                spec((width, heads), lambda i, me, to=to: (to(i, me), 0)),
                spec((rows, width), lambda i, me, to=to: (0, to(i, me))),
            ],
            [fixed(half, width)] * (2 * len(order)) + [fixed(8, rows)],
            [half_shape] * (2 * len(order)) + [jax.ShapeDtypeStruct((8, rows), f32)],
        )(me, proj_grad, logit_grad, query_key_value_weight, strength_projection, normed_in)
        in_parts += parts
        inners.append(inner[0:1])
    order = (2, 1, 3, 0)
    in_parts = [in_parts[2 * order.index(i // 2) + i % 2] for i in range(8)]
    in_grad = reduce_pieces(in_parts)
    by_head = jnp.concatenate(
        [inners[0] + inners[1], jnp.pad(jnp.sum(dgain, axis=0), ((0, 0), (0, rows - HEAD_DIM)))]
    )
    by_head = by_head + along_head(by_head, 2)
    by_head = by_head + along_head(by_head, 1)
    in_dot = by_head[0][:, None] / model
    in_gain = lax.dynamic_slice_in_dim(norm_gain, col_start, width, 0)
    tokens_grad, norm_gain_part = [], 0.0
    for i in range(2):
        scale, inner = in_scale[i * half : (i + 1) * half], in_dot[i * half : (i + 1) * half]
        mine = own_halves[i].astype(f32)
        tokens_grad.append(
            scale * in_gain * in_grad[i] - scale * scale * mine * inner + middle_grad_own[i]
        )
        norm_gain_part += jnp.sum(in_grad[i] * mine * scale, axis=0)
    tokens_grad = jnp.stack(tokens_grad).astype(bf16)

    each, gain_each = width // blocks, HEAD_DIM // blocks
    small = jnp.concatenate(
        [
            jnp.sum(dconv, axis=1).reshape(3 * CONV, width),
            norm_gain_part[None],
            mlp_gain_part[None],
            by_head[1:2, :width],
            strength_part.reshape(heads * model // width, width),
        ]
    )
    small = sum_over_blocks(small)
    mine = lax.axis_index("seq")
    by_block = lax.dynamic_slice_in_dim(small[: 3 * CONV + 2], mine * each, each, 1)
    head_gain_own = lax.dynamic_slice_in_dim(small[3 * CONV + 2], mine * gain_each, gain_each, 0)
    strength_own = lax.dynamic_slice_in_dim(
        small[3 * CONV + 3 :].reshape(heads, model), mine * rows_own, rows_own, 1
    )
    mix_sum = jnp.sum(exchange_chips(mix_joined).astype(f32), axis=0)
    qkv_grad = jnp.moveaxis(mix_sum.reshape(rows_own, 3, width), 1, 0)
    return (
        output.astype(bf16).reshape(seqs, length, width),
        tokens_grad,
        by_block[3 * CONV],
        qkv_grad,
        strength_own.T,
        by_block[: 3 * CONV].reshape(3, CONV, each),
        head_gain_own,
        out_sum.T,
        by_block[3 * CONV + 1],
        jnp.moveaxis(feed_sum[:, : 2 * hidden].reshape(rows_own, 2, hidden), 1, 0),
        feed_sum[:, 2 * hidden :].T,
    )


def solution(mesh):
    return jax.shard_map(
        shards,
        mesh=mesh,
        in_specs=(
            P(None, "seq", "head"),
            P(),
            P(),
            P(None, None, "head"),
            P(None, "head"),
            P(None, None, "head"),
            P(),
            P("head", None),
            P(),
            P(None, None, "head"),
            P("head", None),
            P(None, "seq", "head"),
        ),
        out_specs=(
            P(None, "seq", "head"),
            P(None, "seq", "head"),
            P(("head", "seq")),
            P(None, "seq", "head"),
            P("seq", "head"),
            P(None, None, ("head", "seq")),
            P("seq"),
            P("head", "seq"),
            P(("head", "seq")),
            P(None, "seq", "head"),
            P("head", "seq"),
        ),
        check_vma=False,
    )
```

```python
from functools import partial

import jax
import jax.numpy as jnp
from jax import lax
from jax.experimental import pallas as pl
from jax.experimental.pallas import tpu as pltpu
from jax.sharding import PartitionSpec as P

HEAD_DIM = 128
CONV = 4
HALF = 128
HALO = 8
EPS = 1e-06

f32 = jnp.float32
bf16 = jnp.bfloat16


def dot(a, b, dims=((1,), (0,))):
    return lax.dot_general(
        a.astype(bf16), b.astype(bf16), (dims, ((), ())), preferred_element_type=f32
    )


NT = ((1,), (1,))
TN = ((0,), (0,))


def split(a):
    high = a.astype(bf16)
    return high, (a - high.astype(f32)).astype(bf16)


def dot3(a, b):
    a_high, a_low = split(a)
    b_high, b_low = split(b)
    return dot(a_high, b_high) + (dot(a_high, b_low) + dot(a_low, b_high))


def unit_lower_inverses(stricts):
    size = stricts[0].shape[0]
    row = lax.broadcasted_iota(jnp.int32, (size, size), 0)
    col = lax.broadcasted_iota(jnp.int32, (size, size), 1)
    eye = jnp.where(row == col, 1.0, 0.0)
    below = (row // 2 == col // 2) & (row != col)
    inverses = [eye - jnp.where(below, strict, 0.0) for strict in stricts]
    width = 2
    while width < size:
        below = (row // (2 * width) == col // (2 * width)) & (row // width != col // width)
        parts = [
            dot(jnp.where(below, strict, 0.0), inverse)
            for strict, inverse in zip(stricts, inverses)
        ]
        inverses = [inverse - dot(inverse, part) for inverse, part in zip(inverses, parts)]
        width *= 2
    errors = [
        eye - inverse - dot3(strict, inverse) for strict, inverse in zip(stricts, inverses)
    ]
    return [inverse + dot(inverse, error) for inverse, error in zip(inverses, errors)]


def sigmoid(x):
    return 1.0 / (1.0 + jnp.exp(-x))


def masks():
    row = lax.broadcasted_iota(jnp.int32, (HALF, HALF), 0)
    col = lax.broadcasted_iota(jnp.int32, (HALF, HALF), 1)
    return row > col, row >= col


def conv_rows(j, proj_ref, halo_ref, conv_ref, rows, lanes):
    length = proj_ref.shape[2]
    rows[0:HALO, :] = halo_ref[j, 0, :, lanes].astype(f32)
    rows[HALO : HALO + length, :] = proj_ref[j, 0, :, lanes].astype(f32)
    mixed = None
    for i in range(CONV):
        start = HALO - (CONV - 1) + i
        term = conv_ref[j, i : i + 1, lanes] * rows[start : start + length, :]
        mixed = term if mixed is None else mixed + term
    return mixed


def column_of(values, at):
    lane = lax.broadcasted_iota(jnp.int32, values.shape, 1)
    return jnp.sum(jnp.where(lane == at, values, 0.0), axis=1, keepdims=True)


def span_kernel(
    heads, proj_ref, halo_ref, conv_ref, strength_ref,
    send_ref, q_ref, k_ref, w_ref, u_ref, gram_ref, score_ref, inv_ref, rows,
):
    lower, lower_diag = masks()
    a, b = slice(0, HALF), slice(HALF, 2 * HALF)
    rights, grams, stricts = [], [], []
    for h in range(heads):
        lanes = slice(h * HEAD_DIM, (h + 1) * HEAD_DIM)
        active = []
        for j in range(3):
            mixed = conv_rows(j, proj_ref, halo_ref, conv_ref, rows.at[h * 3 + j], lanes)
            active.append(mixed * sigmoid(mixed))
        q = active[0] * lax.rsqrt(jnp.sum(active[0] * active[0], axis=1, keepdims=True) + EPS)
        k = active[1] * lax.rsqrt(jnp.sum(active[1] * active[1], axis=1, keepdims=True) + EPS)
        v = active[2]
        q_ref[h] = q.astype(bf16)
        k_ref[h] = k.astype(bf16)
        beta = column_of(strength_ref[0], h)
        gram = dot(k, k, NT)
        score = dot(q, k, NT)
        gaa = jnp.where(lower, gram[a, a], 0.0)
        gbb = jnp.where(lower, gram[b, b], 0.0)
        gba = gram[b, a]
        gram_ref[h, 0] = gaa.astype(bf16)
        gram_ref[h, 1] = gba.astype(bf16)
        gram_ref[h, 2] = gbb.astype(bf16)
        score_ref[h, 0] = jnp.where(lower_diag, score[a, a], 0.0).astype(bf16)
        score_ref[h, 1] = score[b, a].astype(bf16)
        score_ref[h, 2] = jnp.where(lower_diag, score[b, b], 0.0).astype(bf16)
        stricts += [beta[a] * gaa, beta[b] * gbb]
        grams.append((beta[b] * gba).astype(bf16))
        rights.append(beta * jnp.concatenate([k, v], axis=1))
    inverses = unit_lower_inverses(stricts)
    for h in range(heads):
        taa, tbb = inverses[2 * h].astype(bf16), inverses[2 * h + 1].astype(bf16)
        inv_ref[h, 0] = taa
        inv_ref[h, 1] = tbb
        k = k_ref[h]
        top = dot(taa, rights[h][a])
        bottom = dot(tbb, rights[h][b] - dot(grams[h], top))
        w = jnp.concatenate([top[:, :HEAD_DIM], bottom[:, :HEAD_DIM]], axis=0)
        u = jnp.concatenate([top[:, HEAD_DIM:], bottom[:, HEAD_DIM:]], axis=0)
        w_ref[h] = w.astype(bf16)
        u_ref[h] = u.astype(bf16)
        step = -dot(w, k, TN)
        add = dot(u, k, TN)
        send_ref[h, 0:HEAD_DIM, :] = step.astype(bf16)
        send_ref[h, HEAD_DIM:, :] = add.astype(bf16)


def through(state, block):
    high, low = split(state)
    step = block[:HEAD_DIM]
    return state + dot(high, step) + dot(low, step)


def through_back(state, block):
    high, low = split(state)
    step = block[:HEAD_DIM]
    return state + dot(high, step, NT) + dot(low, step, NT)


def added(block):
    return block[HEAD_DIM:].astype(f32)


def chip_kernel(place_ref, own_ref, came_ref, out_ref, maps_ref):
    mine_first = place_ref[2] == 0
    for c in range(out_ref.shape[0]):
        own, came = own_ref[c].astype(f32), came_ref[c].astype(f32)
        first = jnp.where(mine_first, own, came)
        second = jnp.where(mine_first, came, own)
        maps_ref[0, c] = first[:HEAD_DIM].astype(bf16)
        step = second[:HEAD_DIM].astype(bf16)
        maps_ref[1, c] = step
        out_ref[c] = (first + second + dot(first, step)).astype(bf16)


def plane_kernel(place_ref, own_ref, one_ref, two_ref, three_ref, out_ref, maps_ref, stack):
    count = stack.shape[0]
    for at, ref in enumerate((own_ref, one_ref, two_ref, three_ref)):
        stack[lax.rem(place_ref[1] - at + count, count)] = ref[...]
    maps_ref[...] = stack[:, :, :HEAD_DIM]
    for c in range(out_ref.shape[0]):
        total = None
        for y in range(count):
            block = stack[y, c]
            if total is None:
                total = block.astype(f32)
            else:
                total = through(total, block) + block.astype(f32)
        out_ref[c] = total.astype(bf16)


def enter_kernel(place_ref, *refs):
    planes, chips, (own_ref, came_ref) = refs[:4], refs[4:8], refs[8:10]
    ours_ref, theirs_ref, maps_ref = refs[10:]
    chains, count = ours_ref.shape[0], len(planes)
    for at in range(count):
        maps_ref[lax.rem(place_ref[0] - at + count, count)] = planes[at][:, :HEAD_DIM]
    states = [jnp.zeros((HEAD_DIM, HEAD_DIM), f32)] * chains
    for level, blocks in ((0, planes), (1, chips)):
        for back in range(count - 1, 0, -1):
            reached = back <= place_ref[level]
            for c in range(chains):
                block = blocks[back][c]
                after = through(states[c], block) + added(block)
                states[c] = jnp.where(reached, after, states[c])
    mine_first = place_ref[2] == 0
    for c in range(chains):
        first = jnp.where(mine_first, own_ref[c].astype(f32), came_ref[c].astype(f32))
        after = through(states[c], first.astype(bf16)) + added(first)
        ours_ref[c] = jnp.where(mine_first, states[c], after).astype(bf16)
        theirs_ref[c] = jnp.where(mine_first, after, states[c]).astype(bf16)


def back_chip_kernel(place_ref, maps_ref, own_ref, came_ref, out_ref, adds_ref):
    mine_first = place_ref[2] == 0
    for c in range(out_ref.shape[0]):
        own, came = own_ref[c].astype(f32), came_ref[c].astype(f32)
        last = jnp.where(mine_first, came, own)
        add = jnp.where(mine_first, own, came)
        adds_ref[c] = last.astype(bf16)
        out_ref[c] = (through_back(last, maps_ref[0, c]) + add).astype(bf16)


def back_plane_kernel(place_ref, maps_ref, *refs):
    adds, (out_ref, adds_ref) = refs[:4], refs[4:]
    count = len(adds)
    for at in range(count):
        adds_ref[lax.rem(place_ref[1] - at + count, count)] = adds[at][...]
    for c in range(out_ref.shape[0]):
        total = None
        for y in range(count - 1, -1, -1):
            add = adds_ref[y, c].astype(f32)
            total = add if total is None else through_back(total, maps_ref[y, c]) + add
        out_ref[c] = total.astype(bf16)


def back_enter_kernel(place_ref, core_maps, chip_maps, plane_maps, last_adds, chip_adds, *refs):
    plane_adds, (ours_ref, theirs_ref, stack) = refs[:4], refs[4:]
    chains, count = ours_ref.shape[0], len(plane_adds)
    for at in range(count):
        stack[lax.rem(place_ref[0] - at + count, count)] = plane_adds[at][...]
    states = [jnp.zeros((HEAD_DIM, HEAD_DIM), f32)] * chains
    for level, maps, adds in ((0, plane_maps, stack), (1, chip_maps, chip_adds)):
        for at in range(count - 1, 0, -1):
            reached = at > place_ref[level]
            for c in range(chains):
                after = through_back(states[c], maps[at, c]) + adds[at, c].astype(f32)
                states[c] = jnp.where(reached, after, states[c])
    mine_first = place_ref[2] == 0
    for c in range(chains):
        after = through_back(states[c], core_maps[1, c]) + last_adds[c].astype(f32)
        ours_ref[c] = jnp.where(mine_first, after, states[c]).astype(bf16)
        theirs_ref[c] = jnp.where(mine_first, states[c], after).astype(bf16)


def state_of(place_ref, ours_ref, came_ref, h):
    mine = pl.program_id(0) == place_ref[2]
    return jnp.where(mine, ours_ref[h].astype(f32), came_ref[h].astype(f32)).astype(bf16)


def mixer_kernel(
    heads, place_ref, ours_ref, came_ref, q_ref, w_ref, u_ref, score_ref, gain_ref, mask_ref,
    out_ref, x_ref, mix_ref,
):
    a, b = slice(0, HALF), slice(HALF, 2 * HALF)
    mask = mask_ref[0]
    for h in range(heads):
        lanes = slice(h * HEAD_DIM, (h + 1) * HEAD_DIM)
        state = state_of(place_ref, ours_ref, came_ref, h)
        x = u_ref[h].astype(f32) - dot(w_ref[h], state, NT)
        x_ref[h] = x.astype(bf16)
        base = dot(q_ref[h], state, NT)
        top = dot(score_ref[h, 0], x[a])
        bottom = dot(score_ref[h, 1], x[a]) + dot(score_ref[h, 2], x[b])
        mixer = base + jnp.concatenate([top, bottom], axis=0)
        mix_ref[h] = mixer
        inv = lax.rsqrt(jnp.mean(mixer * mixer, axis=1, keepdims=True) + EPS)
        out_ref[0, :, lanes] = (mixer * inv * gain_ref[...] * mask).astype(bf16)


def head_back_kernel(
    heads, grad_ref, mix_ref, gain_ref, mask_ref, q_ref, w_ref, score_ref,
    send_ref, dmix_ref, dx_ref, dgain_ref,
):
    a, b = slice(0, HALF), slice(HALF, 2 * HALF)
    mask = mask_ref[0]
    gain = gain_ref[...]
    for h in range(heads):
        lanes = slice(h * HEAD_DIM, (h + 1) * HEAD_DIM)
        grad = grad_ref[0, :, lanes].astype(f32) * mask
        mixer = mix_ref[h]
        inv = lax.rsqrt(jnp.mean(mixer * mixer, axis=1, keepdims=True) + EPS)
        scaled = mixer * inv
        dgain_ref[h] = jnp.sum(grad * scaled, axis=0, keepdims=True)
        inner = jnp.mean(gain * grad * scaled, axis=1, keepdims=True)
        dmix = inv * (gain * grad - scaled * inner)
        dmix_ref[h] = dmix.astype(bf16)
        top = dot(score_ref[h, 0], dmix[a], TN) + dot(score_ref[h, 1], dmix[b], TN)
        bottom = dot(score_ref[h, 2], dmix[b], TN)
        dx = jnp.concatenate([top, bottom], axis=0)
        dx_ref[h] = dx
        send_ref[h] = (dot(dmix, q_ref[h], TN) - dot(dx, w_ref[h], TN)).astype(bf16)


def span_back_kernel(
    heads, place_ref, ours_ref, came_ref, dours_ref, dcame_ref,
    proj_ref, halo_ref, conv_ref, strength_ref,
    x_ref, dmix_ref, dx_ref, gram_ref, inv_ref,
    dproj_ref, tail_ref, ahead_ref, dlogit_ref, dconv_ref, rows, grads,
):
    lower, lower_diag = masks()
    a, b = slice(0, HALF), slice(HALF, 2 * HALF)
    length = proj_ref.shape[2]
    lane = lax.broadcasted_iota(jnp.int32, strength_ref.shape[1:], 1)
    dlogit = jnp.zeros(strength_ref.shape[1:], f32)
    for h in range(heads):
        lanes = slice(h * HEAD_DIM, (h + 1) * HEAD_DIM)
        mixed, sig, active = [], [], []
        for j in range(3):
            mixed.append(conv_rows(j, proj_ref, halo_ref, conv_ref, rows.at[h * 3 + j], lanes))
            sig.append(sigmoid(mixed[j]))
            active.append(mixed[j] * sig[j])
        q_inv = lax.rsqrt(jnp.sum(active[0] * active[0], axis=1, keepdims=True) + EPS)
        k_inv = lax.rsqrt(jnp.sum(active[1] * active[1], axis=1, keepdims=True) + EPS)
        q, k, v = active[0] * q_inv, active[1] * k_inv, active[2]
        kb = k.astype(bf16)
        beta = column_of(strength_ref[0], h)
        state = state_of(place_ref, ours_ref, came_ref, h)
        dstate = state_of(place_ref, dours_ref, dcame_ref, h)
        x, dmix = x_ref[h], dmix_ref[h]
        gaa, gba, gbb = gram_ref[h, 0], gram_ref[h, 1], gram_ref[h, 2]
        dx = dx_ref[h] + dot(kb, dstate, NT)
        y_b = dot(inv_ref[h, 1], dx[b], TN)
        y_a = dot(inv_ref[h, 0], dx[a] - dot(gba, beta[b] * y_b, TN), TN)
        y = jnp.concatenate([y_a, y_b], axis=0)
        inner = jnp.concatenate([dot(gaa, x[a]), dot(gba, x[a]) + dot(gbb, x[b])], axis=0)
        residual = v - dot(kb, state, NT) - inner
        dbeta = jnp.sum(y * residual, axis=1, keepdims=True)
        dlogit = jnp.where(lane == h, dbeta * beta * (1.0 - beta), dlogit)
        dv = beta * y
        dgram = -dot(dv, x, NT)
        dscore = dot(dmix, x, NT)
        dg_aa = jnp.where(lower, dgram[a, a], 0.0).astype(bf16)
        dg_bb = jnp.where(lower, dgram[b, b], 0.0).astype(bf16)
        dg_ba = dgram[b, a].astype(bf16)
        ds_aa = jnp.where(lower_diag, dscore[a, a], 0.0).astype(bf16)
        ds_bb = jnp.where(lower_diag, dscore[b, b], 0.0).astype(bf16)
        ds_ba = dscore[b, a].astype(bf16)
        qb = q.astype(bf16)
        dq = dot(dmix, state) + jnp.concatenate(
            [dot(ds_aa, kb[a]), dot(ds_ba, kb[a]) + dot(ds_bb, kb[b])], axis=0
        )
        dk = dot(x, dstate) - dot(dv, state)
        dk_a = (
            dot(ds_aa, qb[a], TN) + dot(ds_ba, qb[b], TN)
            + dot(dg_aa, kb[a]) + dot(dg_aa, kb[a], TN) + dot(dg_ba, kb[b], TN)
        )
        dk_b = (
            dot(ds_bb, qb[b], TN) + dot(dg_ba, kb[a])
            + dot(dg_bb, kb[b]) + dot(dg_bb, kb[b], TN)
        )
        dk = dk + jnp.concatenate([dk_a, dk_b], axis=0)
        dact = [
            (dq - q * jnp.sum(q * dq, axis=1, keepdims=True)) * q_inv,
            (dk - k * jnp.sum(k * dk, axis=1, keepdims=True)) * k_inv,
            dv,
        ]
        for j in range(3):
            dmixed = dact[j] * sig[j] * (1.0 + mixed[j] * (1.0 - sig[j]))
            own = rows.at[h * 3 + j]
            pad = grads.at[h * 3 + j]
            pad[0:HALO, :] = jnp.zeros((HALO, HEAD_DIM), f32)
            pad[HALO : HALO + length, :] = dmixed
            pad[HALO + length :, :] = jnp.zeros((HALO, HEAD_DIM), f32)
            whole = None
            for i in range(CONV):
                start = HALO - (CONV - 1) + i
                dconv_ref[j, 0, i : i + 1, lanes] = jnp.sum(
                    dmixed * own[start : start + length, :], axis=0, keepdims=True
                )
                shift = CONV - 1 - i
                term = conv_ref[j, i : i + 1, lanes] * pad[shift : shift + HALO + length, :]
                whole = term if whole is None else whole + term
            ahead_ref[j, 0, :, lanes] = whole[0:HALO].astype(bf16)
            dproj_ref[j, 0, :, lanes] = whole[HALO:].astype(bf16)
            tail_ref[j, 0, :, lanes] = whole[length:]
    dlogit_ref[0] = dlogit


def columns_of(me_ref, offset, count, width):
    return pl.ds(pl.multiple_of(lax.rem(me_ref[0] + offset, count) * width, width), width)


def piece(refs, offset):
    first, second = refs[2 * offset], refs[2 * offset + 1]
    in_first = 2 * pl.program_id(0) < pl.num_programs(0)
    return jnp.where(in_first, first[...].astype(f32), second[...].astype(f32))


def norm_pieces(me_ref, refs, gain_ref, normed_ref, scale_ref):
    count = len(refs) // 2
    values = [piece(refs, i) for i in range(count)]
    width = values[0].shape[1]
    total = None
    for value in values:
        square = jnp.sum(value * value, axis=1, keepdims=True)
        total = square if total is None else total + square
    scale = lax.rsqrt(total / (count * width) + EPS)
    scale_ref[...] = scale
    for i in range(count):
        at = columns_of(me_ref, i, count, width)
        normed_ref[:, at] = (values[i] * scale * gain_ref[:, at]).astype(bf16)


def in_norm_kernel(me_ref, *args):
    *refs, gain_ref, weight_ref, mask_ref, normed_ref, scale_ref, strength_ref = args
    norm_pieces(me_ref, refs, gain_ref, normed_ref, scale_ref)
    strength_ref[...] = sigmoid(dot(normed_ref[...], weight_ref[...], NT)) * mask_ref[...]


def mid_norm_kernel(me_ref, *args):
    *refs, gain_ref, normed_ref, scale_ref = args
    norm_pieces(me_ref, refs, gain_ref, normed_ref, scale_ref)


def mid_back_kernel(me_ref, *args):
    *refs, rows_ref, gain_ref, scale_ref, branch_ref, dot_ref = args
    count = len(refs) // 4
    values = [piece(refs[: 2 * count], i) for i in range(count)]
    grads = [piece(refs[2 * count :], i) for i in range(count)]
    width = values[0].shape[1]
    total = None
    for i in range(count):
        at = columns_of(me_ref, i, count, width)
        grads[i] = grads[i] * gain_ref[:, at]
        inner = jnp.sum(grads[i] * values[i], axis=1, keepdims=True)
        total = inner if total is None else total + inner
    inner = total / (count * width)
    dot_ref[...] = inner
    scale = scale_ref[...]
    cubed = scale * scale * scale * inner
    for i in range(count):
        at = columns_of(me_ref, i, count, width)
        grad = grads[i] * scale - values[i] * cubed
        branch_ref[:, at] = (rows_ref[:, at].astype(f32) + grad).astype(bf16)


def store_halves(block, step, halves):
    length = block.shape[0] // 2
    for i in range(len(halves) // 2):

        @pl.when(step == i)
        def _(first=halves[2 * i], second=halves[2 * i + 1]):
            first[...] = block[:length]
            second[...] = block[length:]


def branch_part_kernel(me_ref, head_ref, weight_ref, *halves):
    store_halves(dot(head_ref[...], weight_ref[...]).astype(bf16), pl.program_id(0), halves)


def mid_part_kernel(me_ref, grad_ref, weight_ref, *halves):
    part = dot(grad_ref[0], weight_ref[0], NT) + dot(grad_ref[1], weight_ref[1], NT)
    store_halves(part.astype(bf16), pl.program_id(0), halves)


def in_part_kernel(
    me_ref, proj_ref, logit_ref, weight_ref, strength_ref, normed_ref, *outs
):
    *halves, inner_ref = outs
    step = pl.program_id(0)
    part = dot(logit_ref[...], strength_ref[...])
    for j in range(3):
        part = part + dot(proj_ref[j], weight_ref[j], NT)
    store_halves(part.astype(bf16), step, halves)
    ones = jnp.ones((8, part.shape[1]), f32)
    product = dot(ones, part * normed_ref[...].astype(f32), NT)

    @pl.when(step == 0)
    def _():
        inner_ref[...] = product

    @pl.when(step > 0)
    def _():
        inner_ref[...] += product


def feed_weights_kernel(left_ref, right_ref, *refs):
    refs[-1][...] = dot(left_ref[...], right_ref[...], TN).astype(bf16)


def gate_kernel(gated_ref, hidden_ref, grad_ref, features_ref):
    gate, up, hidden = gated_ref[0], gated_ref[1], hidden_ref[...]
    sig = sigmoid(gate)
    act = gate * sig
    features_ref[...] = (act * up).astype(bf16)
    grad_ref[0] = (hidden * up * sig * (1.0 + gate * (1.0 - sig))).astype(bf16)
    grad_ref[1] = (hidden * act).astype(bf16)


def store_by_core(core_ref, block, columns, ours_ref, theirs_ref):
    chips, rows, _ = ours_ref.shape

    def store(first, second):
        for chip in range(chips):
            start = 2 * chip * rows
            first[chip, :, columns] = block[start : start + rows]
            second[chip, :, columns] = block[start + rows : start + 2 * rows]

    @pl.when(core_ref[0] == 0)
    def _():
        store(ours_ref, theirs_ref)

    @pl.when(core_ref[0] == 1)
    def _():
        store(theirs_ref, ours_ref)


def mix_weights_kernel(
    core_ref, normed_ref, proj_ref, logit_ref, weight_ref, strength_weight_ref,
    ours_ref, theirs_ref, strength_ref, gain_ref,
):
    count, _, width = proj_ref.shape
    total = None
    for j in range(count):
        block = dot(normed_ref[...], proj_ref[j], TN)
        product = block * weight_ref[j].astype(f32)
        total = product if total is None else total + product
        columns = slice(j * width, (j + 1) * width)
        store_by_core(core_ref, block.astype(bf16), columns, ours_ref, theirs_ref)
    strength = dot(logit_ref[...], normed_ref[...], TN)
    strength_ref[...] = strength
    high, low = split(total)
    ones = jnp.ones((8, width), bf16)
    extra = jnp.sum(strength * strength_weight_ref[...].astype(f32), axis=0, keepdims=True)
    gain_ref[...] = dot(ones, high, NT) + dot(ones, low, NT) + extra


def out_weights_kernel(core_ref, branch_ref, head_ref, ours_ref, theirs_ref):
    block = dot(branch_ref[...], head_ref[...], TN).astype(bf16)
    store_by_core(core_ref, block, slice(0, head_ref.shape[1]), ours_ref, theirs_ref)


def in_hbm(*values):
    return [pltpu.with_memory_space_constraint(value, pltpu.HBM) for value in values]


def cost(microseconds):
    return pl.CostEstimate(
        flops=0, bytes_accessed=int(microseconds * 3_000_000), transcendentals=0
    )


def kernel_params():
    return pltpu.CompilerParams(vmem_limit_bytes=20 * 1024 * 1024)


def spec(block, index):
    return pl.BlockSpec(block, index)


def mixer_calls(seqs, length, heads):
    chains = seqs * heads
    width = heads * HEAD_DIM
    at = {
        "proj": spec((3, 1, length, width), lambda s: (0, s, 0, 0)),
        "halo": spec((3, 1, HALO, width), lambda s: (0, s, 0, 0)),
        "conv": spec((3, CONV, width), lambda s: (0, 0, 0)),
        "strength": spec((1, length, heads), lambda s: (s, 0, 0)),
        "tokens": spec((heads, length, HEAD_DIM), lambda s: (s, 0, 0)),
        "fixed": spec((heads, HEAD_DIM, HEAD_DIM), lambda s: (0, 0, 0)),
        "state": spec((heads, HEAD_DIM, HEAD_DIM), lambda s: (s, 0, 0)),
        "three": spec((heads, 3, HALF, HALF), lambda s: (s, 0, 0, 0)),
        "two": spec((heads, 2, HALF, HALF), lambda s: (s, 0, 0, 0)),
        "rows": spec((1, length, width), lambda s: (s, 0, 0)),
        "mask": spec((1, length, 1), lambda s: (s, 0, 0)),
        "gain": spec((1, HEAD_DIM), lambda s: (0, 0)),
    }
    shape = {
        "tokens": lambda kind: pltpu.HBM((chains, length, HEAD_DIM), kind),
        "three": pltpu.HBM((chains, 3, HALF, HALF), bf16),
        "two": pltpu.HBM((chains, 2, HALF, HALF), bf16),
    }
    return at, shape


def from_behind(value, axis, steps):
    count = lax.axis_size(axis)
    initial, last = (max(0, -steps), min(count, count - steps))
    return lax.ppermute(value, axis, [(source, source + steps) for source in range(initial, last)])


def exchange(blocks, axis):
    return lax.all_to_all(blocks, axis, 0, 0)


def along_head(value, steps):
    count = lax.axis_size("head")
    return lax.ppermute(value, "head", [(i, (i + steps) % count) for i in range(count)])


def gather_near(first, second):
    left_first, right_second = along_head(first, 1), along_head(second, -1)
    left_second, right_first = along_head(second, 1), along_head(first, -1)
    return left_first, left_second, right_first, right_second


def gather_far(left_first, right_second):
    return along_head(left_first, 1), along_head(right_second, -1)


def gather_pieces(first, second):
    left_first, left_second, right_first, right_second = gather_near(first, second)
    far = gather_far(left_first, right_second)
    return first, second, right_first, right_second, *far, left_first, left_second


def reduce_far(pieces):
    _, _, right_first, right_second, far_first, far_second, left_first, left_second = pieces
    came_first, came_second = along_head(far_first, 1), along_head(far_second, -1)
    from_left, from_right = along_head(right_second, 1), along_head(left_first, -1)
    to_right = (right_first.astype(f32) + came_first.astype(f32)).astype(bf16)
    to_left = (left_second.astype(f32) + came_second.astype(f32)).astype(bf16)
    return to_right, to_left, from_left, from_right


def reduce_near(pieces, to_right, to_left, from_left, from_right):
    far_left, far_right = along_head(to_right, 1), along_head(to_left, -1)
    return (
        pieces[0].astype(f32) + from_right.astype(f32) + far_left.astype(f32),
        pieces[1].astype(f32) + from_left.astype(f32) + far_right.astype(f32),
    )


def reduce_pieces(pieces):
    return reduce_near(pieces, *reduce_far(pieces))


SIDE = 4
Y_STRIDE, Z_STRIDE = 2, 2 * SIDE


def along_chips(value, stride, steps):
    pairs = []
    for i in range(lax.axis_size("seq")):
        at = i // stride % SIDE
        pairs.append((i, i + ((at + steps) % SIDE - at) * stride))
    return lax.ppermute(value, "seq", pairs)


def from_below(value, stride):
    return [value] + [along_chips(value, stride, steps) for steps in range(1, SIDE)]


def swap_cores(value):
    return lax.ppermute(value, "seq", [(i, i ^ 1) for i in range(lax.axis_size("seq"))])


def sum_over_blocks(value):
    value = value + swap_cores(value)
    for stride in (Y_STRIDE, Z_STRIDE):
        own, one, two, three = from_below(value, stride)
        value = own + one + two + three
    return value


def join_cores(ours, theirs):
    came = swap_cores(theirs)
    return (ours.astype(f32) + came.astype(f32)).astype(bf16)


def exchange_chips(parts):
    count = lax.axis_size("seq")
    groups = [list(range(first, count, 2)) for first in range(2)]
    return lax.all_to_all(parts, "seq", 0, 0, axis_index_groups=groups)


def together(*values):
    return lax.optimization_barrier(values)


def shards(
    tokens,
    lengths,
    norm_gain,
    query_key_value_weight,
    strength_projection,
    conv_weight,
    head_gain,
    output_projection,
    mlp_gain,
    gate_up_weight,
    down_projection,
    out_grad,
):
    seqs, length, width = tokens.shape
    model = norm_gain.shape[0]
    heads = width // HEAD_DIM
    chains = seqs * heads
    rows = seqs * length
    devices = lax.axis_size("head")
    blocks = lax.axis_size("seq")
    hidden = down_projection.shape[0]
    col_start = lax.axis_index("head") * width
    positions = lax.axis_index("seq") * length + jnp.arange(length, dtype=jnp.int32)
    mask = (positions[None, :] < lengths[:, None]).astype(f32)[:, :, None]
    index = lax.axis_index("seq")
    core = lax.rem(index, 2)
    place = jnp.stack([index // Z_STRIDE, index // Y_STRIDE % SIDE, core])
    in_scalars = pl.BlockSpec(memory_space=pltpu.SMEM)
    at, shape = mixer_calls(seqs, length, heads)
    gain_row = head_gain[None, :]
    norm_row, mlp_row = norm_gain[None, :], mlp_gain[None, :]
    own = tokens.reshape(rows, width)
    tile = 128
    whole = lambda *size: spec(size, lambda i: (0,) * len(size))
    row_tile = lambda n: spec((tile, n), lambda i: (i, 0))
    part_tile = spec((devices, tile, width), lambda i: (0, i, 0))

    me = lax.axis_index("head").reshape(1)
    half = rows // 2
    first_half = spec((tile, width), lambda i, me: (jnp.minimum(i, half // tile - 1), 0))
    second_half = spec((tile, width), lambda i, me: (jnp.maximum(i - half // tile, 0), 0))
    pieces = [first_half, second_half] * devices
    on = lambda step, offset: lax.rem(step + offset, devices)
    fixed = lambda *size: spec(size, lambda i, me: (0,) * len(size))
    moving = lambda n: spec((tile, n), lambda i, me: (i, 0))

    def on_pieces(microseconds, kernel, grid, in_specs, out_specs, out_shape):
        return pl.pallas_call(
            kernel,
            grid_spec=pltpu.PrefetchScalarGridSpec(
                num_scalar_prefetch=1, grid=(grid,), in_specs=in_specs, out_specs=out_specs
            ),
            out_shape=out_shape,
            compiler_params=kernel_params(),
            cost_estimate=cost(microseconds),
        )

    half_shape = jax.ShapeDtypeStruct((half, width), bf16)
    own_halves = (tokens[0], tokens[1])
    full = gather_pieces(*own_halves)
    full, grad_own = together(full, out_grad.reshape(rows, width))
    grad_rows = lax.all_gather(grad_own, "head", axis=1, tiled=True)
    normed_in, in_scale, strength = on_pieces(
        2.6,
        in_norm_kernel,
        rows // tile,
        [*pieces, fixed(1, model), fixed(heads, model), moving(1)],
        [moving(model), moving(1), moving(heads)],
        [
            jax.ShapeDtypeStruct((rows, model), bf16),
            jax.ShapeDtypeStruct((rows, 1), f32),
            jax.ShapeDtypeStruct((rows, heads), f32),
        ],
    )(me, *in_hbm(*full), norm_row, strength_projection.T, mask.reshape(rows, 1))
    strength = strength.reshape(seqs, length, heads)
    projected = jnp.einsum(
        "if,tfw->tiw", normed_in, query_key_value_weight, preferred_element_type=f32
    ).astype(bf16).reshape(3, seqs, length, width)
    halo = from_behind(projected[:, :, length - HALO :, :], "seq", 1)

    send, q, k, w, u, gram, score, inv = pl.pallas_call(
        partial(span_kernel, heads),
        grid=(seqs,),
        in_specs=[at["proj"], at["halo"], at["conv"], at["strength"]],
        out_specs=[
            spec((heads, 2 * HEAD_DIM, HEAD_DIM), lambda s: (s, 0, 0)),
            at["tokens"], at["tokens"], at["tokens"], at["tokens"],
            at["three"], at["three"], at["two"],
        ],
        out_shape=[
            jax.ShapeDtypeStruct((chains, 2 * HEAD_DIM, HEAD_DIM), bf16),
            *[shape["tokens"](bf16)] * 4,
            shape["three"], shape["three"], shape["two"],
        ],
        scratch_shapes=[pltpu.VMEM((heads * 3, HALO + length, HEAD_DIM), f32)],
        compiler_params=kernel_params(),
        cost_estimate=cost(11.5),
    )(projected, halo, conv_weight, strength)

    def by_sequence(value):
        value = value.reshape((seqs, heads) + value.shape[1:])
        return [lax.dynamic_index_in_dim(value, n, 0, False) for n in (core, 1 - core)]

    def scan_step(kernel, shapes, scratch, *values):
        return pl.pallas_call(
            kernel,
            in_specs=[in_scalars] + [pl.BlockSpec(memory_space=pltpu.VMEM)] * len(values),
            out_specs=[pl.BlockSpec(memory_space=pltpu.VMEM)] * len(shapes),
            out_shape=[jax.ShapeDtypeStruct(shape, bf16) for shape in shapes],
            scratch_shapes=[pltpu.VMEM(shape, bf16) for shape in scratch],
            compiler_params=kernel_params(),
            cost_estimate=cost(2.0),
        )(place, *values)

    block_shape, map_shape = (heads, 2 * HEAD_DIM, HEAD_DIM), (heads, HEAD_DIM, HEAD_DIM)
    maps_shape = (SIDE,) + map_shape
    send_own, send_other = by_sequence(send)
    cores = (send_own, swap_cores(send_other))
    chip, core_maps = scan_step(chip_kernel, [block_shape, (2,) + map_shape], [], *cores)
    chips = from_below(chip, Y_STRIDE)
    hidden_grad = jnp.einsum("xp,hp->xh", grad_rows, down_projection, preferred_element_type=f32)
    chips[1], hidden_grad = together(chips[1], hidden_grad)
    plane, chip_maps = scan_step(
        plane_kernel, [block_shape, maps_shape], [(SIDE,) + block_shape], *chips
    )
    planes = from_below(plane, Z_STRIDE)
    state_ours, state_theirs, plane_maps = scan_step(
        enter_kernel, [map_shape, map_shape, maps_shape], [], *planes, *chips, *cores
    )
    state = (state_ours, swap_cores(state_theirs))

    head_out, x, mixer = pl.pallas_call(
        partial(mixer_kernel, heads),
        grid=(seqs,),
        in_specs=[
            in_scalars, at["fixed"], at["fixed"], at["tokens"], at["tokens"], at["tokens"],
            at["three"], at["gain"], at["mask"],
        ],
        out_specs=[at["rows"], at["tokens"], at["tokens"]],
        out_shape=[
            jax.ShapeDtypeStruct((seqs, length, width), bf16),
            shape["tokens"](bf16),
            shape["tokens"](f32),
        ],
        compiler_params=kernel_params(),
        cost_estimate=cost(2.3),
    )(place, *state, *in_hbm(q, w, u, score), gain_row, mask)
    head_out = head_out.reshape(rows, width)

    def bound_for(order):
        return lambda i, me: lax.rem(me[0] + sum((i == n) * at for n, at in enumerate(order)), devices)

    order = (2, 1, 3, 0)
    to = bound_for(order)
    came = on_pieces(
        2.2,
        branch_part_kernel,
        devices,
        [fixed(rows, width), spec((width, width), lambda i, me: (0, to(i, me)))],
        [fixed(half, width)] * 8,
        [half_shape] * 8,
    )(me, head_out, output_projection)
    branch = [came[2 * order.index(i // 2) + i % 2] for i in range(8)]
    middle_own = [
        mine.astype(f32) + other for mine, other in zip(own_halves, reduce_pieces(branch))
    ]
    middle = gather_pieces(*[value.astype(bf16) for value in middle_own])
    normed_mid, mid_scale = on_pieces(
        1.5,
        mid_norm_kernel,
        rows // tile,
        [*pieces, fixed(1, model)],
        [moving(model), moving(1)],
        [jax.ShapeDtypeStruct((rows, model), bf16), jax.ShapeDtypeStruct((rows, 1), f32)],
    )(me, *middle, mlp_row)

    gated = jnp.einsum("ux,gxt->gut", normed_mid, gate_up_weight, preferred_element_type=f32)
    gated_grad, features = pl.pallas_call(
        gate_kernel,
        grid=(rows // tile,),
        in_specs=[spec((2, tile, hidden), lambda i: (0, i, 0)), row_tile(hidden)],
        out_specs=[spec((2, tile, hidden), lambda i: (0, i, 0)), row_tile(hidden)],
        out_shape=[
            jax.ShapeDtypeStruct((2, rows, hidden), bf16),
            jax.ShapeDtypeStruct((rows, hidden), bf16),
        ],
        compiler_params=kernel_params(),
        cost_estimate=cost(2.4),
    )(gated, hidden_grad)
    mid_parts = []
    for order in ((2,), (1, 3, 0)):
        to = bound_for(order)
        mid_parts += on_pieces(
            2.0 * len(order),
            mid_part_kernel,
            len(order),
            [
                fixed(2, rows, hidden),
                spec((2, width, hidden), lambda i, me, to=to: (0, to(i, me), 0)),
            ],
            [fixed(half, width)] * (2 * len(order)),
            [half_shape] * (2 * len(order)),
        )(me, gated_grad, gate_up_weight)
    order = (2, 1, 3, 0)
    mid_parts = [mid_parts[2 * order.index(i // 2) + i % 2] for i in range(8)]

    split_rows = 4

    def feed_weights(column, left, right, right_spec, into):
        extra = () if into is None else (into,)
        return pl.pallas_call(
            feed_weights_kernel,
            grid=(split_rows,),
            in_specs=[spec((rows, model // split_rows), lambda i: (0, i)), right_spec]
            + [pl.BlockSpec(memory_space=pl.ANY)] * len(extra),
            out_specs=spec((model // split_rows, hidden), lambda i: (i, column)),
            out_shape=pltpu.HBM((model, 3 * hidden), bf16),
            input_output_aliases={2: 0} if extra else {},
            compiler_params=kernel_params(),
        cost_estimate=cost(5.6),
        )(left, right, *extra)

    to_right, to_left, from_left, from_right = reduce_far(mid_parts)
    to_right, to_left, features = together(to_right, to_left, features)
    feed_part = feed_weights(2, grad_rows, features, whole(rows, hidden), None)
    far_left, far_right = along_head(to_right, 1), along_head(to_left, -1)
    far_left, far_right, feed_part = together(far_left, far_right, feed_part)
    mid_grad_own = (
        mid_parts[0].astype(f32) + from_right.astype(f32) + far_left.astype(f32),
        mid_parts[1].astype(f32) + from_left.astype(f32) + far_right.astype(f32),
    )
    first, second = [value.astype(bf16) for value in mid_grad_own]
    first, second, gated_grad = together(first, second, gated_grad)
    left_first, left_second, right_first, right_second = gather_near(first, second)
    right_spec = lambda j: spec((None, rows, hidden), lambda i: (j, 0, 0))
    feed_part = feed_weights(0, normed_mid, gated_grad, right_spec(0), feed_part)
    left_first, right_second, feed_part, features, gated_grad = together(
        left_first, right_second, feed_part, features, gated_grad
    )
    far = gather_far(left_first, right_second)
    feed_part = feed_weights(1, normed_mid, gated_grad, right_spec(1), feed_part)
    feed = jnp.dot(features, down_projection, preferred_element_type=f32).astype(bf16)
    *far, feed_part, feed = together(*far, feed_part, feed)
    mid_grad = (first, second, right_first, right_second, *far, left_first, left_second)
    feed_sum = lax.psum_scatter(feed_part, "seq", scatter_dimension=0, tiled=True)
    feed, feed_sum = together(feed, feed_sum)
    feed_sum = feed_sum.astype(f32)
    feed_own = lax.psum_scatter(feed, "head", scatter_dimension=1, tiled=True).astype(f32)
    output = jnp.concatenate(middle_own) + feed_own

    branch_grad, mid_dot = on_pieces(
        4.7,
        mid_back_kernel,
        rows // tile,
        [*pieces, *pieces, moving(model), fixed(1, model), moving(1)],
        [moving(model), moving(1)],
        [jax.ShapeDtypeStruct((rows, model), bf16), jax.ShapeDtypeStruct((rows, 1), f32)],
    )(me, *in_hbm(*middle, *mid_grad, grad_rows), mlp_row, mid_scale)
    own_gain = lax.dynamic_slice_in_dim(mlp_gain, col_start, width, 0)
    middle_grad_own, mlp_gain_part = [], 0.0
    for i in range(2):
        scale, inner = mid_scale[i * half : (i + 1) * half], mid_dot[i * half : (i + 1) * half]
        middle_grad_own.append(
            out_grad[i].astype(f32) + scale * own_gain * mid_grad_own[i]
            - scale * scale * scale * middle_own[i] * inner
        )
        mlp_gain_part += jnp.sum(mid_grad_own[i] * middle_own[i] * scale, axis=0)
    head_grad = jnp.einsum(
        "pj,wj->pw", branch_grad, output_projection, preferred_element_type=f32
    ).astype(bf16).reshape(seqs, length, width)

    send_back, dmix, dx, dgain = pl.pallas_call(
        partial(head_back_kernel, heads),
        grid=(seqs,),
        in_specs=[
            at["rows"], at["tokens"], at["gain"], at["mask"], at["tokens"], at["tokens"],
            at["three"],
        ],
        out_specs=[
            at["state"], at["tokens"], at["tokens"],
            spec((heads, 1, HEAD_DIM), lambda s: (s, 0, 0)),
        ],
        out_shape=[
            jax.ShapeDtypeStruct((chains, HEAD_DIM, HEAD_DIM), bf16),
            shape["tokens"](bf16),
            shape["tokens"](f32),
            jax.ShapeDtypeStruct((chains, 1, HEAD_DIM), f32),
        ],
        compiler_params=kernel_params(),
        cost_estimate=cost(3.3),
    )(head_grad, *in_hbm(mixer), gain_row, mask, *in_hbm(q, w, score))

    steps, rows_own = 4, model // blocks
    chip_count = blocks // 2
    by_core = lambda n: spec((chip_count // steps, rows_own, n), lambda i: (i, 0, 0))
    core_shape = lambda n: jax.ShapeDtypeStruct((chip_count, rows_own, n), bf16)
    model_tile = spec((rows, model // steps), lambda i: (0, i))

    back_own, back_other = by_sequence(send_back)
    out_ours, out_theirs = pl.pallas_call(
        out_weights_kernel,
        grid=(steps,),
        in_specs=[in_scalars, model_tile, whole(rows, width)],
        out_specs=[by_core(width)] * 2,
        out_shape=[core_shape(width)] * 2,
        compiler_params=kernel_params(),
        cost_estimate=cost(2.3),
    )(core.reshape(1), branch_grad, head_out)
    chip_add, last_adds = scan_step(
        back_chip_kernel, [map_shape] * 2, [], core_maps, back_own, swap_cores(back_other)
    )
    chip_adds = from_below(chip_add, Y_STRIDE)
    chip_adds[1], out_ours, out_theirs = together(chip_adds[1], out_ours, out_theirs)
    plane_add, chip_adds = scan_step(
        back_plane_kernel, [map_shape, maps_shape], [], chip_maps, *chip_adds
    )
    plane_adds = from_below(plane_add, Z_STRIDE)
    out_joined = join_cores(out_ours, out_theirs)
    plane_adds[1], out_joined = together(plane_adds[1], out_joined)
    dstate_ours, dstate_theirs = scan_step(
        back_enter_kernel, [map_shape] * 2, [maps_shape],
        core_maps, chip_maps, plane_maps, last_adds, chip_adds, *plane_adds,
    )
    dstate = (dstate_ours, swap_cores(dstate_theirs))
    dstate_ours, out_joined = together(dstate_ours, out_joined)
    dstate = (dstate_ours, dstate[1])
    out_spread = exchange_chips(out_joined)

    dproj, tail, ahead, dlogit, dconv = pl.pallas_call(
        partial(span_back_kernel, heads),
        grid=(seqs,),
        in_specs=[
            in_scalars, at["fixed"], at["fixed"], at["fixed"], at["fixed"],
            at["proj"], at["halo"], at["conv"], at["strength"],
            at["tokens"], at["tokens"], at["tokens"], at["three"], at["two"],
        ],
        out_specs=[
            at["proj"], at["halo"], at["halo"], at["strength"],
            spec((3, 1, CONV, width), lambda s: (0, s, 0, 0)),
        ],
        out_shape=[
            jax.ShapeDtypeStruct((3, seqs, length, width), bf16),
            jax.ShapeDtypeStruct((3, seqs, HALO, width), f32),
            jax.ShapeDtypeStruct((3, seqs, HALO, width), bf16),
            jax.ShapeDtypeStruct((seqs, length, heads), f32),
            jax.ShapeDtypeStruct((3, seqs, CONV, width), f32),
        ],
        scratch_shapes=[
            pltpu.VMEM((heads * 3, HALO + length, HEAD_DIM), f32),
            pltpu.VMEM((heads * 3, 2 * HALO + length, HEAD_DIM), f32),
        ],
        compiler_params=kernel_params(),
        cost_estimate=cost(10.5),
    )(
        place, *state, *dstate, projected, halo, conv_weight, strength,
        *in_hbm(x, dmix, dx, gram, inv),
    )

    sent_back = from_behind(ahead, "seq", -1).astype(f32)
    proj_grad = lax.dynamic_update_slice_in_dim(
        dproj, (tail + sent_back).astype(bf16), length - HALO, 2
    ).reshape(3, rows, width)
    logit_grad = dlogit.astype(bf16).reshape(rows, heads)

    mix_ours, mix_theirs, strength_part, norm_gain_part = pl.pallas_call(
        mix_weights_kernel,
        grid=(steps,),
        in_specs=[in_scalars, model_tile, whole(3, rows, width), whole(rows, heads),
            spec((3, model // steps, width), lambda i: (0, i, 0)),
            spec((heads, model // steps), lambda i: (0, i)),
        ],
        out_specs=[by_core(3 * width)] * 2
        + [spec((n, model // steps), lambda i: (0, i)) for n in (heads, 8)],
        out_shape=[pltpu.HBM((chip_count, rows_own, 3 * width), bf16)] * 2
        + [jax.ShapeDtypeStruct((n, model), f32) for n in (heads, 8)],
        compiler_params=kernel_params(),
        cost_estimate=cost(9.0),
    )(core.reshape(1), normed_in, proj_grad, logit_grad, *in_hbm(query_key_value_weight), strength_projection.T)
    mix_ours, mix_theirs, out_spread = together(mix_ours, mix_theirs, out_spread)
    out_sum = jnp.sum(out_spread.astype(f32), axis=0)
    mix_joined = join_cores(mix_ours, mix_theirs)

    in_parts, inners = [], []
    for order in ((2,), (1, 3, 0)):
        to = bound_for(order)
        *parts, inner = on_pieces(
            2.0 * len(order),
            in_part_kernel,
            len(order),
            [
                fixed(3, rows, width), fixed(rows, heads),
                spec((3, width, width), lambda i, me, to=to: (0, to(i, me), 0)),
                spec((heads, width), lambda i, me, to=to: (0, to(i, me))),
                spec((rows, width), lambda i, me, to=to: (0, to(i, me))),
            ],
            [fixed(half, width)] * (2 * len(order)) + [fixed(8, rows)],
            [half_shape] * (2 * len(order)) + [jax.ShapeDtypeStruct((8, rows), f32)],
        )(me, proj_grad, logit_grad, *in_hbm(query_key_value_weight), strength_projection.T, *in_hbm(normed_in))
        in_parts += parts
        inners.append(inner[0:1])
    order = (2, 1, 3, 0)
    in_parts = [in_parts[2 * order.index(i // 2) + i % 2] for i in range(8)]
    in_parts[2], in_parts[7], mix_joined, norm_gain_part, strength_part, inners = together(
        in_parts[2], in_parts[7], mix_joined, norm_gain_part, strength_part, inners
    )
    mix_spread = exchange_chips(mix_joined)
    in_grad = reduce_pieces(in_parts)
    def over_head(value):
        value = value + along_head(value, 2)
        return value + along_head(value, 1)

    in_dot = over_head(inners[0] + inners[1])[0][:, None] / model
    in_gain = lax.dynamic_slice_in_dim(norm_gain, col_start, width, 0)
    tokens_grad = []
    for i in range(2):
        scale, inner = in_scale[i * half : (i + 1) * half], in_dot[i * half : (i + 1) * half]
        mine = own_halves[i].astype(f32)
        tokens_grad.append(
            scale * in_gain * in_grad[i] - scale * scale * mine * inner + middle_grad_own[i]
        )
    tokens_grad = jnp.stack(tokens_grad).astype(bf16)

    each, gain_each = width // blocks, HEAD_DIM // blocks
    by_head = over_head(
        jnp.concatenate(
            [
                norm_gain_part[0].reshape(devices, width),
                jnp.pad(jnp.sum(dgain, axis=0), ((0, 0), (0, width - HEAD_DIM))),
            ]
        )
    )
    small = sum_over_blocks(
        jnp.concatenate(
            [
                jnp.sum(dconv, axis=1).reshape(3 * CONV, width),
                mlp_gain_part[None],
                strength_part.reshape(heads * model // width, width),
                by_head,
            ]
        )
    )
    by_block = lax.dynamic_slice_in_dim(small[: 3 * CONV + 1], index * each, each, 1)
    head_gain_own = lax.dynamic_slice_in_dim(small[-1], index * gain_each, gain_each, 0)
    norm_gain_own = lax.dynamic_slice(
        small[-1 - devices : -1], (lax.axis_index("head"), index * each), (1, each)
    )[0] / lax.dynamic_slice_in_dim(in_gain, index * each, each, 0)
    strength_own = lax.dynamic_slice_in_dim(
        small[3 * CONV + 1 : -1 - devices].reshape(heads, model), index * rows_own, rows_own, 1
    )
    output = output.astype(bf16).reshape(seqs, length, width)
    gate_up_grad = jnp.moveaxis(feed_sum[:, : 2 * hidden].reshape(rows_own, 2, hidden), 1, 0)
    out_weight_grad, down_grad = out_sum.T, feed_sum[:, 2 * hidden :].T
    mix_spread, output, tokens_grad, gate_up_grad, out_weight_grad, down_grad = together(
        mix_spread, output, tokens_grad, gate_up_grad, out_weight_grad, down_grad
    )
    mix_sum = jnp.sum(mix_spread.astype(f32), axis=0)
    qkv_grad = jnp.moveaxis(mix_sum.reshape(rows_own, 3, width), 1, 0)
    return (
        output,
        tokens_grad,
        norm_gain_own,
        qkv_grad,
        strength_own.T,
        by_block[: 3 * CONV].reshape(3, CONV, each),
        head_gain_own,
        out_weight_grad,
        by_block[3 * CONV],
        gate_up_grad,
        down_grad,
    )


def solution(mesh):
    return jax.shard_map(
        shards,
        mesh=mesh,
        in_specs=(
            P(None, "seq", "head"),
            P(),
            P(),
            P(None, None, "head"),
            P(None, "head"),
            P(None, None, "head"),
            P(),
            P("head", None),
            P(),
            P(None, None, "head"),
            P("head", None),
            P(None, "seq", "head"),
        ),
        out_specs=(
            P(None, "seq", "head"),
            P(None, "seq", "head"),
            P(("head", "seq")),
            P(None, "seq", "head"),
            P("seq", "head"),
            P(None, None, ("head", "seq")),
            P("seq"),
            P("head", "seq"),
            P(("head", "seq")),
            P(None, "seq", "head"),
            P("head", "seq"),
        ),
        check_vma=False,
    )
```

```python
from functools import partial

import jax
import jax.numpy as jnp
from jax import lax
from jax.experimental import pallas as pl
from jax.experimental.pallas import tpu as pltpu
from jax.sharding import PartitionSpec as P

HEAD_DIM = 128
CONV = 4
HALF = 128
HALO = 8
EPS = 1e-06

f32 = jnp.float32
bf16 = jnp.bfloat16


def dot(a, b, dims=((1,), (0,))):
    return lax.dot_general(
        a.astype(bf16), b.astype(bf16), (dims, ((), ())), preferred_element_type=f32
    )


NT = ((1,), (1,))
TN = ((0,), (0,))


def split(a):
    high = a.astype(bf16)
    return high, (a - high.astype(f32)).astype(bf16)


def dot3(a, b):
    a_high, a_low = split(a)
    b_high, b_low = split(b)
    return dot(a_high, b_high) + (dot(a_high, b_low) + dot(a_low, b_high))


def unit_lower_inverses(stricts):
    size = stricts[0].shape[0]
    row = lax.broadcasted_iota(jnp.int32, (size, size), 0)
    col = lax.broadcasted_iota(jnp.int32, (size, size), 1)
    eye = jnp.where(row == col, 1.0, 0.0)
    below = (row // 2 == col // 2) & (row != col)
    inverses = [eye - jnp.where(below, strict, 0.0) for strict in stricts]
    width = 2
    while width < size:
        below = (row // (2 * width) == col // (2 * width)) & (row // width != col // width)
        parts = [
            dot(jnp.where(below, strict, 0.0), inverse)
            for strict, inverse in zip(stricts, inverses)
        ]
        inverses = [inverse - dot(inverse, part) for inverse, part in zip(inverses, parts)]
        width *= 2
    errors = [
        eye - inverse - dot3(strict, inverse) for strict, inverse in zip(stricts, inverses)
    ]
    return [inverse + dot(inverse, error) for inverse, error in zip(inverses, errors)]


def sigmoid(x):
    return 1.0 / (1.0 + jnp.exp(-x))


def masks():
    row = lax.broadcasted_iota(jnp.int32, (HALF, HALF), 0)
    col = lax.broadcasted_iota(jnp.int32, (HALF, HALF), 1)
    return row > col, row >= col


def conv_rows(j, proj_ref, halo_ref, conv_ref, rows, lanes):
    length = proj_ref.shape[2]
    rows[0:HALO, :] = halo_ref[j, 0, :, lanes].astype(f32)
    rows[HALO : HALO + length, :] = proj_ref[j, 0, :, lanes].astype(f32)
    mixed = None
    for i in range(CONV):
        start = HALO - (CONV - 1) + i
        term = conv_ref[j, i : i + 1, lanes] * rows[start : start + length, :]
        mixed = term if mixed is None else mixed + term
    return mixed


def column_of(values, at):
    lane = lax.broadcasted_iota(jnp.int32, values.shape, 1)
    return jnp.sum(jnp.where(lane == at, values, 0.0), axis=1, keepdims=True)


def span_kernel(
    heads, proj_ref, halo_ref, conv_ref, strength_ref,
    send_ref, q_ref, k_ref, w_ref, u_ref, gram_ref, score_ref, inv_ref, rows,
):
    lower, lower_diag = masks()
    a, b = slice(0, HALF), slice(HALF, 2 * HALF)
    rights, grams, stricts = [], [], []
    for h in range(heads):
        lanes = slice(h * HEAD_DIM, (h + 1) * HEAD_DIM)
        active = []
        for j in range(3):
            mixed = conv_rows(j, proj_ref, halo_ref, conv_ref, rows.at[h * 3 + j], lanes)
            active.append(mixed * sigmoid(mixed))
        q = active[0] * lax.rsqrt(jnp.sum(active[0] * active[0], axis=1, keepdims=True) + EPS)
        k = active[1] * lax.rsqrt(jnp.sum(active[1] * active[1], axis=1, keepdims=True) + EPS)
        v = active[2]
        q_ref[h] = q.astype(bf16)
        k_ref[h] = k.astype(bf16)
        beta = column_of(strength_ref[0], h)
        gram = dot(k, k, NT)
        score = dot(q, k, NT)
        gaa = jnp.where(lower, gram[a, a], 0.0)
        gbb = jnp.where(lower, gram[b, b], 0.0)
        gba = gram[b, a]
        gram_ref[h, 0] = gaa.astype(bf16)
        gram_ref[h, 1] = gba.astype(bf16)
        gram_ref[h, 2] = gbb.astype(bf16)
        score_ref[h, 0] = jnp.where(lower_diag, score[a, a], 0.0).astype(bf16)
        score_ref[h, 1] = score[b, a].astype(bf16)
        score_ref[h, 2] = jnp.where(lower_diag, score[b, b], 0.0).astype(bf16)
        stricts += [beta[a] * gaa, beta[b] * gbb]
        grams.append((beta[b] * gba).astype(bf16))
        rights.append(beta * jnp.concatenate([k, v], axis=1))
    inverses = unit_lower_inverses(stricts)
    for h in range(heads):
        taa, tbb = inverses[2 * h].astype(bf16), inverses[2 * h + 1].astype(bf16)
        inv_ref[h, 0] = taa
        inv_ref[h, 1] = tbb
        k = k_ref[h]
        top = dot(taa, rights[h][a])
        bottom = dot(tbb, rights[h][b] - dot(grams[h], top))
        w = jnp.concatenate([top[:, :HEAD_DIM], bottom[:, :HEAD_DIM]], axis=0)
        u = jnp.concatenate([top[:, HEAD_DIM:], bottom[:, HEAD_DIM:]], axis=0)
        w_ref[h] = w.astype(bf16)
        u_ref[h] = u.astype(bf16)
        step = -dot(w, k, TN)
        add = dot(u, k, TN)
        send_ref[h, 0:HEAD_DIM, :] = step.astype(bf16)
        send_ref[h, HEAD_DIM:, :] = add.astype(bf16)


def through(state, block):
    high, low = split(state)
    step = block[:HEAD_DIM]
    return state + dot(high, step) + dot(low, step)


def through_back(state, block):
    high, low = split(state)
    step = block[:HEAD_DIM]
    return state + dot(high, step, NT) + dot(low, step, NT)


def added(block):
    return block[HEAD_DIM:].astype(f32)


def chip_kernel(place_ref, own_ref, came_ref, out_ref, maps_ref):
    mine_first = place_ref[2] == 0
    for c in range(out_ref.shape[0]):
        own, came = own_ref[c].astype(f32), came_ref[c].astype(f32)
        first = jnp.where(mine_first, own, came)
        second = jnp.where(mine_first, came, own)
        maps_ref[0, c] = first[:HEAD_DIM].astype(bf16)
        step = second[:HEAD_DIM].astype(bf16)
        maps_ref[1, c] = step
        out_ref[c] = (first + second + dot(first, step)).astype(bf16)


def plane_kernel(place_ref, own_ref, one_ref, two_ref, three_ref, out_ref, maps_ref, stack):
    count = stack.shape[0]
    for at, ref in enumerate((own_ref, one_ref, two_ref, three_ref)):
        stack[lax.rem(place_ref[1] - at + count, count)] = ref[...]
    maps_ref[...] = stack[:, :, :HEAD_DIM]
    for c in range(out_ref.shape[0]):
        total = None
        for y in range(count):
            block = stack[y, c]
            if total is None:
                total = block.astype(f32)
            else:
                total = through(total, block) + block.astype(f32)
        out_ref[c] = total.astype(bf16)


def enter_kernel(place_ref, *refs):
    planes, chips, (own_ref, came_ref) = refs[:4], refs[4:8], refs[8:10]
    ours_ref, theirs_ref, maps_ref = refs[10:]
    chains, count = ours_ref.shape[0], len(planes)
    for at in range(count):
        maps_ref[lax.rem(place_ref[0] - at + count, count)] = planes[at][:, :HEAD_DIM]
    states = [jnp.zeros((HEAD_DIM, HEAD_DIM), f32)] * chains
    for level, blocks in ((0, planes), (1, chips)):
        for back in range(count - 1, 0, -1):
            reached = back <= place_ref[level]
            for c in range(chains):
                block = blocks[back][c]
                after = through(states[c], block) + added(block)
                states[c] = jnp.where(reached, after, states[c])
    mine_first = place_ref[2] == 0
    for c in range(chains):
        first = jnp.where(mine_first, own_ref[c].astype(f32), came_ref[c].astype(f32))
        after = through(states[c], first.astype(bf16)) + added(first)
        ours_ref[c] = jnp.where(mine_first, states[c], after).astype(bf16)
        theirs_ref[c] = jnp.where(mine_first, after, states[c]).astype(bf16)


def back_chip_kernel(place_ref, maps_ref, own_ref, came_ref, out_ref, adds_ref):
    mine_first = place_ref[2] == 0
    for c in range(out_ref.shape[0]):
        own, came = own_ref[c].astype(f32), came_ref[c].astype(f32)
        last = jnp.where(mine_first, came, own)
        add = jnp.where(mine_first, own, came)
        adds_ref[c] = last.astype(bf16)
        out_ref[c] = (through_back(last, maps_ref[0, c]) + add).astype(bf16)


def back_plane_kernel(place_ref, maps_ref, *refs):
    adds, (out_ref, adds_ref) = refs[:4], refs[4:]
    count = len(adds)
    for at in range(count):
        adds_ref[lax.rem(place_ref[1] - at + count, count)] = adds[at][...]
    for c in range(out_ref.shape[0]):
        total = None
        for y in range(count - 1, -1, -1):
            add = adds_ref[y, c].astype(f32)
            total = add if total is None else through_back(total, maps_ref[y, c]) + add
        out_ref[c] = total.astype(bf16)


def back_enter_kernel(place_ref, core_maps, chip_maps, plane_maps, last_adds, chip_adds, *refs):
    plane_adds, (ours_ref, theirs_ref, stack) = refs[:4], refs[4:]
    chains, count = ours_ref.shape[0], len(plane_adds)
    for at in range(count):
        stack[lax.rem(place_ref[0] - at + count, count)] = plane_adds[at][...]
    states = [jnp.zeros((HEAD_DIM, HEAD_DIM), f32)] * chains
    for level, maps, adds in ((0, plane_maps, stack), (1, chip_maps, chip_adds)):
        for at in range(count - 1, 0, -1):
            reached = at > place_ref[level]
            for c in range(chains):
                after = through_back(states[c], maps[at, c]) + adds[at, c].astype(f32)
                states[c] = jnp.where(reached, after, states[c])
    mine_first = place_ref[2] == 0
    for c in range(chains):
        after = through_back(states[c], core_maps[1, c]) + last_adds[c].astype(f32)
        ours_ref[c] = jnp.where(mine_first, after, states[c]).astype(bf16)
        theirs_ref[c] = jnp.where(mine_first, states[c], after).astype(bf16)


def state_of(place_ref, ours_ref, came_ref, h):
    mine = pl.program_id(0) == place_ref[2]
    return jnp.where(mine, ours_ref[h].astype(f32), came_ref[h].astype(f32)).astype(bf16)


def mixer_kernel(
    heads, place_ref, ours_ref, came_ref, q_ref, w_ref, u_ref, score_ref, gain_ref, mask_ref,
    out_ref, x_ref, mix_ref,
):
    a, b = slice(0, HALF), slice(HALF, 2 * HALF)
    mask = mask_ref[0]
    for h in range(heads):
        lanes = slice(h * HEAD_DIM, (h + 1) * HEAD_DIM)
        state = state_of(place_ref, ours_ref, came_ref, h)
        x = u_ref[h].astype(f32) - dot(w_ref[h], state, NT)
        x_ref[h] = x.astype(bf16)
        base = dot(q_ref[h], state, NT)
        top = dot(score_ref[h, 0], x[a])
        bottom = dot(score_ref[h, 1], x[a]) + dot(score_ref[h, 2], x[b])
        mixer = base + jnp.concatenate([top, bottom], axis=0)
        mix_ref[h] = mixer
        inv = lax.rsqrt(jnp.mean(mixer * mixer, axis=1, keepdims=True) + EPS)
        out_ref[0, :, lanes] = (mixer * inv * gain_ref[...] * mask).astype(bf16)


def head_back_kernel(
    heads, grad_ref, mix_ref, gain_ref, mask_ref, q_ref, w_ref, score_ref,
    send_ref, dmix_ref, dx_ref, dgain_ref,
):
    a, b = slice(0, HALF), slice(HALF, 2 * HALF)
    mask = mask_ref[0]
    gain = gain_ref[...]
    for h in range(heads):
        lanes = slice(h * HEAD_DIM, (h + 1) * HEAD_DIM)
        grad = grad_ref[0, :, lanes].astype(f32) * mask
        mixer = mix_ref[h]
        inv = lax.rsqrt(jnp.mean(mixer * mixer, axis=1, keepdims=True) + EPS)
        scaled = mixer * inv
        dgain_ref[h] = jnp.sum(grad * scaled, axis=0, keepdims=True)
        inner = jnp.mean(gain * grad * scaled, axis=1, keepdims=True)
        dmix = inv * (gain * grad - scaled * inner)
        dmix_ref[h] = dmix.astype(bf16)
        top = dot(score_ref[h, 0], dmix[a], TN) + dot(score_ref[h, 1], dmix[b], TN)
        bottom = dot(score_ref[h, 2], dmix[b], TN)
        dx = jnp.concatenate([top, bottom], axis=0)
        dx_ref[h] = dx
        send_ref[h] = (dot(dmix, q_ref[h], TN) - dot(dx, w_ref[h], TN)).astype(bf16)


def span_back_kernel(
    heads, place_ref, ours_ref, came_ref, dours_ref, dcame_ref,
    proj_ref, halo_ref, conv_ref, strength_ref,
    x_ref, dmix_ref, dx_ref, gram_ref, inv_ref,
    dproj_ref, tail_ref, ahead_ref, dlogit_ref, dconv_ref, rows, grads,
):
    lower, lower_diag = masks()
    a, b = slice(0, HALF), slice(HALF, 2 * HALF)
    length = proj_ref.shape[2]
    lane = lax.broadcasted_iota(jnp.int32, strength_ref.shape[1:], 1)
    dlogit = jnp.zeros(strength_ref.shape[1:], f32)
    for h in range(heads):
        lanes = slice(h * HEAD_DIM, (h + 1) * HEAD_DIM)
        mixed, sig, active = [], [], []
        for j in range(3):
            mixed.append(conv_rows(j, proj_ref, halo_ref, conv_ref, rows.at[h * 3 + j], lanes))
            sig.append(sigmoid(mixed[j]))
            active.append(mixed[j] * sig[j])
        q_inv = lax.rsqrt(jnp.sum(active[0] * active[0], axis=1, keepdims=True) + EPS)
        k_inv = lax.rsqrt(jnp.sum(active[1] * active[1], axis=1, keepdims=True) + EPS)
        q, k, v = active[0] * q_inv, active[1] * k_inv, active[2]
        kb = k.astype(bf16)
        beta = column_of(strength_ref[0], h)
        state = state_of(place_ref, ours_ref, came_ref, h)
        dstate = state_of(place_ref, dours_ref, dcame_ref, h)
        x, dmix = x_ref[h], dmix_ref[h]
        gaa, gba, gbb = gram_ref[h, 0], gram_ref[h, 1], gram_ref[h, 2]
        dx = dx_ref[h] + dot(kb, dstate, NT)
        y_b = dot(inv_ref[h, 1], dx[b], TN)
        y_a = dot(inv_ref[h, 0], dx[a] - dot(gba, beta[b] * y_b, TN), TN)
        y = jnp.concatenate([y_a, y_b], axis=0)
        inner = jnp.concatenate([dot(gaa, x[a]), dot(gba, x[a]) + dot(gbb, x[b])], axis=0)
        residual = v - dot(kb, state, NT) - inner
        dbeta = jnp.sum(y * residual, axis=1, keepdims=True)
        dlogit = jnp.where(lane == h, dbeta * beta * (1.0 - beta), dlogit)
        dv = beta * y
        dgram = -dot(dv, x, NT)
        dscore = dot(dmix, x, NT)
        dg_aa = jnp.where(lower, dgram[a, a], 0.0).astype(bf16)
        dg_bb = jnp.where(lower, dgram[b, b], 0.0).astype(bf16)
        dg_ba = dgram[b, a].astype(bf16)
        ds_aa = jnp.where(lower_diag, dscore[a, a], 0.0).astype(bf16)
        ds_bb = jnp.where(lower_diag, dscore[b, b], 0.0).astype(bf16)
        ds_ba = dscore[b, a].astype(bf16)
        qb = q.astype(bf16)
        dq = dot(dmix, state) + jnp.concatenate(
            [dot(ds_aa, kb[a]), dot(ds_ba, kb[a]) + dot(ds_bb, kb[b])], axis=0
        )
        dk = dot(x, dstate) - dot(dv, state)
        dk_a = (
            dot(ds_aa, qb[a], TN) + dot(ds_ba, qb[b], TN)
            + dot(dg_aa, kb[a]) + dot(dg_aa, kb[a], TN) + dot(dg_ba, kb[b], TN)
        )
        dk_b = (
            dot(ds_bb, qb[b], TN) + dot(dg_ba, kb[a])
            + dot(dg_bb, kb[b]) + dot(dg_bb, kb[b], TN)
        )
        dk = dk + jnp.concatenate([dk_a, dk_b], axis=0)
        dact = [
            (dq - q * jnp.sum(q * dq, axis=1, keepdims=True)) * q_inv,
            (dk - k * jnp.sum(k * dk, axis=1, keepdims=True)) * k_inv,
            dv,
        ]
        for j in range(3):
            dmixed = dact[j] * sig[j] * (1.0 + mixed[j] * (1.0 - sig[j]))
            own = rows.at[h * 3 + j]
            pad = grads.at[h * 3 + j]
            pad[0:HALO, :] = jnp.zeros((HALO, HEAD_DIM), f32)
            pad[HALO : HALO + length, :] = dmixed
            pad[HALO + length :, :] = jnp.zeros((HALO, HEAD_DIM), f32)
            whole = None
            for i in range(CONV):
                start = HALO - (CONV - 1) + i
                dconv_ref[j, 0, i : i + 1, lanes] = jnp.sum(
                    dmixed * own[start : start + length, :], axis=0, keepdims=True
                )
                shift = CONV - 1 - i
                term = conv_ref[j, i : i + 1, lanes] * pad[shift : shift + HALO + length, :]
                whole = term if whole is None else whole + term
            ahead_ref[j, 0, :, lanes] = whole[0:HALO].astype(bf16)
            dproj_ref[j, 0, :, lanes] = whole[HALO:].astype(bf16)
            tail_ref[j, 0, :, lanes] = whole[length:]
    dlogit_ref[0] = dlogit


def columns_of(me_ref, offset, count, width):
    return pl.ds(pl.multiple_of(lax.rem(me_ref[0] + offset, count) * width, width), width)


def piece(refs, offset):
    first, second = refs[2 * offset], refs[2 * offset + 1]
    in_first = 2 * pl.program_id(0) < pl.num_programs(0)
    return jnp.where(in_first, first[...].astype(f32), second[...].astype(f32))


def norm_pieces(me_ref, refs, gain_ref, normed_ref, scale_ref):
    count = len(refs) // 2
    values = [piece(refs, i) for i in range(count)]
    width = values[0].shape[1]
    total = None
    for value in values:
        square = jnp.sum(value * value, axis=1, keepdims=True)
        total = square if total is None else total + square
    scale = lax.rsqrt(total / (count * width) + EPS)
    scale_ref[...] = scale
    for i in range(count):
        at = columns_of(me_ref, i, count, width)
        normed_ref[:, at] = (values[i] * scale * gain_ref[:, at]).astype(bf16)


def in_norm_kernel(me_ref, *args):
    *refs, gain_ref, weight_ref, mask_ref, normed_ref, scale_ref, strength_ref = args
    norm_pieces(me_ref, refs, gain_ref, normed_ref, scale_ref)
    strength_ref[...] = sigmoid(dot(normed_ref[...], weight_ref[...], NT)) * mask_ref[...]


def mid_norm_kernel(me_ref, *args):
    *refs, gain_ref, normed_ref, scale_ref = args
    norm_pieces(me_ref, refs, gain_ref, normed_ref, scale_ref)


def mid_back_kernel(me_ref, *args):
    *refs, rows_ref, gain_ref, scale_ref, branch_ref, dot_ref = args
    count = len(refs) // 4
    values = [piece(refs[: 2 * count], i) for i in range(count)]
    grads = [piece(refs[2 * count :], i) for i in range(count)]
    width = values[0].shape[1]
    total = None
    for i in range(count):
        at = columns_of(me_ref, i, count, width)
        grads[i] = grads[i] * gain_ref[:, at]
        inner = jnp.sum(grads[i] * values[i], axis=1, keepdims=True)
        total = inner if total is None else total + inner
    inner = total / (count * width)
    dot_ref[...] = inner
    scale = scale_ref[...]
    cubed = scale * scale * scale * inner
    for i in range(count):
        at = columns_of(me_ref, i, count, width)
        grad = grads[i] * scale - values[i] * cubed
        branch_ref[:, at] = (rows_ref[:, at].astype(f32) + grad).astype(bf16)


def store_halves(block, step, halves):
    length = block.shape[0] // 2
    for i in range(len(halves) // 2):

        @pl.when(step == i)
        def _(first=halves[2 * i], second=halves[2 * i + 1]):
            first[...] = block[:length]
            second[...] = block[length:]


def branch_part_kernel(me_ref, head_ref, weight_ref, *halves):
    store_halves(dot(head_ref[...], weight_ref[...]).astype(bf16), pl.program_id(0), halves)


def mid_part_kernel(me_ref, grad_ref, weight_ref, *halves):
    part = dot(grad_ref[0], weight_ref[0], NT) + dot(grad_ref[1], weight_ref[1], NT)
    store_halves(part.astype(bf16), pl.program_id(0), halves)


def in_part_kernel(
    me_ref, proj_ref, logit_ref, weight_ref, strength_ref, normed_ref, *outs
):
    *halves, inner_ref = outs
    step = pl.program_id(0)
    part = dot(logit_ref[...], strength_ref[...])
    for j in range(3):
        part = part + dot(proj_ref[j], weight_ref[j], NT)
    store_halves(part.astype(bf16), step, halves)
    ones = jnp.ones((8, part.shape[1]), f32)
    product = dot(ones, part * normed_ref[...].astype(f32), NT)

    @pl.when(step == 0)
    def _():
        inner_ref[...] = product

    @pl.when(step > 0)
    def _():
        inner_ref[...] += product


def feed_weights_kernel(left_ref, right_ref, *refs):
    refs[-1][...] = dot(left_ref[...], right_ref[...], TN).astype(bf16)


def gate_kernel(gated_ref, hidden_ref, grad_ref, features_ref):
    gate, up, hidden = gated_ref[0], gated_ref[1], hidden_ref[...]
    sig = sigmoid(gate)
    act = gate * sig
    features_ref[...] = (act * up).astype(bf16)
    grad_ref[0] = (hidden * up * sig * (1.0 + gate * (1.0 - sig))).astype(bf16)
    grad_ref[1] = (hidden * act).astype(bf16)


def store_by_core(core_ref, block, columns, ours_ref, theirs_ref):
    chips, rows, _ = ours_ref.shape

    def store(first, second):
        for chip in range(chips):
            start = 2 * chip * rows
            first[chip, :, columns] = block[start : start + rows]
            second[chip, :, columns] = block[start + rows : start + 2 * rows]

    @pl.when(core_ref[0] == 0)
    def _():
        store(ours_ref, theirs_ref)

    @pl.when(core_ref[0] == 1)
    def _():
        store(theirs_ref, ours_ref)


def mix_weights_kernel(
    core_ref, normed_ref, proj_ref, logit_ref, weight_ref, strength_weight_ref,
    ours_ref, theirs_ref, strength_ref, gain_ref,
):
    count, _, width = proj_ref.shape
    total = None
    for j in range(count):
        block = dot(normed_ref[...], proj_ref[j], TN)
        product = block * weight_ref[j].astype(f32)
        total = product if total is None else total + product
        columns = slice(j * width, (j + 1) * width)
        store_by_core(core_ref, block.astype(bf16), columns, ours_ref, theirs_ref)
    strength = dot(logit_ref[...], normed_ref[...], TN)
    strength_ref[...] = strength
    high, low = split(total)
    ones = jnp.ones((8, width), bf16)
    extra = jnp.sum(strength * strength_weight_ref[...].astype(f32), axis=0, keepdims=True)
    gain_ref[...] = dot(ones, high, NT) + dot(ones, low, NT) + extra


def out_weights_kernel(core_ref, branch_ref, head_ref, ours_ref, theirs_ref):
    block = dot(branch_ref[...], head_ref[...], TN).astype(bf16)
    store_by_core(core_ref, block, slice(0, head_ref.shape[1]), ours_ref, theirs_ref)


def in_hbm(*values):
    return [pltpu.with_memory_space_constraint(value, pltpu.HBM) for value in values]


def cost(microseconds):
    return pl.CostEstimate(
        flops=0, bytes_accessed=int(microseconds * 3_000_000), transcendentals=0
    )


def kernel_params():
    return pltpu.CompilerParams(vmem_limit_bytes=20 * 1024 * 1024)


def spec(block, index):
    return pl.BlockSpec(block, index)


def mixer_calls(seqs, length, heads):
    chains = seqs * heads
    width = heads * HEAD_DIM
    at = {
        "proj": spec((3, 1, length, width), lambda s: (0, s, 0, 0)),
        "halo": spec((3, 1, HALO, width), lambda s: (0, s, 0, 0)),
        "conv": spec((3, CONV, width), lambda s: (0, 0, 0)),
        "strength": spec((1, length, heads), lambda s: (s, 0, 0)),
        "tokens": spec((heads, length, HEAD_DIM), lambda s: (s, 0, 0)),
        "fixed": spec((heads, HEAD_DIM, HEAD_DIM), lambda s: (0, 0, 0)),
        "state": spec((heads, HEAD_DIM, HEAD_DIM), lambda s: (s, 0, 0)),
        "three": spec((heads, 3, HALF, HALF), lambda s: (s, 0, 0, 0)),
        "two": spec((heads, 2, HALF, HALF), lambda s: (s, 0, 0, 0)),
        "rows": spec((1, length, width), lambda s: (s, 0, 0)),
        "mask": spec((1, length, 1), lambda s: (s, 0, 0)),
        "gain": spec((1, HEAD_DIM), lambda s: (0, 0)),
    }
    shape = {
        "tokens": lambda kind: pltpu.HBM((chains, length, HEAD_DIM), kind),
        "three": pltpu.HBM((chains, 3, HALF, HALF), bf16),
        "two": pltpu.HBM((chains, 2, HALF, HALF), bf16),
    }
    return at, shape


def from_behind(value, axis, steps):
    count = lax.axis_size(axis)
    initial, last = (max(0, -steps), min(count, count - steps))
    return lax.ppermute(value, axis, [(source, source + steps) for source in range(initial, last)])


def exchange(blocks, axis):
    return lax.all_to_all(blocks, axis, 0, 0)


def along_head(value, steps):
    count = lax.axis_size("head")
    return lax.ppermute(value, "head", [(i, (i + steps) % count) for i in range(count)])


def gather_near(first, second):
    left_first, right_second = along_head(first, 1), along_head(second, -1)
    left_second, right_first = along_head(second, 1), along_head(first, -1)
    return left_first, left_second, right_first, right_second


def gather_far(left_first, right_second):
    return along_head(left_first, 1), along_head(right_second, -1)


def gather_pieces(first, second):
    left_first, left_second, right_first, right_second = gather_near(first, second)
    far = gather_far(left_first, right_second)
    return first, second, right_first, right_second, *far, left_first, left_second


def reduce_far(pieces):
    _, _, right_first, right_second, far_first, far_second, left_first, left_second = pieces
    came_first, came_second = along_head(far_first, 1), along_head(far_second, -1)
    from_left, from_right = along_head(right_second, 1), along_head(left_first, -1)
    to_right = (right_first.astype(f32) + came_first.astype(f32)).astype(bf16)
    to_left = (left_second.astype(f32) + came_second.astype(f32)).astype(bf16)
    return to_right, to_left, from_left, from_right


def reduce_near(pieces, to_right, to_left, from_left, from_right):
    far_left, far_right = along_head(to_right, 1), along_head(to_left, -1)
    return (
        pieces[0].astype(f32) + from_right.astype(f32) + far_left.astype(f32),
        pieces[1].astype(f32) + from_left.astype(f32) + far_right.astype(f32),
    )


def reduce_pieces(pieces):
    return reduce_near(pieces, *reduce_far(pieces))


SIDE = 4
Y_STRIDE, Z_STRIDE = 2, 2 * SIDE


def along_chips(value, stride, steps):
    pairs = []
    for i in range(lax.axis_size("seq")):
        at = i // stride % SIDE
        pairs.append((i, i + ((at + steps) % SIDE - at) * stride))
    return lax.ppermute(value, "seq", pairs)


def from_below(value, stride):
    return [value] + [along_chips(value, stride, steps) for steps in range(1, SIDE)]


def swap_cores(value):
    return lax.ppermute(value, "seq", [(i, i ^ 1) for i in range(lax.axis_size("seq"))])


def join_cores(ours, theirs):
    came = swap_cores(theirs)
    return (ours.astype(f32) + came.astype(f32)).astype(bf16)


def exchange_chips(parts):
    count = lax.axis_size("seq")
    groups = [list(range(first, count, 2)) for first in range(2)]
    return lax.all_to_all(parts, "seq", 0, 0, axis_index_groups=groups)


def together(*values):
    return lax.optimization_barrier(values)


def shards(
    tokens,
    lengths,
    norm_gain,
    query_key_value_weight,
    strength_projection,
    conv_weight,
    head_gain,
    output_projection,
    mlp_gain,
    gate_up_weight,
    down_projection,
    out_grad,
):
    seqs, length, width = tokens.shape
    model = norm_gain.shape[0]
    heads = width // HEAD_DIM
    chains = seqs * heads
    rows = seqs * length
    devices = lax.axis_size("head")
    blocks = lax.axis_size("seq")
    hidden = down_projection.shape[0]
    col_start = lax.axis_index("head") * width
    positions = lax.axis_index("seq") * length + jnp.arange(length, dtype=jnp.int32)
    mask = (positions[None, :] < lengths[:, None]).astype(f32)[:, :, None]
    index = lax.axis_index("seq")
    core = lax.rem(index, 2)
    place = jnp.stack([index // Z_STRIDE, index // Y_STRIDE % SIDE, core])
    in_scalars = pl.BlockSpec(memory_space=pltpu.SMEM)
    at, shape = mixer_calls(seqs, length, heads)
    gain_row = head_gain[None, :]
    norm_row, mlp_row = norm_gain[None, :], mlp_gain[None, :]
    own = tokens.reshape(rows, width)
    tile = 128
    whole = lambda *size: spec(size, lambda i: (0,) * len(size))
    row_tile = lambda n: spec((tile, n), lambda i: (i, 0))
    part_tile = spec((devices, tile, width), lambda i: (0, i, 0))

    me = lax.axis_index("head").reshape(1)
    half = rows // 2
    first_half = spec((tile, width), lambda i, me: (jnp.minimum(i, half // tile - 1), 0))
    second_half = spec((tile, width), lambda i, me: (jnp.maximum(i - half // tile, 0), 0))
    pieces = [first_half, second_half] * devices
    on = lambda step, offset: lax.rem(step + offset, devices)
    fixed = lambda *size: spec(size, lambda i, me: (0,) * len(size))
    moving = lambda n: spec((tile, n), lambda i, me: (i, 0))

    def on_pieces(microseconds, kernel, grid, in_specs, out_specs, out_shape):
        return pl.pallas_call(
            kernel,
            grid_spec=pltpu.PrefetchScalarGridSpec(
                num_scalar_prefetch=1, grid=(grid,), in_specs=in_specs, out_specs=out_specs
            ),
            out_shape=out_shape,
            compiler_params=kernel_params(),
            cost_estimate=cost(microseconds),
        )

    half_shape = jax.ShapeDtypeStruct((half, width), bf16)
    own_halves = (tokens[0], tokens[1])
    full = gather_pieces(*own_halves)
    full, grad_own = together(full, out_grad.reshape(rows, width))
    grad_rows = lax.all_gather(grad_own, "head", axis=1, tiled=True)
    normed_in, in_scale, strength = on_pieces(
        2.6,
        in_norm_kernel,
        rows // tile,
        [*pieces, fixed(1, model), fixed(heads, model), moving(1)],
        [moving(model), moving(1), moving(heads)],
        [
            jax.ShapeDtypeStruct((rows, model), bf16),
            jax.ShapeDtypeStruct((rows, 1), f32),
            jax.ShapeDtypeStruct((rows, heads), f32),
        ],
    )(me, *in_hbm(*full), norm_row, strength_projection.T, mask.reshape(rows, 1))
    strength = strength.reshape(seqs, length, heads)
    projected = jnp.einsum(
        "if,tfw->tiw", normed_in, query_key_value_weight, preferred_element_type=f32
    ).astype(bf16).reshape(3, seqs, length, width)
    halo = from_behind(projected[:, :, length - HALO :, :], "seq", 1)

    send, q, k, w, u, gram, score, inv = pl.pallas_call(
        partial(span_kernel, heads),
        grid=(seqs,),
        in_specs=[at["proj"], at["halo"], at["conv"], at["strength"]],
        out_specs=[
            spec((heads, 2 * HEAD_DIM, HEAD_DIM), lambda s: (s, 0, 0)),
            at["tokens"], at["tokens"], at["tokens"], at["tokens"],
            at["three"], at["three"], at["two"],
        ],
        out_shape=[
            jax.ShapeDtypeStruct((chains, 2 * HEAD_DIM, HEAD_DIM), bf16),
            *[shape["tokens"](bf16)] * 4,
            shape["three"], shape["three"], shape["two"],
        ],
        scratch_shapes=[pltpu.VMEM((heads * 3, HALO + length, HEAD_DIM), f32)],
        compiler_params=kernel_params(),
        cost_estimate=cost(11.5),
    )(projected, halo, conv_weight, strength)

    def by_sequence(value):
        value = value.reshape((seqs, heads) + value.shape[1:])
        return [lax.dynamic_index_in_dim(value, n, 0, False) for n in (core, 1 - core)]

    def scan_step(kernel, shapes, scratch, *values):
        return pl.pallas_call(
            kernel,
            in_specs=[in_scalars] + [pl.BlockSpec(memory_space=pltpu.VMEM)] * len(values),
            out_specs=[pl.BlockSpec(memory_space=pltpu.VMEM)] * len(shapes),
            out_shape=[jax.ShapeDtypeStruct(shape, bf16) for shape in shapes],
            scratch_shapes=[pltpu.VMEM(shape, bf16) for shape in scratch],
            compiler_params=kernel_params(),
            cost_estimate=cost(2.0),
        )(place, *values)

    block_shape, map_shape = (heads, 2 * HEAD_DIM, HEAD_DIM), (heads, HEAD_DIM, HEAD_DIM)
    maps_shape = (SIDE,) + map_shape
    send_own, send_other = by_sequence(send)
    cores = (send_own, swap_cores(send_other))
    chip, core_maps = scan_step(chip_kernel, [block_shape, (2,) + map_shape], [], *cores)
    chips = from_below(chip, Y_STRIDE)
    hidden_grad = jnp.einsum("xp,hp->xh", grad_rows, down_projection, preferred_element_type=f32)
    chips[1], hidden_grad = together(chips[1], hidden_grad)
    plane, chip_maps = scan_step(
        plane_kernel, [block_shape, maps_shape], [(SIDE,) + block_shape], *chips
    )
    planes = from_below(plane, Z_STRIDE)
    state_ours, state_theirs, plane_maps = scan_step(
        enter_kernel, [map_shape, map_shape, maps_shape], [], *planes, *chips, *cores
    )
    state = (state_ours, swap_cores(state_theirs))

    head_out, x, mixer = pl.pallas_call(
        partial(mixer_kernel, heads),
        grid=(seqs,),
        in_specs=[
            in_scalars, at["fixed"], at["fixed"], at["tokens"], at["tokens"], at["tokens"],
            at["three"], at["gain"], at["mask"],
        ],
        out_specs=[at["rows"], at["tokens"], at["tokens"]],
        out_shape=[
            jax.ShapeDtypeStruct((seqs, length, width), bf16),
            shape["tokens"](bf16),
            shape["tokens"](f32),
        ],
        compiler_params=kernel_params(),
        cost_estimate=cost(2.3),
    )(place, *state, *in_hbm(q, w, u, score), gain_row, mask)
    head_out = head_out.reshape(rows, width)

    def bound_for(order):
        return lambda i, me: lax.rem(me[0] + sum((i == n) * at for n, at in enumerate(order)), devices)

    order = (2, 1, 3, 0)
    to = bound_for(order)
    came = on_pieces(
        2.2,
        branch_part_kernel,
        devices,
        [fixed(rows, width), spec((width, width), lambda i, me: (0, to(i, me)))],
        [fixed(half, width)] * 8,
        [half_shape] * 8,
    )(me, head_out, output_projection)
    branch = [came[2 * order.index(i // 2) + i % 2] for i in range(8)]
    middle_own = [
        mine.astype(f32) + other for mine, other in zip(own_halves, reduce_pieces(branch))
    ]
    middle = gather_pieces(*[value.astype(bf16) for value in middle_own])
    normed_mid, mid_scale = on_pieces(
        1.5,
        mid_norm_kernel,
        rows // tile,
        [*pieces, fixed(1, model)],
        [moving(model), moving(1)],
        [jax.ShapeDtypeStruct((rows, model), bf16), jax.ShapeDtypeStruct((rows, 1), f32)],
    )(me, *middle, mlp_row)

    gated = jnp.einsum("ux,gxt->gut", normed_mid, gate_up_weight, preferred_element_type=f32)
    gated_grad, features = pl.pallas_call(
        gate_kernel,
        grid=(rows // tile,),
        in_specs=[spec((2, tile, hidden), lambda i: (0, i, 0)), row_tile(hidden)],
        out_specs=[spec((2, tile, hidden), lambda i: (0, i, 0)), row_tile(hidden)],
        out_shape=[
            jax.ShapeDtypeStruct((2, rows, hidden), bf16),
            jax.ShapeDtypeStruct((rows, hidden), bf16),
        ],
        compiler_params=kernel_params(),
        cost_estimate=cost(2.4),
    )(gated, hidden_grad)
    mid_parts = []
    for order in ((2,), (1, 3, 0)):
        to = bound_for(order)
        mid_parts += on_pieces(
            2.0 * len(order),
            mid_part_kernel,
            len(order),
            [
                fixed(2, rows, hidden),
                spec((2, width, hidden), lambda i, me, to=to: (0, to(i, me), 0)),
            ],
            [fixed(half, width)] * (2 * len(order)),
            [half_shape] * (2 * len(order)),
        )(me, gated_grad, gate_up_weight)
    order = (2, 1, 3, 0)
    mid_parts = [mid_parts[2 * order.index(i // 2) + i % 2] for i in range(8)]

    split_rows = 4

    def feed_weights(column, left, right, right_spec, into):
        extra = () if into is None else (into,)
        return pl.pallas_call(
            feed_weights_kernel,
            grid=(split_rows,),
            in_specs=[spec((rows, model // split_rows), lambda i: (0, i)), right_spec]
            + [pl.BlockSpec(memory_space=pl.ANY)] * len(extra),
            out_specs=spec((model // split_rows, hidden), lambda i: (i, column)),
            out_shape=pltpu.HBM((model, 3 * hidden), bf16),
            input_output_aliases={2: 0} if extra else {},
            compiler_params=kernel_params(),
        cost_estimate=cost(5.6),
        )(left, right, *extra)

    to_right, to_left, from_left, from_right = reduce_far(mid_parts)
    to_right, to_left, features = together(to_right, to_left, features)
    feed_part = feed_weights(2, grad_rows, features, whole(rows, hidden), None)
    far_left, far_right = along_head(to_right, 1), along_head(to_left, -1)
    far_left, far_right, feed_part = together(far_left, far_right, feed_part)
    mid_grad_own = (
        mid_parts[0].astype(f32) + from_right.astype(f32) + far_left.astype(f32),
        mid_parts[1].astype(f32) + from_left.astype(f32) + far_right.astype(f32),
    )
    first, second = [value.astype(bf16) for value in mid_grad_own]
    first, second, gated_grad = together(first, second, gated_grad)
    left_first, left_second, right_first, right_second = gather_near(first, second)
    right_spec = lambda j: spec((None, rows, hidden), lambda i: (j, 0, 0))
    feed_part = feed_weights(0, normed_mid, gated_grad, right_spec(0), feed_part)
    left_first, right_second, feed_part, features = together(
        left_first, right_second, feed_part, features
    )
    far = gather_far(left_first, right_second)
    feed = jnp.dot(features, down_projection, preferred_element_type=f32).astype(bf16)
    left_second, right_first, gated_grad, feed = together(left_second, right_first, gated_grad, feed)
    feed_part = feed_weights(1, normed_mid, gated_grad, right_spec(1), feed_part)
    *far, feed_part = together(*far, feed_part)
    mid_grad = (first, second, right_first, right_second, *far, left_first, left_second)
    feed_sum = lax.psum_scatter(feed_part, "seq", scatter_dimension=0, tiled=True)

    branch_grad, mid_dot = on_pieces(
        4.7,
        mid_back_kernel,
        rows // tile,
        [*pieces, *pieces, moving(model), fixed(1, model), moving(1)],
        [moving(model), moving(1)],
        [jax.ShapeDtypeStruct((rows, model), bf16), jax.ShapeDtypeStruct((rows, 1), f32)],
    )(me, *in_hbm(*middle, *mid_grad, grad_rows), mlp_row, mid_scale)
    own_gain = lax.dynamic_slice_in_dim(mlp_gain, col_start, width, 0)
    middle_grad_own, mlp_gain_part = [], 0.0
    for i in range(2):
        scale, inner = mid_scale[i * half : (i + 1) * half], mid_dot[i * half : (i + 1) * half]
        middle_grad_own.append(
            out_grad[i].astype(f32) + scale * own_gain * mid_grad_own[i]
            - scale * scale * scale * middle_own[i] * inner
        )
        mlp_gain_part += jnp.sum(mid_grad_own[i] * middle_own[i] * scale, axis=0)
    head_grad = jnp.einsum(
        "pj,wj->pw", branch_grad, output_projection, preferred_element_type=f32
    ).astype(bf16).reshape(seqs, length, width)

    send_back, dmix, dx, dgain = pl.pallas_call(
        partial(head_back_kernel, heads),
        grid=(seqs,),
        in_specs=[
            at["rows"], at["tokens"], at["gain"], at["mask"], at["tokens"], at["tokens"],
            at["three"],
        ],
        out_specs=[
            at["state"], at["tokens"], at["tokens"],
            spec((heads, 1, HEAD_DIM), lambda s: (s, 0, 0)),
        ],
        out_shape=[
            jax.ShapeDtypeStruct((chains, HEAD_DIM, HEAD_DIM), bf16),
            shape["tokens"](bf16),
            shape["tokens"](f32),
            jax.ShapeDtypeStruct((chains, 1, HEAD_DIM), f32),
        ],
        compiler_params=kernel_params(),
        cost_estimate=cost(3.3),
    )(head_grad, *in_hbm(mixer), gain_row, mask, *in_hbm(q, w, score))

    steps, rows_own = 4, model // blocks
    chip_count = blocks // 2
    by_core = lambda n: spec((chip_count // steps, rows_own, n), lambda i: (i, 0, 0))
    core_shape = lambda n: jax.ShapeDtypeStruct((chip_count, rows_own, n), bf16)
    model_tile = spec((rows, model // steps), lambda i: (0, i))

    back_own, back_other = by_sequence(send_back)
    out_ours, out_theirs = pl.pallas_call(
        out_weights_kernel,
        grid=(steps,),
        in_specs=[in_scalars, model_tile, whole(rows, width)],
        out_specs=[by_core(width)] * 2,
        out_shape=[core_shape(width)] * 2,
        compiler_params=kernel_params(),
        cost_estimate=cost(2.3),
    )(core.reshape(1), branch_grad, head_out)
    chip_add, last_adds = scan_step(
        back_chip_kernel, [map_shape] * 2, [], core_maps, back_own, swap_cores(back_other)
    )
    chip_adds = from_below(chip_add, Y_STRIDE)
    chip_adds[1], out_ours, out_theirs = together(chip_adds[1], out_ours, out_theirs)
    plane_add, chip_adds = scan_step(
        back_plane_kernel, [map_shape, maps_shape], [], chip_maps, *chip_adds
    )
    plane_adds = from_below(plane_add, Z_STRIDE)
    out_joined = join_cores(out_ours, out_theirs)
    plane_adds[1], out_joined = together(plane_adds[1], out_joined)
    dstate_ours, dstate_theirs = scan_step(
        back_enter_kernel, [map_shape] * 2, [maps_shape],
        core_maps, chip_maps, plane_maps, last_adds, chip_adds, *plane_adds,
    )
    dstate = (dstate_ours, swap_cores(dstate_theirs))
    dstate_ours, out_joined = together(dstate_ours, out_joined)
    dstate = (dstate_ours, dstate[1])
    out_spread = exchange_chips(out_joined)

    dproj, tail, ahead, dlogit, dconv = pl.pallas_call(
        partial(span_back_kernel, heads),
        grid=(seqs,),
        in_specs=[
            in_scalars, at["fixed"], at["fixed"], at["fixed"], at["fixed"],
            at["proj"], at["halo"], at["conv"], at["strength"],
            at["tokens"], at["tokens"], at["tokens"], at["three"], at["two"],
        ],
        out_specs=[
            at["proj"], at["halo"], at["halo"], at["strength"],
            spec((3, 1, CONV, width), lambda s: (0, s, 0, 0)),
        ],
        out_shape=[
            jax.ShapeDtypeStruct((3, seqs, length, width), bf16),
            jax.ShapeDtypeStruct((3, seqs, HALO, width), f32),
            jax.ShapeDtypeStruct((3, seqs, HALO, width), bf16),
            jax.ShapeDtypeStruct((seqs, length, heads), f32),
            jax.ShapeDtypeStruct((3, seqs, CONV, width), f32),
        ],
        scratch_shapes=[
            pltpu.VMEM((heads * 3, HALO + length, HEAD_DIM), f32),
            pltpu.VMEM((heads * 3, 2 * HALO + length, HEAD_DIM), f32),
        ],
        compiler_params=kernel_params(),
        cost_estimate=cost(10.5),
    )(
        place, *state, *dstate, projected, halo, conv_weight, strength,
        *in_hbm(x, dmix, dx, gram, inv),
    )

    sent_back = from_behind(ahead, "seq", -1).astype(f32)
    proj_grad = lax.dynamic_update_slice_in_dim(
        dproj, (tail + sent_back).astype(bf16), length - HALO, 2
    ).reshape(3, rows, width)
    logit_grad = dlogit.astype(bf16).reshape(rows, heads)

    mix_ours, mix_theirs, strength_part, norm_gain_part = pl.pallas_call(
        mix_weights_kernel,
        grid=(steps,),
        in_specs=[in_scalars, model_tile, whole(3, rows, width), whole(rows, heads),
            spec((3, model // steps, width), lambda i: (0, i, 0)),
            spec((heads, model // steps), lambda i: (0, i)),
        ],
        out_specs=[by_core(3 * width)] * 2
        + [spec((n, model // steps), lambda i: (0, i)) for n in (heads, 8)],
        out_shape=[pltpu.HBM((chip_count, rows_own, 3 * width), bf16)] * 2
        + [jax.ShapeDtypeStruct((n, model), f32) for n in (heads, 8)],
        compiler_params=kernel_params(),
        cost_estimate=cost(9.0),
    )(core.reshape(1), normed_in, proj_grad, logit_grad, *in_hbm(query_key_value_weight), strength_projection.T)
    mix_ours, mix_theirs, out_spread = together(mix_ours, mix_theirs, out_spread)
    out_sum = jnp.sum(out_spread.astype(f32), axis=0)
    mix_joined = join_cores(mix_ours, mix_theirs)

    in_parts, inners = [], []
    for order in ((2,), (1, 3, 0)):
        to = bound_for(order)
        *parts, inner = on_pieces(
            2.0 * len(order),
            in_part_kernel,
            len(order),
            [
                fixed(3, rows, width), fixed(rows, heads),
                spec((3, width, width), lambda i, me, to=to: (0, to(i, me), 0)),
                spec((heads, width), lambda i, me, to=to: (0, to(i, me))),
                spec((rows, width), lambda i, me, to=to: (0, to(i, me))),
            ],
            [fixed(half, width)] * (2 * len(order)) + [fixed(8, rows)],
            [half_shape] * (2 * len(order)) + [jax.ShapeDtypeStruct((8, rows), f32)],
        )(me, proj_grad, logit_grad, *in_hbm(query_key_value_weight), strength_projection.T, *in_hbm(normed_in))
        in_parts += parts
        inners.append(inner[0:1])
    order = (2, 1, 3, 0)
    in_parts = [in_parts[2 * order.index(i // 2) + i % 2] for i in range(8)]

    def over_head(value):
        value = value + along_head(value, 2)
        return value + along_head(value, 1)

    each, gain_each = width // blocks, HEAD_DIM // blocks
    by_columns = jnp.concatenate(
        [
            jnp.sum(dconv, axis=1).reshape(3 * CONV, width),
            mlp_gain_part[None],
            norm_gain_part[0].reshape(devices, width),
        ]
    )
    n_own = 3 * CONV + 1
    by_columns = jnp.swapaxes(by_columns.reshape(n_own + devices, blocks, each), 0, 1)
    by_rows = jnp.swapaxes(strength_part.reshape(heads, blocks, rows_own), 0, 1)
    by_gains = jnp.pad(
        jnp.sum(dgain, axis=(0, 1)).reshape(blocks, gain_each), ((0, 0), (0, each - gain_each))
    )
    small = jnp.concatenate(
        [by_rows.reshape(blocks, -1), by_columns.reshape(blocks, -1), by_gains], axis=1
    )
    small = exchange(small[:, None], "seq")
    in_parts[2], in_parts[7], mix_joined, small, inners = together(
        in_parts[2], in_parts[7], mix_joined, small, inners
    )
    mix_spread = exchange_chips(mix_joined)
    in_grad = reduce_pieces(in_parts)
    in_dot = inners[0] + inners[1]
    in_dot = in_dot + along_head(in_dot, 2)
    in_dot, feed, feed_sum = together(in_dot, feed, feed_sum)
    feed_sum = feed_sum.astype(f32)
    feed_own = lax.psum_scatter(feed, "head", scatter_dimension=1, tiled=True).astype(f32)
    output = jnp.concatenate(middle_own) + feed_own
    in_dot = (in_dot + along_head(in_dot, 1))[0][:, None] / model
    in_gain = lax.dynamic_slice_in_dim(norm_gain, col_start, width, 0)
    tokens_grad = []
    for i in range(2):
        scale, inner = in_scale[i * half : (i + 1) * half], in_dot[i * half : (i + 1) * half]
        mine = own_halves[i].astype(f32)
        tokens_grad.append(
            scale * in_gain * in_grad[i] - scale * scale * mine * inner + middle_grad_own[i]
        )
    tokens_grad = jnp.stack(tokens_grad).astype(bf16)

    small = jnp.sum(small, axis=(0, 1))
    n_rows = heads * rows_own
    head_sums = small[n_rows + n_own * each :]
    head_sums = head_sums + along_head(head_sums, 2)
    head_sums = head_sums + along_head(head_sums, 1)
    own_columns = small[n_rows : n_rows + n_own * each].reshape(n_own, each)
    norm_gain_own = lax.dynamic_slice_in_dim(
        head_sums, lax.axis_index("head") * each, each, 0
    ) / lax.dynamic_slice_in_dim(in_gain, index * each, each, 0)
    head_gain_own = head_sums[devices * each : devices * each + gain_each]
    output = output.astype(bf16).reshape(seqs, length, width)
    gate_up_grad = jnp.moveaxis(feed_sum[:, : 2 * hidden].reshape(rows_own, 2, hidden), 1, 0)
    out_weight_grad, down_grad = out_sum.T, feed_sum[:, 2 * hidden :].T
    mix_spread, output, tokens_grad, gate_up_grad, out_weight_grad, down_grad = together(
        mix_spread, output, tokens_grad, gate_up_grad, out_weight_grad, down_grad
    )
    mix_sum = jnp.sum(mix_spread.astype(f32), axis=0)
    qkv_grad = jnp.moveaxis(mix_sum.reshape(rows_own, 3, width), 1, 0)
    return (
        output,
        tokens_grad,
        norm_gain_own,
        qkv_grad,
        small[:n_rows].reshape(heads, rows_own).T,
        own_columns[: 3 * CONV].reshape(3, CONV, each),
        head_gain_own,
        out_weight_grad,
        own_columns[3 * CONV],
        gate_up_grad,
        down_grad,
    )


def solution(mesh):
    return jax.shard_map(
        shards,
        mesh=mesh,
        in_specs=(
            P(None, "seq", "head"),
            P(),
            P(),
            P(None, None, "head"),
            P(None, "head"),
            P(None, None, "head"),
            P(),
            P("head", None),
            P(),
            P(None, None, "head"),
            P("head", None),
            P(None, "seq", "head"),
        ),
        out_specs=(
            P(None, "seq", "head"),
            P(None, "seq", "head"),
            P(("head", "seq")),
            P(None, "seq", "head"),
            P("seq", "head"),
            P(None, None, ("head", "seq")),
            P("seq"),
            P("head", "seq"),
            P(("head", "seq")),
            P(None, "seq", "head"),
            P("head", "seq"),
        ),
        check_vma=False,
    )
```

```python
from functools import partial

import jax
import jax.numpy as jnp
from jax import lax
from jax.experimental import pallas as pl
from jax.experimental.pallas import tpu as pltpu
from jax.sharding import PartitionSpec as P

HEAD_DIM = 128
CONV = 4
HALF = 128
HALO = 8
EPS = 1e-06

f32 = jnp.float32
bf16 = jnp.bfloat16


def dot(a, b, dims=((1,), (0,))):
    return lax.dot_general(
        a.astype(bf16), b.astype(bf16), (dims, ((), ())), preferred_element_type=f32
    )


NT = ((1,), (1,))
TN = ((0,), (0,))


def split(a):
    high = a.astype(bf16)
    return high, (a - high.astype(f32)).astype(bf16)


def dot3(a, b):
    a_high, a_low = split(a)
    b_high, b_low = split(b)
    return dot(a_high, b_high) + (dot(a_high, b_low) + dot(a_low, b_high))


def unit_lower_inverses(stricts):
    size = stricts[0].shape[0]
    row = lax.broadcasted_iota(jnp.int32, (size, size), 0)
    col = lax.broadcasted_iota(jnp.int32, (size, size), 1)
    eye = jnp.where(row == col, 1.0, 0.0)
    below = (row // 2 == col // 2) & (row != col)
    inverses = [eye - jnp.where(below, strict, 0.0) for strict in stricts]
    width = 2
    while width < size:
        below = (row // (2 * width) == col // (2 * width)) & (row // width != col // width)
        parts = [
            dot(jnp.where(below, strict, 0.0), inverse)
            for strict, inverse in zip(stricts, inverses)
        ]
        inverses = [inverse - dot(inverse, part) for inverse, part in zip(inverses, parts)]
        width *= 2
    errors = [
        eye - inverse - dot3(strict, inverse) for strict, inverse in zip(stricts, inverses)
    ]
    return [inverse + dot(inverse, error) for inverse, error in zip(inverses, errors)]


def sigmoid(x):
    return 1.0 / (1.0 + jnp.exp(-x))


def masks():
    row = lax.broadcasted_iota(jnp.int32, (HALF, HALF), 0)
    col = lax.broadcasted_iota(jnp.int32, (HALF, HALF), 1)
    return row > col, row >= col


def conv_rows(j, proj_ref, halo_ref, conv_ref, rows, lanes):
    length = proj_ref.shape[2]
    rows[0:HALO, :] = halo_ref[j, 0, :, lanes].astype(f32)
    rows[HALO : HALO + length, :] = proj_ref[j, 0, :, lanes].astype(f32)
    mixed = None
    for i in range(CONV):
        start = HALO - (CONV - 1) + i
        term = conv_ref[j, i : i + 1, lanes] * rows[start : start + length, :]
        mixed = term if mixed is None else mixed + term
    return mixed


def column_of(values, at):
    lane = lax.broadcasted_iota(jnp.int32, values.shape, 1)
    return jnp.sum(jnp.where(lane == at, values, 0.0), axis=1, keepdims=True)


def span_kernel(
    heads, proj_ref, halo_ref, conv_ref, strength_ref,
    send_ref, q_ref, k_ref, w_ref, u_ref, gram_ref, score_ref, inv_ref, rows,
):
    lower, lower_diag = masks()
    a, b = slice(0, HALF), slice(HALF, 2 * HALF)
    rights, grams, stricts = [], [], []
    for h in range(heads):
        lanes = slice(h * HEAD_DIM, (h + 1) * HEAD_DIM)
        active = []
        for j in range(3):
            mixed = conv_rows(j, proj_ref, halo_ref, conv_ref, rows.at[h * 3 + j], lanes)
            active.append(mixed * sigmoid(mixed))
        q = active[0] * lax.rsqrt(jnp.sum(active[0] * active[0], axis=1, keepdims=True) + EPS)
        k = active[1] * lax.rsqrt(jnp.sum(active[1] * active[1], axis=1, keepdims=True) + EPS)
        v = active[2]
        q_ref[h] = q.astype(bf16)
        k_ref[h] = k.astype(bf16)
        beta = column_of(strength_ref[0], h)
        gram = dot(k, k, NT)
        score = dot(q, k, NT)
        gaa = jnp.where(lower, gram[a, a], 0.0)
        gbb = jnp.where(lower, gram[b, b], 0.0)
        gba = gram[b, a]
        gram_ref[h, 0] = gaa.astype(bf16)
        gram_ref[h, 1] = gba.astype(bf16)
        gram_ref[h, 2] = gbb.astype(bf16)
        score_ref[h, 0] = jnp.where(lower_diag, score[a, a], 0.0).astype(bf16)
        score_ref[h, 1] = score[b, a].astype(bf16)
        score_ref[h, 2] = jnp.where(lower_diag, score[b, b], 0.0).astype(bf16)
        stricts += [beta[a] * gaa, beta[b] * gbb]
        grams.append((beta[b] * gba).astype(bf16))
        rights.append(beta * jnp.concatenate([k, v], axis=1))
    inverses = unit_lower_inverses(stricts)
    for h in range(heads):
        taa, tbb = inverses[2 * h].astype(bf16), inverses[2 * h + 1].astype(bf16)
        inv_ref[h, 0] = taa
        inv_ref[h, 1] = tbb
        k = k_ref[h]
        top = dot(taa, rights[h][a])
        bottom = dot(tbb, rights[h][b] - dot(grams[h], top))
        w = jnp.concatenate([top[:, :HEAD_DIM], bottom[:, :HEAD_DIM]], axis=0)
        u = jnp.concatenate([top[:, HEAD_DIM:], bottom[:, HEAD_DIM:]], axis=0)
        w_ref[h] = w.astype(bf16)
        u_ref[h] = u.astype(bf16)
        step = -dot(w, k, TN)
        add = dot(u, k, TN)
        send_ref[h, 0:HEAD_DIM, :] = step.astype(bf16)
        send_ref[h, HEAD_DIM:, :] = add.astype(bf16)


def through(state, block):
    high, low = split(state)
    step = block[:HEAD_DIM]
    return state + dot(high, step) + dot(low, step)


def through_back(state, block):
    high, low = split(state)
    step = block[:HEAD_DIM]
    return state + dot(high, step, NT) + dot(low, step, NT)


def added(block):
    return block[HEAD_DIM:].astype(f32)


def chip_kernel(place_ref, own_ref, came_ref, out_ref, maps_ref):
    mine_first = place_ref[2] == 0
    for c in range(out_ref.shape[0]):
        own, came = own_ref[c].astype(f32), came_ref[c].astype(f32)
        first = jnp.where(mine_first, own, came)
        second = jnp.where(mine_first, came, own)
        maps_ref[0, c] = first[:HEAD_DIM].astype(bf16)
        step = second[:HEAD_DIM].astype(bf16)
        maps_ref[1, c] = step
        out_ref[c] = (first + second + dot(first, step)).astype(bf16)


def plane_kernel(place_ref, own_ref, one_ref, two_ref, three_ref, out_ref, maps_ref, stack):
    count = stack.shape[0]
    for at, ref in enumerate((own_ref, one_ref, two_ref, three_ref)):
        stack[lax.rem(place_ref[1] - at + count, count)] = ref[...]
    maps_ref[...] = stack[:, :, :HEAD_DIM]
    for c in range(out_ref.shape[0]):
        total = None
        for y in range(count):
            block = stack[y, c]
            if total is None:
                total = block.astype(f32)
            else:
                total = through(total, block) + block.astype(f32)
        out_ref[c] = total.astype(bf16)


def enter_kernel(place_ref, *refs):
    planes, chips, (own_ref, came_ref) = refs[:4], refs[4:8], refs[8:10]
    ours_ref, theirs_ref, maps_ref = refs[10:]
    chains, count = ours_ref.shape[0], len(planes)
    for at in range(count):
        maps_ref[lax.rem(place_ref[0] - at + count, count)] = planes[at][:, :HEAD_DIM]
    states = [jnp.zeros((HEAD_DIM, HEAD_DIM), f32)] * chains
    for level, blocks in ((0, planes), (1, chips)):
        for back in range(count - 1, 0, -1):
            reached = back <= place_ref[level]
            for c in range(chains):
                block = blocks[back][c]
                after = through(states[c], block) + added(block)
                states[c] = jnp.where(reached, after, states[c])
    mine_first = place_ref[2] == 0
    for c in range(chains):
        first = jnp.where(mine_first, own_ref[c].astype(f32), came_ref[c].astype(f32))
        after = through(states[c], first.astype(bf16)) + added(first)
        ours_ref[c] = jnp.where(mine_first, states[c], after).astype(bf16)
        theirs_ref[c] = jnp.where(mine_first, after, states[c]).astype(bf16)


def back_chip_kernel(place_ref, maps_ref, own_ref, came_ref, out_ref, adds_ref):
    mine_first = place_ref[2] == 0
    for c in range(out_ref.shape[0]):
        own, came = own_ref[c].astype(f32), came_ref[c].astype(f32)
        last = jnp.where(mine_first, came, own)
        add = jnp.where(mine_first, own, came)
        adds_ref[c] = last.astype(bf16)
        out_ref[c] = (through_back(last, maps_ref[0, c]) + add).astype(bf16)


def back_plane_kernel(place_ref, maps_ref, *refs):
    adds, (out_ref, adds_ref) = refs[:4], refs[4:]
    count = len(adds)
    for at in range(count):
        adds_ref[lax.rem(place_ref[1] - at + count, count)] = adds[at][...]
    for c in range(out_ref.shape[0]):
        total = None
        for y in range(count - 1, -1, -1):
            add = adds_ref[y, c].astype(f32)
            total = add if total is None else through_back(total, maps_ref[y, c]) + add
        out_ref[c] = total.astype(bf16)


def back_enter_kernel(place_ref, core_maps, chip_maps, plane_maps, last_adds, chip_adds, *refs):
    plane_adds, (ours_ref, theirs_ref, stack) = refs[:4], refs[4:]
    chains, count = ours_ref.shape[0], len(plane_adds)
    for at in range(count):
        stack[lax.rem(place_ref[0] - at + count, count)] = plane_adds[at][...]
    states = [jnp.zeros((HEAD_DIM, HEAD_DIM), f32)] * chains
    for level, maps, adds in ((0, plane_maps, stack), (1, chip_maps, chip_adds)):
        for at in range(count - 1, 0, -1):
            reached = at > place_ref[level]
            for c in range(chains):
                after = through_back(states[c], maps[at, c]) + adds[at, c].astype(f32)
                states[c] = jnp.where(reached, after, states[c])
    mine_first = place_ref[2] == 0
    for c in range(chains):
        after = through_back(states[c], core_maps[1, c]) + last_adds[c].astype(f32)
        ours_ref[c] = jnp.where(mine_first, after, states[c]).astype(bf16)
        theirs_ref[c] = jnp.where(mine_first, states[c], after).astype(bf16)


def state_of(place_ref, ours_ref, came_ref, h):
    mine = pl.program_id(0) == place_ref[2]
    return jnp.where(mine, ours_ref[h].astype(f32), came_ref[h].astype(f32)).astype(bf16)


def mixer_kernel(
    heads, place_ref, ours_ref, came_ref, q_ref, w_ref, u_ref, score_ref, gain_ref, mask_ref,
    out_ref, x_ref, mix_ref,
):
    a, b = slice(0, HALF), slice(HALF, 2 * HALF)
    mask = mask_ref[0]
    for h in range(heads):
        lanes = slice(h * HEAD_DIM, (h + 1) * HEAD_DIM)
        state = state_of(place_ref, ours_ref, came_ref, h)
        x = u_ref[h].astype(f32) - dot(w_ref[h], state, NT)
        x_ref[h] = x.astype(bf16)
        base = dot(q_ref[h], state, NT)
        top = dot(score_ref[h, 0], x[a])
        bottom = dot(score_ref[h, 1], x[a]) + dot(score_ref[h, 2], x[b])
        mixer = base + jnp.concatenate([top, bottom], axis=0)
        mix_ref[h] = mixer
        inv = lax.rsqrt(jnp.mean(mixer * mixer, axis=1, keepdims=True) + EPS)
        out_ref[0, :, lanes] = (mixer * inv * gain_ref[...] * mask).astype(bf16)


def head_back_kernel(
    heads, grad_ref, mix_ref, gain_ref, mask_ref, q_ref, w_ref, score_ref,
    send_ref, dmix_ref, dx_ref, dgain_ref,
):
    a, b = slice(0, HALF), slice(HALF, 2 * HALF)
    mask = mask_ref[0]
    gain = gain_ref[...]
    for h in range(heads):
        lanes = slice(h * HEAD_DIM, (h + 1) * HEAD_DIM)
        grad = grad_ref[0, :, lanes].astype(f32) * mask
        mixer = mix_ref[h]
        inv = lax.rsqrt(jnp.mean(mixer * mixer, axis=1, keepdims=True) + EPS)
        scaled = mixer * inv
        dgain_ref[h] = jnp.sum(grad * scaled, axis=0, keepdims=True)
        inner = jnp.mean(gain * grad * scaled, axis=1, keepdims=True)
        dmix = inv * (gain * grad - scaled * inner)
        dmix_ref[h] = dmix.astype(bf16)
        top = dot(score_ref[h, 0], dmix[a], TN) + dot(score_ref[h, 1], dmix[b], TN)
        bottom = dot(score_ref[h, 2], dmix[b], TN)
        dx = jnp.concatenate([top, bottom], axis=0)
        dx_ref[h] = dx
        send_ref[h] = (dot(dmix, q_ref[h], TN) - dot(dx, w_ref[h], TN)).astype(bf16)


def span_back_kernel(
    heads, place_ref, ours_ref, came_ref, dours_ref, dcame_ref,
    proj_ref, halo_ref, conv_ref, strength_ref,
    x_ref, dmix_ref, dx_ref, gram_ref, inv_ref,
    dproj_ref, tail_ref, ahead_ref, dlogit_ref, dconv_ref, rows, grads,
):
    lower, lower_diag = masks()
    a, b = slice(0, HALF), slice(HALF, 2 * HALF)
    length = proj_ref.shape[2]
    lane = lax.broadcasted_iota(jnp.int32, strength_ref.shape[1:], 1)
    dlogit = jnp.zeros(strength_ref.shape[1:], f32)
    for h in range(heads):
        lanes = slice(h * HEAD_DIM, (h + 1) * HEAD_DIM)
        mixed, sig, active = [], [], []
        for j in range(3):
            mixed.append(conv_rows(j, proj_ref, halo_ref, conv_ref, rows.at[h * 3 + j], lanes))
            sig.append(sigmoid(mixed[j]))
            active.append(mixed[j] * sig[j])
        q_inv = lax.rsqrt(jnp.sum(active[0] * active[0], axis=1, keepdims=True) + EPS)
        k_inv = lax.rsqrt(jnp.sum(active[1] * active[1], axis=1, keepdims=True) + EPS)
        q, k, v = active[0] * q_inv, active[1] * k_inv, active[2]
        kb = k.astype(bf16)
        beta = column_of(strength_ref[0], h)
        state = state_of(place_ref, ours_ref, came_ref, h)
        dstate = state_of(place_ref, dours_ref, dcame_ref, h)
        x, dmix = x_ref[h], dmix_ref[h]
        gaa, gba, gbb = gram_ref[h, 0], gram_ref[h, 1], gram_ref[h, 2]
        dx = dx_ref[h] + dot(kb, dstate, NT)
        y_b = dot(inv_ref[h, 1], dx[b], TN)
        y_a = dot(inv_ref[h, 0], dx[a] - dot(gba, beta[b] * y_b, TN), TN)
        y = jnp.concatenate([y_a, y_b], axis=0)
        inner = jnp.concatenate([dot(gaa, x[a]), dot(gba, x[a]) + dot(gbb, x[b])], axis=0)
        residual = v - dot(kb, state, NT) - inner
        dbeta = jnp.sum(y * residual, axis=1, keepdims=True)
        dlogit = jnp.where(lane == h, dbeta * beta * (1.0 - beta), dlogit)
        dv = beta * y
        dgram = -dot(dv, x, NT)
        dscore = dot(dmix, x, NT)
        dg_aa = jnp.where(lower, dgram[a, a], 0.0).astype(bf16)
        dg_bb = jnp.where(lower, dgram[b, b], 0.0).astype(bf16)
        dg_ba = dgram[b, a].astype(bf16)
        ds_aa = jnp.where(lower_diag, dscore[a, a], 0.0).astype(bf16)
        ds_bb = jnp.where(lower_diag, dscore[b, b], 0.0).astype(bf16)
        ds_ba = dscore[b, a].astype(bf16)
        qb = q.astype(bf16)
        dq = dot(dmix, state) + jnp.concatenate(
            [dot(ds_aa, kb[a]), dot(ds_ba, kb[a]) + dot(ds_bb, kb[b])], axis=0
        )
        dk = dot(x, dstate) - dot(dv, state)
        dk_a = (
            dot(ds_aa, qb[a], TN) + dot(ds_ba, qb[b], TN)
            + dot(dg_aa, kb[a]) + dot(dg_aa, kb[a], TN) + dot(dg_ba, kb[b], TN)
        )
        dk_b = (
            dot(ds_bb, qb[b], TN) + dot(dg_ba, kb[a])
            + dot(dg_bb, kb[b]) + dot(dg_bb, kb[b], TN)
        )
        dk = dk + jnp.concatenate([dk_a, dk_b], axis=0)
        dact = [
            (dq - q * jnp.sum(q * dq, axis=1, keepdims=True)) * q_inv,
            (dk - k * jnp.sum(k * dk, axis=1, keepdims=True)) * k_inv,
            dv,
        ]
        for j in range(3):
            dmixed = dact[j] * sig[j] * (1.0 + mixed[j] * (1.0 - sig[j]))
            own = rows.at[h * 3 + j]
            pad = grads.at[h * 3 + j]
            pad[0:HALO, :] = jnp.zeros((HALO, HEAD_DIM), f32)
            pad[HALO : HALO + length, :] = dmixed
            pad[HALO + length :, :] = jnp.zeros((HALO, HEAD_DIM), f32)
            whole = None
            for i in range(CONV):
                start = HALO - (CONV - 1) + i
                dconv_ref[j, 0, i : i + 1, lanes] = jnp.sum(
                    dmixed * own[start : start + length, :], axis=0, keepdims=True
                )
                shift = CONV - 1 - i
                term = conv_ref[j, i : i + 1, lanes] * pad[shift : shift + HALO + length, :]
                whole = term if whole is None else whole + term
            ahead_ref[j, 0, :, lanes] = whole[0:HALO].astype(bf16)
            dproj_ref[j, 0, :, lanes] = whole[HALO:].astype(bf16)
            tail_ref[j, 0, :, lanes] = whole[length:]
    dlogit_ref[0] = dlogit


def columns_of(me_ref, offset, count, width):
    return pl.ds(pl.multiple_of(lax.rem(me_ref[0] + offset, count) * width, width), width)


def piece(refs, offset):
    first, second = refs[2 * offset], refs[2 * offset + 1]
    in_first = 2 * pl.program_id(0) < pl.num_programs(0)
    return jnp.where(in_first, first[...].astype(f32), second[...].astype(f32))


def norm_pieces(me_ref, refs, gain_ref, normed_ref, scale_ref):
    count = len(refs) // 2
    values = [piece(refs, i) for i in range(count)]
    width = values[0].shape[1]
    total = None
    for value in values:
        square = jnp.sum(value * value, axis=1, keepdims=True)
        total = square if total is None else total + square
    scale = lax.rsqrt(total / (count * width) + EPS)
    scale_ref[...] = scale
    for i in range(count):
        at = columns_of(me_ref, i, count, width)
        normed_ref[:, at] = (values[i] * scale * gain_ref[:, at]).astype(bf16)


def in_norm_kernel(me_ref, *args):
    *refs, gain_ref, weight_ref, mask_ref, normed_ref, scale_ref, strength_ref = args
    norm_pieces(me_ref, refs, gain_ref, normed_ref, scale_ref)
    strength_ref[...] = sigmoid(dot(normed_ref[...], weight_ref[...], NT)) * mask_ref[...]


def mid_norm_kernel(me_ref, *args):
    *refs, gain_ref, normed_ref, scale_ref = args
    norm_pieces(me_ref, refs, gain_ref, normed_ref, scale_ref)


def mid_back_kernel(me_ref, *args):
    *refs, rows_ref, gain_ref, scale_ref, branch_ref, dot_ref = args
    count = len(refs) // 4
    values = [piece(refs[: 2 * count], i) for i in range(count)]
    grads = [piece(refs[2 * count :], i) for i in range(count)]
    width = values[0].shape[1]
    total = None
    for i in range(count):
        at = columns_of(me_ref, i, count, width)
        grads[i] = grads[i] * gain_ref[:, at]
        inner = jnp.sum(grads[i] * values[i], axis=1, keepdims=True)
        total = inner if total is None else total + inner
    inner = total / (count * width)
    dot_ref[...] = inner
    scale = scale_ref[...]
    cubed = scale * scale * scale * inner
    for i in range(count):
        at = columns_of(me_ref, i, count, width)
        grad = grads[i] * scale - values[i] * cubed
        branch_ref[:, at] = (rows_ref[:, at].astype(f32) + grad).astype(bf16)


def store_halves(block, step, halves):
    length = block.shape[0] // 2
    for i in range(len(halves) // 2):

        @pl.when(step == i)
        def _(first=halves[2 * i], second=halves[2 * i + 1]):
            first[...] = block[:length]
            second[...] = block[length:]


def branch_part_kernel(me_ref, head_ref, weight_ref, *halves):
    store_halves(dot(head_ref[...], weight_ref[...]).astype(bf16), pl.program_id(0), halves)


def mid_part_kernel(me_ref, grad_ref, weight_ref, *halves):
    part = dot(grad_ref[0], weight_ref[0], NT) + dot(grad_ref[1], weight_ref[1], NT)
    store_halves(part.astype(bf16), pl.program_id(0), halves)


def in_part_kernel(
    me_ref, proj_ref, logit_ref, weight_ref, strength_ref, normed_ref, *outs
):
    *halves, inner_ref = outs
    step = pl.program_id(0)
    part = dot(logit_ref[...], strength_ref[...])
    for j in range(3):
        part = part + dot(proj_ref[j], weight_ref[j], NT)
    store_halves(part.astype(bf16), step, halves)
    ones = jnp.ones((8, part.shape[1]), f32)
    product = dot(ones, part * normed_ref[...].astype(f32), NT)

    @pl.when(step == 0)
    def _():
        inner_ref[...] = product

    @pl.when(step > 0)
    def _():
        inner_ref[...] += product


def feed_weights_kernel(left_ref, right_ref, *refs):
    refs[-1][...] = dot(left_ref[...], right_ref[...], TN).astype(bf16)


def gate_kernel(gated_ref, hidden_ref, grad_ref, features_ref):
    gate, up, hidden = gated_ref[0], gated_ref[1], hidden_ref[...]
    sig = sigmoid(gate)
    act = gate * sig
    features_ref[...] = (act * up).astype(bf16)
    grad_ref[0] = (hidden * up * sig * (1.0 + gate * (1.0 - sig))).astype(bf16)
    grad_ref[1] = (hidden * act).astype(bf16)


def store_by_core(core_ref, block, columns, ours_ref, theirs_ref):
    chips, rows, _ = ours_ref.shape

    def store(first, second):
        for chip in range(chips):
            start = 2 * chip * rows
            first[chip, :, columns] = block[start : start + rows]
            second[chip, :, columns] = block[start + rows : start + 2 * rows]

    @pl.when(core_ref[0] == 0)
    def _():
        store(ours_ref, theirs_ref)

    @pl.when(core_ref[0] == 1)
    def _():
        store(theirs_ref, ours_ref)


def mix_weights_kernel(
    core_ref, normed_ref, proj_ref, logit_ref, weight_ref, strength_weight_ref,
    ours_ref, theirs_ref, strength_ref, gain_ref,
):
    count, _, width = proj_ref.shape
    total = None
    for j in range(count):
        block = dot(normed_ref[...], proj_ref[j], TN)
        product = block * weight_ref[j].astype(f32)
        total = product if total is None else total + product
        columns = slice(j * width, (j + 1) * width)
        store_by_core(core_ref, block.astype(bf16), columns, ours_ref, theirs_ref)
    strength = dot(logit_ref[...], normed_ref[...], TN)
    strength_ref[...] = strength
    high, low = split(total)
    ones = jnp.ones((8, width), bf16)
    extra = jnp.sum(strength * strength_weight_ref[...].astype(f32), axis=0, keepdims=True)
    gain_ref[...] = dot(ones, high, NT) + dot(ones, low, NT) + extra


def out_weights_kernel(core_ref, branch_ref, head_ref, ours_ref, theirs_ref):
    block = dot(branch_ref[...], head_ref[...], TN).astype(bf16)
    store_by_core(core_ref, block, slice(0, head_ref.shape[1]), ours_ref, theirs_ref)


def in_hbm(*values):
    return [pltpu.with_memory_space_constraint(value, pltpu.HBM) for value in values]


def cost(microseconds):
    return pl.CostEstimate(
        flops=0, bytes_accessed=int(microseconds * 3_000_000), transcendentals=0
    )


def kernel_params():
    return pltpu.CompilerParams(vmem_limit_bytes=24 * 1024 * 1024)


def spec(block, index):
    return pl.BlockSpec(block, index)


def mixer_calls(seqs, length, heads):
    chains = seqs * heads
    width = heads * HEAD_DIM
    at = {
        "proj": spec((3, 1, length, width), lambda s: (0, s, 0, 0)),
        "halo": spec((3, 1, HALO, width), lambda s: (0, s, 0, 0)),
        "conv": spec((3, CONV, width), lambda s: (0, 0, 0)),
        "strength": spec((1, length, heads), lambda s: (s, 0, 0)),
        "tokens": spec((heads, length, HEAD_DIM), lambda s: (s, 0, 0)),
        "fixed": spec((heads, HEAD_DIM, HEAD_DIM), lambda s: (0, 0, 0)),
        "state": spec((heads, HEAD_DIM, HEAD_DIM), lambda s: (s, 0, 0)),
        "three": spec((heads, 3, HALF, HALF), lambda s: (s, 0, 0, 0)),
        "two": spec((heads, 2, HALF, HALF), lambda s: (s, 0, 0, 0)),
        "rows": spec((1, length, width), lambda s: (s, 0, 0)),
        "mask": spec((1, length, 1), lambda s: (s, 0, 0)),
        "gain": spec((1, HEAD_DIM), lambda s: (0, 0)),
    }
    shape = {
        "tokens": lambda kind: pltpu.HBM((chains, length, HEAD_DIM), kind),
        "three": pltpu.HBM((chains, 3, HALF, HALF), bf16),
        "two": pltpu.HBM((chains, 2, HALF, HALF), bf16),
    }
    return at, shape


def from_behind(value, axis, steps):
    count = lax.axis_size(axis)
    initial, last = (max(0, -steps), min(count, count - steps))
    return lax.ppermute(value, axis, [(source, source + steps) for source in range(initial, last)])


def exchange(blocks, axis):
    return lax.all_to_all(blocks, axis, 0, 0)


def along_head(value, steps):
    count = lax.axis_size("head")
    return lax.ppermute(value, "head", [(i, (i + steps) % count) for i in range(count)])


def gather_near(first, second):
    left_first, right_second = along_head(first, 1), along_head(second, -1)
    left_second, right_first = along_head(second, 1), along_head(first, -1)
    return left_first, left_second, right_first, right_second


def gather_far(left_first, right_second):
    return along_head(left_first, 1), along_head(right_second, -1)


def gather_pieces(first, second):
    left_first, left_second, right_first, right_second = gather_near(first, second)
    far = gather_far(left_first, right_second)
    return first, second, right_first, right_second, *far, left_first, left_second


def reduce_far(pieces):
    _, _, right_first, right_second, far_first, far_second, left_first, left_second = pieces
    came_first, came_second = along_head(far_first, 1), along_head(far_second, -1)
    from_left, from_right = along_head(right_second, 1), along_head(left_first, -1)
    to_right = (right_first.astype(f32) + came_first.astype(f32)).astype(bf16)
    to_left = (left_second.astype(f32) + came_second.astype(f32)).astype(bf16)
    return to_right, to_left, from_left, from_right


def reduce_near(pieces, to_right, to_left, from_left, from_right):
    far_left, far_right = along_head(to_right, 1), along_head(to_left, -1)
    return (
        pieces[0].astype(f32) + from_right.astype(f32) + far_left.astype(f32),
        pieces[1].astype(f32) + from_left.astype(f32) + far_right.astype(f32),
    )


def reduce_pieces(pieces):
    return reduce_near(pieces, *reduce_far(pieces))


SIDE = 4
Y_STRIDE, Z_STRIDE = 2, 2 * SIDE


def along_chips(value, stride, steps):
    pairs = []
    for i in range(lax.axis_size("seq")):
        at = i // stride % SIDE
        pairs.append((i, i + ((at + steps) % SIDE - at) * stride))
    return lax.ppermute(value, "seq", pairs)


def from_below(value, stride):
    return [value] + [along_chips(value, stride, steps) for steps in range(1, SIDE)]


def swap_cores(value):
    return lax.ppermute(value, "seq", [(i, i ^ 1) for i in range(lax.axis_size("seq"))])


def join_cores(ours, theirs):
    came = swap_cores(theirs)
    return (ours.astype(f32) + came.astype(f32)).astype(bf16)


def exchange_chips(parts):
    count = lax.axis_size("seq")
    groups = [list(range(first, count, 2)) for first in range(2)]
    return lax.all_to_all(parts, "seq", 0, 0, axis_index_groups=groups)


def together(*values):
    return lax.optimization_barrier(values)


def shards(
    tokens,
    lengths,
    norm_gain,
    query_key_value_weight,
    strength_projection,
    conv_weight,
    head_gain,
    output_projection,
    mlp_gain,
    gate_up_weight,
    down_projection,
    out_grad,
):
    seqs, length, width = tokens.shape
    model = norm_gain.shape[0]
    heads = width // HEAD_DIM
    chains = seqs * heads
    rows = seqs * length
    devices = lax.axis_size("head")
    blocks = lax.axis_size("seq")
    hidden = down_projection.shape[0]
    col_start = lax.axis_index("head") * width
    positions = lax.axis_index("seq") * length + jnp.arange(length, dtype=jnp.int32)
    mask = (positions[None, :] < lengths[:, None]).astype(f32)[:, :, None]
    index = lax.axis_index("seq")
    core = lax.rem(index, 2)
    place = jnp.stack([index // Z_STRIDE, index // Y_STRIDE % SIDE, core])
    in_scalars = pl.BlockSpec(memory_space=pltpu.SMEM)
    at, shape = mixer_calls(seqs, length, heads)
    gain_row = head_gain[None, :]
    norm_row, mlp_row = norm_gain[None, :], mlp_gain[None, :]
    own = tokens.reshape(rows, width)
    tile = 256
    whole = lambda *size: spec(size, lambda i: (0,) * len(size))
    row_tile = lambda n: spec((tile, n), lambda i: (i, 0))
    part_tile = spec((devices, tile, width), lambda i: (0, i, 0))

    me = lax.axis_index("head").reshape(1)
    half = rows // 2
    first_half = spec((tile, width), lambda i, me: (jnp.minimum(i, half // tile - 1), 0))
    second_half = spec((tile, width), lambda i, me: (jnp.maximum(i - half // tile, 0), 0))
    pieces = [first_half, second_half] * devices
    on = lambda step, offset: lax.rem(step + offset, devices)
    fixed = lambda *size: spec(size, lambda i, me: (0,) * len(size))
    moving = lambda n: spec((tile, n), lambda i, me: (i, 0))

    def on_pieces(microseconds, kernel, grid, in_specs, out_specs, out_shape):
        return pl.pallas_call(
            kernel,
            grid_spec=pltpu.PrefetchScalarGridSpec(
                num_scalar_prefetch=1, grid=(grid,), in_specs=in_specs, out_specs=out_specs
            ),
            out_shape=out_shape,
            compiler_params=kernel_params(),
            cost_estimate=cost(microseconds),
        )

    half_shape = jax.ShapeDtypeStruct((half, width), bf16)
    own_halves = (tokens[0], tokens[1])
    full = gather_pieces(*own_halves)
    full, grad_own = together(full, out_grad.reshape(rows, width))
    grad_rows = lax.all_gather(grad_own, "head", axis=1, tiled=True)
    normed_in, in_scale, strength = on_pieces(
        2.6,
        in_norm_kernel,
        rows // tile,
        [*pieces, fixed(1, model), fixed(heads, model), moving(1)],
        [moving(model), moving(1), moving(heads)],
        [
            jax.ShapeDtypeStruct((rows, model), bf16),
            pltpu.HBM((rows, 1), f32),
            pltpu.HBM((rows, heads), f32),
        ],
    )(me, *in_hbm(*full, norm_row, strength_projection.T, mask.reshape(rows, 1)))
    strength = strength.reshape(seqs, length, heads)
    projected = jnp.einsum(
        "if,tfw->tiw", normed_in, query_key_value_weight, preferred_element_type=f32
    ).astype(bf16).reshape(3, seqs, length, width)
    halo = from_behind(projected[:, :, length - HALO :, :], "seq", 1)

    send, q, k, w, u, gram, score, inv = pl.pallas_call(
        partial(span_kernel, heads),
        grid=(seqs,),
        in_specs=[at["proj"], at["halo"], at["conv"], at["strength"]],
        out_specs=[
            spec((heads, 2 * HEAD_DIM, HEAD_DIM), lambda s: (s, 0, 0)),
            at["tokens"], at["tokens"], at["tokens"], at["tokens"],
            at["three"], at["three"], at["two"],
        ],
        out_shape=[
            jax.ShapeDtypeStruct((chains, 2 * HEAD_DIM, HEAD_DIM), bf16),
            *[shape["tokens"](bf16)] * 4,
            shape["three"], shape["three"], shape["two"],
        ],
        scratch_shapes=[pltpu.VMEM((heads * 3, HALO + length, HEAD_DIM), f32)],
        compiler_params=kernel_params(),
        cost_estimate=cost(11.5),
    )(projected, halo, *in_hbm(conv_weight, strength))

    def by_sequence(value):
        value = value.reshape((seqs, heads) + value.shape[1:])
        return [lax.dynamic_index_in_dim(value, n, 0, False) for n in (core, 1 - core)]

    def scan_step(kernel, shapes, scratch, *values):
        return pl.pallas_call(
            kernel,
            in_specs=[in_scalars] + [pl.BlockSpec(memory_space=pltpu.VMEM)] * len(values),
            out_specs=[pl.BlockSpec(memory_space=pltpu.VMEM)] * len(shapes),
            out_shape=[jax.ShapeDtypeStruct(shape, bf16) for shape in shapes],
            scratch_shapes=[pltpu.VMEM(shape, bf16) for shape in scratch],
            compiler_params=kernel_params(),
            cost_estimate=cost(2.0),
        )(place, *values)

    block_shape, map_shape = (heads, 2 * HEAD_DIM, HEAD_DIM), (heads, HEAD_DIM, HEAD_DIM)
    maps_shape = (SIDE,) + map_shape
    send_own, send_other = by_sequence(send)
    cores = (send_own, swap_cores(send_other))
    chip, core_maps = scan_step(chip_kernel, [block_shape, (2,) + map_shape], [], *cores)
    chips = from_below(chip, Y_STRIDE)
    hidden_grad = jnp.einsum("xp,hp->xh", grad_rows, down_projection, preferred_element_type=f32)
    chips[1], hidden_grad = together(chips[1], hidden_grad)
    plane, chip_maps = scan_step(
        plane_kernel, [block_shape, maps_shape], [(SIDE,) + block_shape], *chips
    )
    planes = from_below(plane, Z_STRIDE)
    state_ours, state_theirs, plane_maps = scan_step(
        enter_kernel, [map_shape, map_shape, maps_shape], [], *planes, *chips, *cores
    )
    state = (state_ours, swap_cores(state_theirs))

    head_out, x, mixer = pl.pallas_call(
        partial(mixer_kernel, heads),
        grid=(seqs,),
        in_specs=[
            in_scalars, at["fixed"], at["fixed"], at["tokens"], at["tokens"], at["tokens"],
            at["three"], at["gain"], at["mask"],
        ],
        out_specs=[at["rows"], at["tokens"], at["tokens"]],
        out_shape=[
            jax.ShapeDtypeStruct((seqs, length, width), bf16),
            shape["tokens"](bf16),
            shape["tokens"](f32),
        ],
        compiler_params=kernel_params(),
        cost_estimate=cost(2.3),
    )(place, *state, *in_hbm(q, w, u, score, gain_row, mask))
    head_out = head_out.reshape(rows, width)

    def bound_for(order):
        return lambda i, me: lax.rem(me[0] + sum((i == n) * at for n, at in enumerate(order)), devices)

    order = (2, 1, 3, 0)
    to = bound_for(order)
    came = on_pieces(
        2.2,
        branch_part_kernel,
        devices,
        [fixed(rows, width), spec((width, width), lambda i, me: (0, to(i, me)))],
        [fixed(half, width)] * 8,
        [half_shape] * 8,
    )(me, head_out, output_projection)
    branch = [came[2 * order.index(i // 2) + i % 2] for i in range(8)]
    middle_own = [
        mine.astype(f32) + other for mine, other in zip(own_halves, reduce_pieces(branch))
    ]
    middle = gather_pieces(*[value.astype(bf16) for value in middle_own])
    normed_mid, mid_scale = on_pieces(
        1.5,
        mid_norm_kernel,
        rows // tile,
        [*pieces, fixed(1, model)],
        [moving(model), moving(1)],
        [jax.ShapeDtypeStruct((rows, model), bf16), pltpu.HBM((rows, 1), f32)],
    )(me, *middle, *in_hbm(mlp_row))

    gated = jnp.einsum("ux,gxt->gut", normed_mid, gate_up_weight, preferred_element_type=f32)
    gated_grad, features = pl.pallas_call(
        gate_kernel,
        grid=(rows // tile,),
        in_specs=[spec((2, tile, hidden), lambda i: (0, i, 0)), row_tile(hidden)],
        out_specs=[spec((2, tile, hidden), lambda i: (0, i, 0)), row_tile(hidden)],
        out_shape=[
            jax.ShapeDtypeStruct((2, rows, hidden), bf16),
            jax.ShapeDtypeStruct((rows, hidden), bf16),
        ],
        compiler_params=kernel_params(),
        cost_estimate=cost(2.4),
    )(gated, hidden_grad)
    mid_parts = []
    for order in ((2,), (1, 3, 0)):
        to = bound_for(order)
        mid_parts += on_pieces(
            2.0 * len(order),
            mid_part_kernel,
            len(order),
            [
                fixed(2, rows, hidden),
                spec((2, width, hidden), lambda i, me, to=to: (0, to(i, me), 0)),
            ],
            [fixed(half, width)] * (2 * len(order)),
            [half_shape] * (2 * len(order)),
        )(me, gated_grad, gate_up_weight)
    order = (2, 1, 3, 0)
    mid_parts = [mid_parts[2 * order.index(i // 2) + i % 2] for i in range(8)]

    split_rows = 4

    def feed_weights(column, left, right, right_spec, into):
        extra = () if into is None else (into,)
        return pl.pallas_call(
            feed_weights_kernel,
            grid=(split_rows,),
            in_specs=[spec((rows, model // split_rows), lambda i: (0, i)), right_spec]
            + [pl.BlockSpec(memory_space=pl.ANY)] * len(extra),
            out_specs=spec((model // split_rows, hidden), lambda i: (i, column)),
            out_shape=pltpu.HBM((model, 3 * hidden), bf16),
            input_output_aliases={2: 0} if extra else {},
            compiler_params=kernel_params(),
        cost_estimate=cost(5.6),
        )(left, right, *extra)

    to_right, to_left, from_left, from_right = reduce_far(mid_parts)
    to_right, to_left, features = together(to_right, to_left, features)
    feed_part = feed_weights(2, grad_rows, features, whole(rows, hidden), None)
    far_left, far_right = along_head(to_right, 1), along_head(to_left, -1)
    far_left, far_right, feed_part = together(far_left, far_right, feed_part)
    mid_grad_own = (
        mid_parts[0].astype(f32) + from_right.astype(f32) + far_left.astype(f32),
        mid_parts[1].astype(f32) + from_left.astype(f32) + far_right.astype(f32),
    )
    first, second = [value.astype(bf16) for value in mid_grad_own]
    first, second, gated_grad = together(first, second, gated_grad)
    left_first, left_second, right_first, right_second = gather_near(first, second)
    right_spec = lambda j: spec((None, rows, hidden), lambda i: (j, 0, 0))
    feed_part = feed_weights(0, normed_mid, gated_grad, right_spec(0), feed_part)
    left_first, right_second, feed_part, features = together(
        left_first, right_second, feed_part, features
    )
    far = gather_far(left_first, right_second)
    feed = jnp.dot(features, down_projection, preferred_element_type=f32).astype(bf16)
    left_second, right_first, gated_grad, feed = together(left_second, right_first, gated_grad, feed)
    feed_part = feed_weights(1, normed_mid, gated_grad, right_spec(1), feed_part)
    *far, feed_part = together(*far, feed_part)
    mid_grad = (first, second, right_first, right_second, *far, left_first, left_second)
    feed_sum = lax.psum_scatter(feed_part, "seq", scatter_dimension=0, tiled=True)

    branch_grad, mid_dot = on_pieces(
        4.7,
        mid_back_kernel,
        rows // tile,
        [*pieces, *pieces, moving(model), fixed(1, model), moving(1)],
        [moving(model), moving(1)],
        [jax.ShapeDtypeStruct((rows, model), bf16), pltpu.HBM((rows, 1), f32)],
    )(me, *in_hbm(*middle, *mid_grad, grad_rows, mlp_row, mid_scale))
    own_gain = lax.dynamic_slice_in_dim(mlp_gain, col_start, width, 0)
    middle_grad_own, mlp_gain_part = [], 0.0
    for i in range(2):
        scale, inner = mid_scale[i * half : (i + 1) * half], mid_dot[i * half : (i + 1) * half]
        middle_grad_own.append(
            out_grad[i].astype(f32) + scale * own_gain * mid_grad_own[i]
            - scale * scale * scale * middle_own[i] * inner
        )
        mlp_gain_part += jnp.sum(mid_grad_own[i] * middle_own[i] * scale, axis=0)
    head_grad = jnp.einsum(
        "pj,wj->pw", branch_grad, output_projection, preferred_element_type=f32
    ).astype(bf16).reshape(seqs, length, width)

    send_back, dmix, dx, dgain = pl.pallas_call(
        partial(head_back_kernel, heads),
        grid=(seqs,),
        in_specs=[
            at["rows"], at["tokens"], at["gain"], at["mask"], at["tokens"], at["tokens"],
            at["three"],
        ],
        out_specs=[
            at["state"], at["tokens"], at["tokens"],
            spec((heads, 1, HEAD_DIM), lambda s: (s, 0, 0)),
        ],
        out_shape=[
            jax.ShapeDtypeStruct((chains, HEAD_DIM, HEAD_DIM), bf16),
            shape["tokens"](bf16),
            shape["tokens"](f32),
            jax.ShapeDtypeStruct((chains, 1, HEAD_DIM), f32),
        ],
        compiler_params=kernel_params(),
        cost_estimate=cost(3.3),
    )(head_grad, *in_hbm(mixer, gain_row, mask, q, w, score))

    steps, rows_own = 4, model // blocks
    chip_count = blocks // 2
    by_core = lambda n: spec((chip_count // steps, rows_own, n), lambda i: (i, 0, 0))
    core_shape = lambda n: jax.ShapeDtypeStruct((chip_count, rows_own, n), bf16)
    model_tile = spec((rows, model // steps), lambda i: (0, i))

    back_own, back_other = by_sequence(send_back)
    out_ours, out_theirs = pl.pallas_call(
        out_weights_kernel,
        grid=(steps,),
        in_specs=[in_scalars, model_tile, whole(rows, width)],
        out_specs=[by_core(width)] * 2,
        out_shape=[core_shape(width)] * 2,
        compiler_params=kernel_params(),
        cost_estimate=cost(2.3),
    )(core.reshape(1), branch_grad, head_out)
    chip_add, last_adds = scan_step(
        back_chip_kernel, [map_shape] * 2, [], core_maps, back_own, swap_cores(back_other)
    )
    chip_adds = from_below(chip_add, Y_STRIDE)
    chip_adds[1], out_ours, out_theirs = together(chip_adds[1], out_ours, out_theirs)
    plane_add, chip_adds = scan_step(
        back_plane_kernel, [map_shape, maps_shape], [], chip_maps, *chip_adds
    )
    plane_adds = from_below(plane_add, Z_STRIDE)
    out_joined = join_cores(out_ours, out_theirs)
    plane_adds[1], out_joined = together(plane_adds[1], out_joined)
    dstate_ours, dstate_theirs = scan_step(
        back_enter_kernel, [map_shape] * 2, [maps_shape],
        core_maps, chip_maps, plane_maps, last_adds, chip_adds, *plane_adds,
    )
    dstate = (dstate_ours, swap_cores(dstate_theirs))
    dstate_ours, out_joined = together(dstate_ours, out_joined)
    dstate = (dstate_ours, dstate[1])
    out_spread = exchange_chips(out_joined)

    dproj, tail, ahead, dlogit, dconv = pl.pallas_call(
        partial(span_back_kernel, heads),
        grid=(seqs,),
        in_specs=[
            in_scalars, at["fixed"], at["fixed"], at["fixed"], at["fixed"],
            at["proj"], at["halo"], at["conv"], at["strength"],
            at["tokens"], at["tokens"], at["tokens"], at["three"], at["two"],
        ],
        out_specs=[
            at["proj"], at["halo"], at["halo"], at["strength"],
            spec((3, 1, CONV, width), lambda s: (0, s, 0, 0)),
        ],
        out_shape=[
            jax.ShapeDtypeStruct((3, seqs, length, width), bf16),
            jax.ShapeDtypeStruct((3, seqs, HALO, width), f32),
            jax.ShapeDtypeStruct((3, seqs, HALO, width), bf16),
            jax.ShapeDtypeStruct((seqs, length, heads), f32),
            jax.ShapeDtypeStruct((3, seqs, CONV, width), f32),
        ],
        scratch_shapes=[
            pltpu.VMEM((heads * 3, HALO + length, HEAD_DIM), f32),
            pltpu.VMEM((heads * 3, 2 * HALO + length, HEAD_DIM), f32),
        ],
        compiler_params=kernel_params(),
        cost_estimate=cost(10.5),
    )(
        place, *state, *dstate, projected, *in_hbm(halo, conv_weight, strength, x, dmix, dx, gram, inv),
    )

    sent_back = from_behind(ahead, "seq", -1).astype(f32)
    proj_grad = lax.dynamic_update_slice_in_dim(
        dproj, (tail + sent_back).astype(bf16), length - HALO, 2
    ).reshape(3, rows, width)
    logit_grad = dlogit.astype(bf16).reshape(rows, heads)

    mix_ours, mix_theirs, strength_part, norm_gain_part = pl.pallas_call(
        mix_weights_kernel,
        grid=(steps,),
        in_specs=[in_scalars, model_tile, whole(3, rows, width), whole(rows, heads),
            spec((3, model // steps, width), lambda i: (0, i, 0)),
            spec((heads, model // steps), lambda i: (0, i)),
        ],
        out_specs=[by_core(3 * width)] * 2
        + [spec((n, model // steps), lambda i: (0, i)) for n in (heads, 8)],
        out_shape=[pltpu.HBM((chip_count, rows_own, 3 * width), bf16)] * 2
        + [jax.ShapeDtypeStruct((n, model), f32) for n in (heads, 8)],
        compiler_params=kernel_params(),
        cost_estimate=cost(9.0),
    )(core.reshape(1), normed_in, proj_grad, logit_grad, *in_hbm(query_key_value_weight), strength_projection.T)
    mix_ours, mix_theirs, out_spread = together(mix_ours, mix_theirs, out_spread)
    out_sum = jnp.sum(out_spread.astype(f32), axis=0)
    mix_joined = join_cores(mix_ours, mix_theirs)

    in_parts, inners = [], []
    for order in ((2,), (1, 3, 0)):
        to = bound_for(order)
        *parts, inner = on_pieces(
            2.0 * len(order),
            in_part_kernel,
            len(order),
            [
                fixed(3, rows, width), fixed(rows, heads),
                spec((3, width, width), lambda i, me, to=to: (0, to(i, me), 0)),
                spec((heads, width), lambda i, me, to=to: (0, to(i, me))),
                spec((rows, width), lambda i, me, to=to: (0, to(i, me))),
            ],
            [fixed(half, width)] * (2 * len(order)) + [fixed(8, rows)],
            [half_shape] * (2 * len(order)) + [jax.ShapeDtypeStruct((8, rows), f32)],
        )(me, proj_grad, logit_grad, *in_hbm(query_key_value_weight, strength_projection.T, normed_in))
        in_parts += parts
        inners.append(inner[0:1])
    order = (2, 1, 3, 0)
    in_parts = [in_parts[2 * order.index(i // 2) + i % 2] for i in range(8)]

    def over_head(value):
        value = value + along_head(value, 2)
        return value + along_head(value, 1)

    each, gain_each = width // blocks, HEAD_DIM // blocks
    by_columns = jnp.concatenate(
        [
            jnp.sum(dconv, axis=1).reshape(3 * CONV, width),
            mlp_gain_part[None],
            norm_gain_part[0].reshape(devices, width),
        ]
    )
    n_own = 3 * CONV + 1
    by_columns = jnp.swapaxes(by_columns.reshape(n_own + devices, blocks, each), 0, 1)
    by_rows = jnp.swapaxes(strength_part.reshape(heads, blocks, rows_own), 0, 1)
    by_gains = jnp.pad(
        jnp.sum(dgain, axis=(0, 1)).reshape(blocks, gain_each), ((0, 0), (0, each - gain_each))
    )
    small = jnp.concatenate(
        [by_rows.reshape(blocks, -1), by_columns.reshape(blocks, -1), by_gains], axis=1
    )
    small = exchange(small[:, None], "seq")
    in_parts[2], in_parts[7], mix_joined, small, inners = together(
        in_parts[2], in_parts[7], mix_joined, small, inners
    )
    mix_spread = exchange_chips(mix_joined)
    ring = reduce_far(in_parts)
    *ring, in_dot = together(*ring, inners[0] + inners[1])
    in_grad = reduce_near(in_parts, *ring)
    in_dot = in_dot + along_head(in_dot, 2)
    in_dot, feed, feed_sum = together(in_dot, feed, feed_sum)
    feed_sum = feed_sum.astype(f32)
    feed_own = lax.psum_scatter(feed, "head", scatter_dimension=1, tiled=True).astype(f32)
    output = jnp.concatenate(middle_own) + feed_own
    in_dot = (in_dot + along_head(in_dot, 1))[0][:, None] / model
    in_gain = lax.dynamic_slice_in_dim(norm_gain, col_start, width, 0)
    tokens_grad = []
    for i in range(2):
        scale, inner = in_scale[i * half : (i + 1) * half], in_dot[i * half : (i + 1) * half]
        mine = own_halves[i].astype(f32)
        tokens_grad.append(
            scale * in_gain * in_grad[i] - scale * scale * mine * inner + middle_grad_own[i]
        )
    tokens_grad = jnp.stack(tokens_grad).astype(bf16)

    small = jnp.sum(small, axis=(0, 1))
    n_rows = heads * rows_own
    head_sums = small[n_rows + n_own * each :]
    head_sums = head_sums + along_head(head_sums, 2)
    head_sums = head_sums + along_head(head_sums, 1)
    own_columns = small[n_rows : n_rows + n_own * each].reshape(n_own, each)
    norm_gain_own = lax.dynamic_slice_in_dim(
        head_sums, lax.axis_index("head") * each, each, 0
    ) / lax.dynamic_slice_in_dim(in_gain, index * each, each, 0)
    head_gain_own = head_sums[devices * each : devices * each + gain_each]
    output = output.astype(bf16).reshape(seqs, length, width)
    gate_up_grad = jnp.moveaxis(feed_sum[:, : 2 * hidden].reshape(rows_own, 2, hidden), 1, 0)
    out_weight_grad, down_grad = out_sum.T, feed_sum[:, 2 * hidden :].T
    mix_spread, output, tokens_grad, gate_up_grad, out_weight_grad, down_grad = together(
        mix_spread, output, tokens_grad, gate_up_grad, out_weight_grad, down_grad
    )
    mix_sum = jnp.sum(mix_spread.astype(f32), axis=0)
    qkv_grad = jnp.moveaxis(mix_sum.reshape(rows_own, 3, width), 1, 0)
    return (
        output,
        tokens_grad,
        norm_gain_own,
        qkv_grad,
        small[:n_rows].reshape(heads, rows_own).T,
        own_columns[: 3 * CONV].reshape(3, CONV, each),
        head_gain_own,
        out_weight_grad,
        own_columns[3 * CONV],
        gate_up_grad,
        down_grad,
    )


def solution(mesh):
    return jax.shard_map(
        shards,
        mesh=mesh,
        in_specs=(
            P(None, "seq", "head"),
            P(),
            P(),
            P(None, None, "head"),
            P(None, "head"),
            P(None, None, "head"),
            P(),
            P("head", None),
            P(),
            P(None, None, "head"),
            P("head", None),
            P(None, "seq", "head"),
        ),
        out_specs=(
            P(None, "seq", "head"),
            P(None, "seq", "head"),
            P(("head", "seq")),
            P(None, "seq", "head"),
            P("seq", "head"),
            P(None, None, ("head", "seq")),
            P("seq"),
            P("head", "seq"),
            P(("head", "seq")),
            P(None, "seq", "head"),
            P("head", "seq"),
        ),
        check_vma=False,
    )
```
